32 devices in a mesh: row: 4 (over y, x), col: 8 (over z, core).
Axes of the slice: x: 2, y: 2, z: 4, core: 2. Of those that a mesh axis runs over, the one named last changes fastest.
Arguments:
- features: bfloat16 [8192, 128], P('col'), may hold values from -6 to 6
- degrees: int32 [8192], replicated, may hold values from 1 to 400
- block_rows: int32 [4, 8, 384], P('row', 'col'), may hold values from 0 to 15
- block_cols: int32 [4, 8, 384], P('row', 'col'), may hold values from 0 to 7
- live_slots: int32 [4, 8], P('row', 'col'), may hold values from 96 to 384, as said below
- blocks: bfloat16 [4, 8, 384, 128, 128], P('row', 'col'), may hold values from 0 to 0.19921875
- weight: bfloat16 [128, 256], replicated, may hold values from -0.5 to 0.5
- cotangent: bfloat16 [8192, 256], P(('row', 'col')), may hold values from -6 to 6
Outputs:
- out_act: bfloat16 [8192, 256], P(('row', 'col'))
- feat_grad: float32 [8192, 128], P('col')
- weight_grad: float32 [128, 256], replicated
The draws below stay inside these ranges and needn't reach their ends.
Inputs may be any that keep to these rules, and one draw needn't show every extreme that they name: `live_slots`: some tile uses all 384 slots.
All inputs are finite; a program needn't handle non-finite values.
Results may differ from the reference program's by a relative error of at most 0.0028.
Values sent between devices are 32-bit elements; how exact they have to be, the bound alone decides.
No kernel may reach another device: no remote copies, remote signals or barrier semaphores. Data moves between devices by JAX's collectives and lax.ppermute only.
A program may use at most 192 MiB of HBM per device.

```python
import jax
import jax.numpy as jnp
from jax import lax

F = 128
HID = 256
BLK = 128
NODE_DEV = 256
SLOTS = 384
NODES = 8192
N_ROW = 4
N_COL = 8


def draw_degrees(key, part):
    key = jax.random.fold_in(key, 11)
    roots = jax.random.randint(key, (NODES,), 1, 21)
    roots = roots.at[0].set(20)
    return (roots * roots).astype(jnp.int32)


def draw_live_slots(key, part):
    key = jax.random.fold_in(key, 12)
    counts = jax.random.randint(key, (N_ROW, N_COL), SLOTS // 4, SLOTS + 1)
    return counts.at[0, 0].set(SLOTS).astype(jnp.int32)


def with_ends(result, own_key, low, largest):
    shape = result.shape
    place = [jax.random.randint(jax.random.fold_in(own_key, axis), (), 0, shape[axis]) for axis in range(len(shape))]
    result = result.at[tuple(place)].set(low)
    longest = shape.index(max(shape))
    place[longest] = (place[longest] + 1) % shape[longest]
    return result.at[tuple(place)].set(largest)


def block_levels(rng, extent, shards, low, high):
    level = 1.0
    for position, blocks in shards:
        heights = jax.random.uniform(jax.random.fold_in(jax.random.fold_in(rng, 6), position), (blocks,), jnp.float32, low / len(shards), high / len(shards))
        level = level * jnp.repeat(jnp.exp(heights), extent[position] // blocks).reshape((-1,) + (1,) * (len(extent) - 1 - position))
    return level


def scatter_about(rng, shape, deviation, bound, cuts=(), kind=jnp.bfloat16):
    loudness = block_levels(rng, shape, cuts, -0.22, 0.18) if cuts else 1.0
    entries = jax.random.normal(rng, shape, jnp.float32) * deviation * loudness
    return jnp.minimum(jnp.maximum(entries, -bound), bound).astype(kind)


def setup_inputs(seed: int = 0) -> dict:
    seeds = jax.random.split(jax.random.key(seed), 9)
    features = scatter_about(seeds[0], (NODES, F), 1.0, 6.0, ((0, 8),))
    degrees = draw_degrees(jax.random.fold_in(seeds[8], 71), 0)
    block_rows = with_ends(jax.random.randint(seeds[2], (N_ROW, N_COL, SLOTS), 0, NODE_DEV * N_COL // BLK), jax.random.fold_in(seeds[2], 1), 0, (NODE_DEV * N_COL // BLK) - 1).astype(jnp.int32)
    block_cols = with_ends(jax.random.randint(seeds[3], (N_ROW, N_COL, SLOTS), 0, NODE_DEV * N_ROW // BLK), jax.random.fold_in(seeds[3], 1), 0, (NODE_DEV * N_ROW // BLK) - 1).astype(jnp.int32)
    live_slots = draw_live_slots(jax.random.fold_in(seeds[8], 71), 0)
    blocks = jnp.clip(0.19921875 * jax.random.uniform(seeds[5], (N_ROW, N_COL, SLOTS, BLK, BLK), jnp.float32) ** block_levels(seeds[5], (N_ROW, N_COL, SLOTS, BLK, BLK), ((0, 4), (1, 8)), -0.2, 0.2), 0.0, 0.19921875).astype(jnp.bfloat16)
    weight = scatter_about(seeds[6], (F, HID), F ** -0.5, 0.5)
    cotangent = scatter_about(seeds[7], (NODES, HID), 1.0, 6.0, ((0, 32),))
    return dict(features=features, degrees=degrees, block_rows=block_rows, block_cols=block_cols, live_slots=live_slots, blocks=blocks, weight=weight, cotangent=cotangent)


HIGH = lax.Precision.HIGHEST

def smooth_act(values):
    return jax.nn.gelu(values, approximate=True)

def reference(features, degrees, block_rows, block_cols, live_slots, blocks, weight, cotangent):
    inv_deg = lax.rsqrt(degrees.astype(jnp.float32))
    scaled = (inv_deg[:, None] * features.astype(jnp.float32)).astype(jnp.bfloat16)
    row_nodes = NODES // N_ROW
    col_nodes = NODES // N_COL
    row_blocks = row_nodes // BLK
    col_blocks = col_nodes // BLK
    slot_ids = jnp.arange(SLOTS)

    def forward_step(tile_index, total):
        row_index = tile_index // N_COL
        col_index = tile_index % N_COL
        tile_blocks = blocks[row_index, col_index].astype(jnp.float32)
        in_use = (slot_ids < live_slots[row_index, col_index])[:, None, None]
        source = lax.dynamic_slice_in_dim(scaled, (col_index * col_nodes).astype(jnp.int32), col_nodes)
        picked = source.astype(jnp.float32).reshape(col_blocks, BLK, F)[block_cols[row_index, col_index]]
        products = jnp.einsum('sij,sjf->sif', tile_blocks, picked, precision=HIGH)
        products = jnp.where(in_use, products, 0.0)
        piece = jax.ops.segment_sum(products, block_rows[row_index, col_index], num_segments=row_blocks)
        row_start = (row_index * row_nodes).astype(jnp.int32)
        current = lax.dynamic_slice_in_dim(total, row_start, row_nodes)
        return lax.dynamic_update_slice_in_dim(total, current + piece.reshape(row_nodes, F), row_start, 0)
    summed = lax.fori_loop(0, N_ROW * N_COL, forward_step, jnp.zeros((NODES, F), jnp.float32))
    propagated = inv_deg[:, None] * summed
    preact = jnp.dot(propagated, weight.astype(jnp.float32), precision=HIGH)
    out_act = smooth_act(preact).astype(jnp.bfloat16)
    unused, pullback = jax.vjp(smooth_act, preact)
    gprime = pullback(cotangent.astype(jnp.float32))[0]
    pulled = inv_deg[:, None] * jnp.dot(gprime, weight.astype(jnp.float32).T, precision=HIGH)

    def backward_step(tile_index, total):
        row_index = tile_index // N_COL
        col_index = tile_index % N_COL
        tile_blocks = blocks[row_index, col_index].astype(jnp.float32)
        in_use = (slot_ids < live_slots[row_index, col_index])[:, None, None]
        source = lax.dynamic_slice_in_dim(pulled, (row_index * row_nodes).astype(jnp.int32), row_nodes)
        picked = source.reshape(row_blocks, BLK, F)[block_rows[row_index, col_index]]
        products = jnp.einsum('sij,sif->sjf', tile_blocks, picked, precision=HIGH)
        products = jnp.where(in_use, products, 0.0)
        piece = jax.ops.segment_sum(products, block_cols[row_index, col_index], num_segments=col_blocks)
        col_start = (col_index * col_nodes).astype(jnp.int32)
        current = lax.dynamic_slice_in_dim(total, col_start, col_nodes)
        return lax.dynamic_update_slice_in_dim(total, current + piece.reshape(col_nodes, F), col_start, 0)
    transposed = lax.fori_loop(0, N_ROW * N_COL, backward_step, jnp.zeros((NODES, F), jnp.float32))
    feat_grad = inv_deg[:, None] * transposed
    weight_grad = jnp.dot(propagated.T, gprime, precision=HIGH) * float(NODES) ** (-0.5)
    return (out_act, feat_grad, weight_grad)
```

```python
import functools

import jax
import jax.numpy as jnp
from jax import lax
from jax.experimental import pallas as pl
from jax.experimental.pallas import tpu as pltpu
from jax.sharding import PartitionSpec as P

HIGH = lax.Precision.HIGHEST
F32 = jnp.float32
BF16 = jnp.bfloat16
EDGE = 128
QUARTERS = 4
GROUP = 8
ACC_BYTES = 16 << 20
GELU_C = 0.7978845608028654
GELU_K = 0.044715


def inv_column(deg_ref, start):
    row = lax.rsqrt(deg_ref[pl.ds(start, 1), :].astype(F32))
    return jnp.transpose(jnp.broadcast_to(row, (EDGE, EDGE)))


def forward_kernel(
    n_col, chunk, panel_dev,
    rows_ref, cols_ref, live_ref, deg_ref, feat_ref, blocks_ref,
    keep_ref, send_ref, dense_ref,
    buf, acc0, acc1, acc2, acc3, hi_scr, lo_scr, scaled, in_sems, out_sems,
):
    accs = (acc0, acc1, acc2, acc3)
    n_chip = n_col // 2
    slots = buf.shape[0]
    part = EDGE // QUARTERS
    col_nodes, width = feat_ref.shape
    col_blocks = col_nodes // EDGE
    node_dev = keep_ref.shape[1]
    dev_blocks = node_dev // EDGE
    panel_blocks = panel_dev * dev_blocks
    positions = panel_blocks * col_blocks
    n_panels = n_col // panel_dev
    n_chunks = slots // chunk
    col = lax.axis_index("col")
    chip, core = col // 2, col % 2
    live = live_ref[0, 0]

    def block_copy(c):
        span = pl.ds(c * chunk, chunk)
        return pltpu.make_async_copy(blocks_ref.at[0, 0, span], buf.at[span], in_sems.at[c])

    def dense_copy(panel, j):
        span = pl.ds(j * node_dev, node_dev)
        there = pl.ds((panel * panel_dev + j) * node_dev, node_dev)
        return pltpu.make_async_copy(hi_scr.at[span], dense_ref.at[there], out_sems.at[j])

    for c in range(n_chunks):
        block_copy(c).start()

    for k in range(col_blocks):
        inv = inv_column(deg_ref, col * col_blocks + k)
        span = pl.ds(k * EDGE, EDGE)
        scaled[span, :] = (inv * feat_ref[span, :].astype(F32)).astype(BF16)

    def do_panel(panel, first):
        base = panel * panel_blocks

        @pl.loop(0, positions)
        def _(p):
            for acc in accs:
                acc[p] = jnp.zeros((part, EDGE), F32)

        @pl.loop(0, n_chunks)
        def _(c):
            if first is True:
                block_copy(c).wait()
            else:
                @pl.when(first)
                def _():
                    block_copy(c).wait()

            @pl.loop(0, chunk // GROUP)
            def _(g):
                for u in range(GROUP):
                    s = c * chunk + g * GROUP + u
                    r = rows_ref[0, 0, s] - base
                    ok = s < live
                    if n_panels > 1:
                        ok = ok & (r >= 0) & (r < panel_blocks)
                    p = jnp.where(ok, r * col_blocks + cols_ref[0, 0, s], positions)
                    for q in range(QUARTERS):
                        accs[q][p] += buf[s, q * part:(q + 1) * part, :].astype(F32)

        @pl.loop(0, panel_dev)
        def _(j):
            if first is not True:
                @pl.when(jnp.logical_not(first))
                def _():
                    dense_copy(panel, j).wait()
            for b in range(dev_blocks):
                for cb in range(col_blocks):
                    for q in range(QUARTERS):
                        value = accs[q][(j * dev_blocks + b) * col_blocks + cb]
                        hi = value.astype(BF16)
                        lo = (value - hi.astype(F32)).astype(BF16)
                        at = b * EDGE + q * part
                        lanes = slice(cb * EDGE, (cb + 1) * EDGE)
                        hi_scr[pl.ds(j * node_dev + at, part), lanes] = hi
                        lo_scr[pl.ds(at, part), lanes] = lo
            dense_copy(panel, j).start()
            total = jnp.dot(
                hi_scr[pl.ds(j * node_dev, node_dev), :], scaled[...], preferred_element_type=F32
            ) + jnp.dot(lo_scr[...], scaled[...], preferred_element_type=F32)
            dev = panel * panel_dev + j
            place = lax.rem(dev // 2 - chip + n_chip, n_chip)
            mine = dev % 2 == core

            @pl.when(mine)
            def _():
                keep_ref[place] = total

            @pl.when(jnp.logical_not(mine))
            def _():
                send_ref[place] = total

    if n_panels == 1:
        do_panel(0, True)
    else:
        @pl.loop(0, n_panels)
        def _(panel):
            do_panel(panel, panel == 0)

    for j in range(panel_dev):
        dense_copy(n_panels - 1, j).wait()


def middle_kernel(
    n_col, n_row, n_in, scale, deg_ref, cot_ref, weight_ref, *refs
):
    parts, (act_ref, pulled_ref, wkeep_ref, wsend_ref) = refs[:n_in], refs[n_in:]
    row, col = lax.axis_index("row"), lax.axis_index("col")
    core = col % 2
    node_dev = cot_ref.shape[0]
    dev_blocks = node_dev // EDGE
    summed = parts[0][...]
    for ref in parts[1:]:
        summed = summed + ref[...]
    base = (row * n_col + col) * dev_blocks
    inv = jnp.concatenate([inv_column(deg_ref, base + k) for k in range(dev_blocks)], axis=0)
    weight = weight_ref[...].astype(F32)
    propagated = inv * summed
    v = jnp.dot(propagated, weight, precision=HIGH, preferred_element_type=F32)
    t = jnp.tanh(GELU_C * (v + GELU_K * v * v * v))
    act_ref[...] = (0.5 * v * (1.0 + t)).astype(BF16)
    slope = 0.5 * (1.0 + t) + 0.5 * v * (1.0 - t * t) * (GELU_C * (1.0 + 3.0 * GELU_K * v * v))
    gprime = cot_ref[...].astype(F32) * slope
    pulled = inv * lax.dot_general(
        gprime, weight, (((1,), (1,)), ((), ())), precision=HIGH, preferred_element_type=F32
    )
    pulled_ref[...] = jnp.transpose(pulled)
    wpart = scale * lax.dot_general(
        propagated, gprime, (((0,), (0,)), ((), ())), precision=HIGH, preferred_element_type=F32
    )
    pieces, piece = wkeep_ref.shape[0], wkeep_ref.shape[1]
    for half in range(2):
        for j in range(pieces):
            at = (half * pieces + j) * piece
            place = lax.rem(j - row + n_row, n_row)

            @pl.when(core == half)
            def _():
                wkeep_ref[place] = wpart[at:at + piece]

            @pl.when(core != half)
            def _():
                wsend_ref[place] = wpart[at:at + piece]


def backward_kernel(n_col, deg_ref, dense_ref, *refs):
    parts, (out_ref, dense, lhs, sems) = refs[:n_col], refs[n_col:]
    n_chip = n_col // 2
    col = lax.axis_index("col")
    chip, core = col // 2, col % 2
    width, node_dev = parts[0].shape
    col_nodes = dense.shape[1]

    def dense_copy(j):
        span = pl.ds(j * node_dev, node_dev)
        return pltpu.make_async_copy(dense_ref.at[span], dense.at[span], sems.at[j])

    for j in range(n_col):
        dense_copy(j).start()
    for i in range(n_col):
        k, other = i % n_chip, i // n_chip
        source = lax.rem(chip - k + n_chip, n_chip) * 2 + (core if other == 0 else 1 - core)
        lanes = pl.ds(pl.multiple_of(source * node_dev, EDGE), node_dev)
        value = parts[i][...]
        hi = value.astype(BF16)
        lhs[:width, lanes] = hi
        lhs[width:, lanes] = (value - hi.astype(F32)).astype(BF16)
    for j in range(n_col):
        dense_copy(j).wait()
    step = 2 * EDGE if col_nodes % (2 * EDGE) == 0 else EDGE
    for n in range(col_nodes // step):
        both = jnp.dot(lhs[...], dense[:, n * step:(n + 1) * step], preferred_element_type=F32)
        total = both[:width] + both[width:]
        for b in range(step // EDGE):
            at = n * step + b * EDGE
            inv = inv_column(deg_ref, col * (col_nodes // EDGE) + at // EDGE)
            out_ref[at:at + EDGE, :] = inv * jnp.transpose(total[:, b * EDGE:(b + 1) * EDGE])


def whole_vmem():
    return pl.BlockSpec(memory_space=pltpu.VMEM)


def body(n_row, n_col, features, degrees, block_rows, block_cols, live_slots, blocks, weight, cotangent):
    n_chip = n_col // 2
    node_dev, hidden = cotangent.shape
    col_nodes, width = features.shape
    row_nodes = node_dev * n_col
    nodes = col_nodes * n_col
    slots = blocks.shape[2]
    deg = degrees.reshape(nodes // EDGE, EDGE)
    col_blocks = col_nodes // EDGE
    chunk = 32

    panel_dev = n_col
    while panel_dev % 2 == 0 and panel_dev * node_dev * col_nodes * 4 > ACC_BYTES:
        panel_dev //= 2
    positions = panel_dev * (node_dev // EDGE) * col_blocks
    smem = pl.BlockSpec(memory_space=pltpu.SMEM)
    hbm = pl.BlockSpec(memory_space=pl.ANY)
    vmem = whole_vmem()
    limit = 60 << 20

    keep, send, dense = pl.pallas_call(
        functools.partial(forward_kernel, n_col, chunk, panel_dev),
        out_shape=(
            jax.ShapeDtypeStruct((n_chip, node_dev, width), F32),
            jax.ShapeDtypeStruct((n_chip, node_dev, width), F32),
            jax.ShapeDtypeStruct((row_nodes, col_nodes), BF16),
        ),
        in_specs=[smem, smem, smem, vmem, vmem, hbm],
        out_specs=(vmem, vmem, hbm),
        scratch_shapes=[pltpu.VMEM((slots, EDGE, EDGE), BF16)]
        + [pltpu.VMEM((positions + 1, EDGE // QUARTERS, EDGE), F32) for _ in range(QUARTERS)]
        + [
            pltpu.VMEM((panel_dev * node_dev, col_nodes), BF16),
            pltpu.VMEM((node_dev, col_nodes), BF16),
            pltpu.VMEM((col_nodes, width), BF16),
            pltpu.SemaphoreType.DMA((slots // chunk,)),
            pltpu.SemaphoreType.DMA((panel_dev,)),
        ],
        compiler_params=pltpu.CompilerParams(vmem_limit_bytes=limit),
        name="densify_forward",
    )(block_rows, block_cols, live_slots, deg, features, blocks)

    swap = [(i, i ^ 1) for i in range(n_col)]

    def to_sibling(x):
        return lax.ppermute(x, "col", swap)

    def to_chip(x, k):
        pairs = [(i, ((i // 2 + k) % n_chip) * 2 + i % 2) for i in range(n_col)]
        return lax.ppermute(x, "col", pairs)

    def to_row(x, k):
        return lax.ppermute(x, "row", [(i, (i + k) % n_row) for i in range(n_row)])

    def row_flip(x, bit):
        return lax.ppermute(x, "row", [(i, i ^ (1 << bit)) for i in range(n_row)])

    got = to_sibling(send)
    arrived = [to_chip(keep[k] + got[k], k) for k in range(1, n_chip)]
    parts = [keep[0], got[0]] + arrived

    half = width // 2
    out_act, pulled, wkeep, wsend = pl.pallas_call(
        functools.partial(middle_kernel, n_col, n_row, len(parts), float(nodes) ** (-0.5)),
        out_shape=(
            jax.ShapeDtypeStruct((node_dev, hidden), BF16),
            jax.ShapeDtypeStruct((width, node_dev), F32),
            jax.ShapeDtypeStruct((n_row, half // n_row, hidden), F32),
            jax.ShapeDtypeStruct((n_row, half // n_row, hidden), F32),
        ),
        in_specs=[vmem] * (3 + len(parts)),
        out_specs=(vmem,) * 4,
        compiler_params=pltpu.CompilerParams(vmem_limit_bytes=limit),
        name="middle",
    )(deg, cotangent, weight, *parts)

    own = [pulled] + [to_chip(pulled, k) for k in range(1, n_chip)]
    sibling = [to_sibling(x) for x in own]
    col_part = pl.pallas_call(
        functools.partial(backward_kernel, n_col),
        out_shape=jax.ShapeDtypeStruct((col_nodes, width), F32),
        in_specs=[vmem, hbm] + [vmem] * n_col,
        out_specs=vmem,
        scratch_shapes=[
            pltpu.VMEM((row_nodes, col_nodes), BF16),
            pltpu.VMEM((2 * width, row_nodes), BF16),
            pltpu.SemaphoreType.DMA((n_col,)),
        ],
        compiler_params=pltpu.CompilerParams(vmem_limit_bytes=limit),
        name="backward",
    )(deg, dense, *own, *sibling)

    bits = n_row.bit_length() - 1
    if n_row == 1 << bits and bits > 0:
        pieces = bits
        while col_nodes % (8 * pieces):
            pieces -= 1
        size = col_nodes // pieces
        done = []
        for i in range(pieces):
            value = col_part[i * size:(i + 1) * size]
            for t in range(bits):
                value = value + row_flip(value, (i + t) % bits)
            done.append(value)
        feat_grad = jnp.concatenate(done, axis=0) if pieces > 1 else done[0]
    else:
        feat_grad = lax.psum(col_part, "row")

    wgot = to_sibling(wsend)
    wpiece = wkeep[0] + wgot[0]
    for k in range(1, n_row):
        wpiece = wpiece + to_row(wkeep[k] + wgot[k], k)
    others = jnp.stack([wpiece] + [to_chip(wpiece, k) for k in range(1, n_chip)])
    chip = lax.axis_index("col") // 2
    ordered = jnp.roll(others[::-1], chip + 1, axis=0)
    wsum = ordered[0]
    for k in range(1, n_chip):
        wsum = wsum + ordered[k]
    ring = jnp.stack([wsum] + [to_row(wsum, k) for k in range(1, n_row)])
    whole_half = jnp.roll(ring[::-1], lax.axis_index("row") + 1, axis=0).reshape(half, hidden)
    other_half = to_sibling(whole_half)
    low = lax.axis_index("col") % 2 == 0
    weight_grad = jnp.concatenate(
        [jnp.where(low, whole_half, other_half), jnp.where(low, other_half, whole_half)], axis=0
    )
    return out_act, feat_grad, weight_grad


def solution(mesh):
    n_row, n_col = mesh.shape["row"], mesh.shape["col"]
    return jax.shard_map(
        functools.partial(body, n_row, n_col),
        mesh=mesh,
        in_specs=(
            P("col", None),
            P(),
            P("row", "col", None),
            P("row", "col", None),
            P("row", "col"),
            P("row", "col", None, None, None),
            P(),
            P(("row", "col"), None),
        ),
        out_specs=(P(("row", "col"), None), P("col", None), P()),
        check_vma=False,
    )
```

```python
import functools

import jax
import jax.numpy as jnp
from jax import lax
from jax.experimental import pallas as pl
from jax.experimental.pallas import tpu as pltpu
from jax.sharding import PartitionSpec as P

HIGH = lax.Precision.HIGHEST
F32 = jnp.float32
BF16 = jnp.bfloat16
EDGE = 128
QUARTERS = 4
GROUP = 8
ACC_BYTES = 16 << 20
GELU_C = 0.7978845608028654
GELU_K = 0.044715


def inv_column(deg_ref, start):
    row = lax.rsqrt(deg_ref[pl.ds(start, 1), :].astype(F32))
    return jnp.transpose(jnp.broadcast_to(row, (EDGE, EDGE)))


def forward_kernel(
    n_col, chunk, panel_dev,
    rows_ref, cols_ref, live_ref, deg_ref, feat_ref, blocks_ref,
    keep_ref, send_ref, dense_ref,
    buf, acc0, acc1, acc2, acc3, hi_scr, lo_scr, scaled, in_sems, out_sems,
):
    accs = (acc0, acc1, acc2, acc3)
    slots = buf.shape[0]
    part = EDGE // QUARTERS
    col_nodes, width = feat_ref.shape
    col_blocks = col_nodes // EDGE
    node_dev = keep_ref.shape[1]
    dev_blocks = node_dev // EDGE
    panel_blocks = panel_dev * dev_blocks
    positions = panel_blocks * col_blocks
    n_panels = n_col // panel_dev
    n_chunks = slots // chunk
    col = lax.axis_index("col")
    core = col % 2
    live = live_ref[0, 0]

    def block_copy(c):
        span = pl.ds(c * chunk, chunk)
        return pltpu.make_async_copy(blocks_ref.at[0, 0, span], buf.at[span], in_sems.at[c])

    def dense_copy(panel, j):
        span = pl.ds(j * node_dev, node_dev)
        there = pl.ds((panel * panel_dev + j) * node_dev, node_dev)
        return pltpu.make_async_copy(hi_scr.at[span], dense_ref.at[there], out_sems.at[j])

    for c in range(n_chunks):
        block_copy(c).start()

    for k in range(col_blocks):
        inv = inv_column(deg_ref, col * col_blocks + k)
        span = pl.ds(k * EDGE, EDGE)
        scaled[span, :] = (inv * feat_ref[span, :].astype(F32)).astype(BF16)

    def do_panel(panel, first):
        base = panel * panel_blocks

        @pl.loop(0, positions)
        def _(p):
            for acc in accs:
                acc[p] = jnp.zeros((part, EDGE), F32)

        @pl.loop(0, n_chunks)
        def _(c):
            if first is True:
                block_copy(c).wait()
            else:
                @pl.when(first)
                def _():
                    block_copy(c).wait()

            @pl.loop(0, chunk // GROUP)
            def _(g):
                for u in range(GROUP):
                    s = c * chunk + g * GROUP + u
                    r = rows_ref[0, 0, s] - base
                    ok = s < live
                    if n_panels > 1:
                        ok = ok & (r >= 0) & (r < panel_blocks)
                    p = jnp.where(ok, r * col_blocks + cols_ref[0, 0, s], positions)
                    for q in range(QUARTERS):
                        accs[q][p] += buf[s, q * part:(q + 1) * part, :].astype(F32)

        @pl.loop(0, panel_dev)
        def _(j):
            if first is not True:
                @pl.when(jnp.logical_not(first))
                def _():
                    dense_copy(panel, j).wait()
            for b in range(dev_blocks):
                for cb in range(col_blocks):
                    for q in range(QUARTERS):
                        value = accs[q][(j * dev_blocks + b) * col_blocks + cb]
                        hi = value.astype(BF16)
                        lo = (value - hi.astype(F32)).astype(BF16)
                        at = b * EDGE + q * part
                        lanes = slice(cb * EDGE, (cb + 1) * EDGE)
                        hi_scr[pl.ds(j * node_dev + at, part), lanes] = hi
                        lo_scr[pl.ds(at, part), lanes] = lo
            dense_copy(panel, j).start()
            total = jnp.dot(
                hi_scr[pl.ds(j * node_dev, node_dev), :], scaled[...], preferred_element_type=F32
            ) + jnp.dot(lo_scr[...], scaled[...], preferred_element_type=F32)
            dev = panel * panel_dev + j
            place = dev // 2
            mine = dev % 2 == core

            @pl.when(mine)
            def _():
                keep_ref[place] = total

            @pl.when(jnp.logical_not(mine))
            def _():
                send_ref[place] = total

    if n_panels == 1:
        do_panel(0, True)
    else:
        @pl.loop(0, n_panels)
        def _(panel):
            do_panel(panel, panel == 0)

    for j in range(panel_dev):
        dense_copy(n_panels - 1, j).wait()


def middle_kernel(
    n_col, scale, deg_ref, cot_ref, weight_ref, parts_ref,
    act_ref, pulled_ref, wkeep_ref, wsend_ref,
):
    row, col = lax.axis_index("row"), lax.axis_index("col")
    core = col % 2
    node_dev = cot_ref.shape[0]
    dev_blocks = node_dev // EDGE
    summed = parts_ref[0]
    for k in range(1, parts_ref.shape[0]):
        summed = summed + parts_ref[k]
    base = (row * n_col + col) * dev_blocks
    inv = jnp.concatenate([inv_column(deg_ref, base + k) for k in range(dev_blocks)], axis=0)
    weight = weight_ref[...].astype(F32)
    propagated = inv * summed
    v = jnp.dot(propagated, weight, precision=HIGH, preferred_element_type=F32)
    t = jnp.tanh(GELU_C * (v + GELU_K * v * v * v))
    act_ref[...] = (0.5 * v * (1.0 + t)).astype(BF16)
    slope = 0.5 * (1.0 + t) + 0.5 * v * (1.0 - t * t) * (GELU_C * (1.0 + 3.0 * GELU_K * v * v))
    gprime = cot_ref[...].astype(F32) * slope
    pulled = jnp.transpose(inv * lax.dot_general(
        gprime, weight, (((1,), (1,)), ((), ())), precision=HIGH, preferred_element_type=F32
    ))
    for k in range(pulled_ref.shape[0]):
        pulled_ref[k] = pulled
    wpart = scale * lax.dot_general(
        propagated, gprime, (((0,), (0,)), ((), ())), precision=HIGH, preferred_element_type=F32
    )
    half = wkeep_ref.shape[0]
    low = core == 0
    wkeep_ref[...] = jnp.where(low, wpart[:half], wpart[half:])
    wsend_ref[...] = jnp.where(low, wpart[half:], wpart[:half])


def backward_kernel(n_col, deg_ref, dense_ref, own_ref, sibling_ref, out_ref, dense, lhs, sems):
    n_chip, width, node_dev = own_ref.shape
    core = lax.axis_index("col") % 2
    col = lax.axis_index("col")
    col_nodes = dense.shape[1]

    def dense_copy(j):
        span = pl.ds(j * node_dev, node_dev)
        return pltpu.make_async_copy(dense_ref.at[span], dense.at[span], sems.at[j])

    for j in range(n_col):
        dense_copy(j).start()
    for k in range(n_chip):
        for ref, place in ((own_ref, core), (sibling_ref, 1 - core)):
            lanes = pl.ds(pl.multiple_of((2 * k + place) * node_dev, EDGE), node_dev)
            value = ref[k]
            hi = value.astype(BF16)
            lhs[:width, lanes] = hi
            lhs[width:, lanes] = (value - hi.astype(F32)).astype(BF16)
    for j in range(n_col):
        dense_copy(j).wait()
    step = 2 * EDGE if col_nodes % (2 * EDGE) == 0 else EDGE
    for n in range(col_nodes // step):
        both = jnp.dot(lhs[...], dense[:, n * step:(n + 1) * step], preferred_element_type=F32)
        total = both[:width] + both[width:]
        for b in range(step // EDGE):
            at = n * step + b * EDGE
            inv = inv_column(deg_ref, col * (col_nodes // EDGE) + at // EDGE)
            out_ref[at:at + EDGE, :] = inv * jnp.transpose(total[:, b * EDGE:(b + 1) * EDGE])


def whole_vmem():
    return pl.BlockSpec(memory_space=pltpu.VMEM)


def body(n_row, n_col, features, degrees, block_rows, block_cols, live_slots, blocks, weight, cotangent):
    n_chip = n_col // 2
    node_dev, hidden = cotangent.shape
    col_nodes, width = features.shape
    row_nodes = node_dev * n_col
    nodes = col_nodes * n_col
    slots = blocks.shape[2]
    deg = degrees.reshape(nodes // EDGE, EDGE)
    col_blocks = col_nodes // EDGE
    chunk = 32

    panel_dev = n_col
    while panel_dev % 2 == 0 and panel_dev * node_dev * col_nodes * 4 > ACC_BYTES:
        panel_dev //= 2
    positions = panel_dev * (node_dev // EDGE) * col_blocks
    smem = pl.BlockSpec(memory_space=pltpu.SMEM)
    hbm = pl.BlockSpec(memory_space=pl.ANY)
    vmem = whole_vmem()
    limit = 60 << 20

    keep, send, dense = pl.pallas_call(
        functools.partial(forward_kernel, n_col, chunk, panel_dev),
        out_shape=(
            jax.ShapeDtypeStruct((n_chip, node_dev, width), F32),
            jax.ShapeDtypeStruct((n_chip, node_dev, width), F32),
            jax.ShapeDtypeStruct((row_nodes, col_nodes), BF16),
        ),
        in_specs=[smem, smem, smem, vmem, vmem, hbm],
        out_specs=(vmem, vmem, hbm),
        scratch_shapes=[pltpu.VMEM((slots, EDGE, EDGE), BF16)]
        + [pltpu.VMEM((positions + 1, EDGE // QUARTERS, EDGE), F32) for _ in range(QUARTERS)]
        + [
            pltpu.VMEM((panel_dev * node_dev, col_nodes), BF16),
            pltpu.VMEM((node_dev, col_nodes), BF16),
            pltpu.VMEM((col_nodes, width), BF16),
            pltpu.SemaphoreType.DMA((slots // chunk,)),
            pltpu.SemaphoreType.DMA((panel_dev,)),
        ],
        compiler_params=pltpu.CompilerParams(vmem_limit_bytes=limit),
        name="densify_forward",
    )(block_rows, block_cols, live_slots, deg, features, blocks)

    swap = [(i, i ^ 1) for i in range(n_col)]
    same_core = [list(range(c, n_col, 2)) for c in range(2)]

    def to_sibling(x):
        return lax.ppermute(x, "col", swap)

    def chips(x):
        return lax.all_to_all(x, "col", 0, 0, axis_index_groups=same_core)

    def rows(x):
        return lax.all_to_all(x, "row", 0, 0)

    def copies(x, n):
        return jnp.broadcast_to(x[None], (n,) + x.shape)

    parts = chips(keep + to_sibling(send))

    half = width // 2
    out_act, pulled, wkeep, wsend = pl.pallas_call(
        functools.partial(middle_kernel, n_col, float(nodes) ** (-0.5)),
        out_shape=(
            jax.ShapeDtypeStruct((node_dev, hidden), BF16),
            jax.ShapeDtypeStruct((n_chip, width, node_dev), F32),
            jax.ShapeDtypeStruct((half, hidden), F32),
            jax.ShapeDtypeStruct((half, hidden), F32),
        ),
        in_specs=[vmem] * 4,
        out_specs=(vmem,) * 4,
        compiler_params=pltpu.CompilerParams(vmem_limit_bytes=limit),
        name="middle",
    )(deg, cotangent, weight, parts)

    own = chips(pulled)
    own, wkeep, wsend = lax.optimization_barrier((own, wkeep, wsend))
    sibling = to_sibling(own)
    col_part = pl.pallas_call(
        functools.partial(backward_kernel, n_col),
        out_shape=jax.ShapeDtypeStruct((col_nodes, width), F32),
        in_specs=[vmem, hbm, vmem, vmem],
        out_specs=vmem,
        scratch_shapes=[
            pltpu.VMEM((row_nodes, col_nodes), BF16),
            pltpu.VMEM((2 * width, row_nodes), BF16),
            pltpu.SemaphoreType.DMA((n_col,)),
        ],
        compiler_params=pltpu.CompilerParams(vmem_limit_bytes=limit),
        name="backward",
    )(deg, dense, own, sibling)

    feat = rows(col_part.reshape(n_row, col_nodes // n_row, width))
    feat_grad = rows(copies(feat.sum(axis=0), n_row)).reshape(col_nodes, width)

    wparts = rows((wkeep + to_sibling(wsend)).reshape(n_row, half // n_row, hidden))
    wsum = chips(copies(wparts.sum(axis=0), n_chip)).sum(axis=0)
    whole_half = rows(copies(wsum, n_row)).reshape(half, hidden)
    other_half = to_sibling(whole_half)
    low = lax.axis_index("col") % 2 == 0
    weight_grad = jnp.concatenate(
        [jnp.where(low, whole_half, other_half), jnp.where(low, other_half, whole_half)], axis=0
    )
    return out_act, feat_grad, weight_grad


def solution(mesh):
    n_row, n_col = mesh.shape["row"], mesh.shape["col"]
    return jax.shard_map(
        functools.partial(body, n_row, n_col),
        mesh=mesh,
        in_specs=(
            P("col", None),
            P(),
            P("row", "col", None),
            P("row", "col", None),
            P("row", "col"),
            P("row", "col", None, None, None),
            P(),
            P(("row", "col"), None),
        ),
        out_specs=(P(("row", "col"), None), P("col", None), P()),
        check_vma=False,
    )
```

```python
import functools

import jax
import jax.numpy as jnp
from jax import lax
from jax.experimental import pallas as pl
from jax.experimental.pallas import tpu as pltpu
from jax.sharding import PartitionSpec as P

HIGH = lax.Precision.HIGHEST
F32 = jnp.float32
BF16 = jnp.bfloat16
EDGE = 128
GROUP = 8
ACC_BYTES = 16 << 20
GELU_C = 0.7978845608028654
GELU_K = 0.044715


def inv_column(deg_ref, start):
    row = lax.rsqrt(deg_ref[pl.ds(start, 1), :].astype(F32))
    return jnp.transpose(jnp.broadcast_to(row, (EDGE, EDGE)))


def split(value):
    hi = value.astype(BF16)
    return hi, (value - hi.astype(F32)).astype(BF16)


def fetch(pairs, sems):
    copies = [pltpu.make_async_copy(src, dst, sems.at[i]) for i, (src, dst) in enumerate(pairs)]
    for copy in copies:
        copy.start()
    return copies


def forward_kernel(
    n_col, chunk, panel_dev, node_dev, groups,
    rows_ref, cols_ref, live_ref, deg_ref, feat_ref, blocks_ref, *refs,
):
    n_out = 2 * len(groups) + 1
    outs, dense_ref = refs[:n_out - 1], refs[n_out - 1]
    acc, both, buf, scaled, in_sems, out_sems = refs[n_out:]
    slots = buf.shape[0]
    col_nodes, width = feat_ref.shape
    col_blocks = col_nodes // EDGE
    dev_blocks = node_dev // EDGE
    panel_blocks = panel_dev * dev_blocks
    positions = panel_blocks * col_blocks
    n_panels = n_col // panel_dev
    n_chunks = slots // chunk
    me = lax.axis_index("col")
    live = live_ref[0, 0]

    def block_copy(c):
        span = pl.ds(c * chunk, chunk)
        return pltpu.make_async_copy(blocks_ref.at[0, 0, span], buf.at[span], in_sems.at[c])

    def dense_copy(panel, j):
        there = pl.ds((panel * panel_dev + j) * node_dev, node_dev)
        return pltpu.make_async_copy(
            both.at[j, pl.ds(0, node_dev)], dense_ref.at[there], out_sems.at[j]
        )

    for c in range(n_chunks):
        block_copy(c).start()

    for k in range(col_blocks):
        inv = inv_column(deg_ref, me * col_blocks + k)
        span = pl.ds(k * EDGE, EDGE)
        scaled[span, :] = (inv * feat_ref[span, :].astype(F32)).astype(BF16)

    def emit(rel, total):
        for g, members in enumerate(groups):
            for q in range(2):
                ref = outs[2 * g + q]
                if isinstance(rel, int):
                    if rel % 2 == q and rel // 2 in members:
                        ref[members.index(rel // 2)] = total
                else:
                    first = members[0]
                    inside = (rel % 2 == q) & (rel // 2 <= first) & (rel // 2 > first - len(members))

                    @pl.when(inside)
                    def _():
                        ref[first - rel // 2] = total

    def do_panel(panel, first):
        base = panel * panel_blocks

        @pl.loop(0, positions, unroll=4)
        def _(p):
            acc[p] = jnp.zeros((EDGE, EDGE), F32)

        def place(s):
            r = rows_ref[0, 0, s]
            r = ((r // dev_blocks) ^ me) * dev_blocks + r % dev_blocks - base
            ok = s < live
            if n_panels > 1:
                ok = ok & (r >= 0) & (r < panel_blocks)
            return jnp.where(ok, r * col_blocks + cols_ref[0, 0, s], positions)

        @pl.loop(0, n_chunks)
        def _(c):
            if first is True:
                block_copy(c).wait()
            else:
                @pl.when(first)
                def _():
                    block_copy(c).wait()

            @pl.loop(0, chunk // GROUP)
            def _(g):
                for u in range(0, GROUP, 2):
                    s = c * chunk + g * GROUP + u
                    p0, p1 = place(s), place(s + 1)
                    same = jnp.where(p0 == p1, 1.0, 0.0).astype(F32)
                    b0, b1 = buf[s].astype(F32), buf[s + 1].astype(F32)
                    a0, a1 = acc[p0], acc[p1]
                    acc[p0] = a0 + b0
                    acc[p1] = a1 + (b1 + same * b0)

        def one(j):
            for b in range(dev_blocks):
                for cb in range(col_blocks):
                    hi, lo = split(acc[(j * dev_blocks + b) * col_blocks + cb])
                    lanes = slice(cb * EDGE, (cb + 1) * EDGE)
                    both[j, b * EDGE:(b + 1) * EDGE, lanes] = hi
                    both[j, node_dev + b * EDGE:node_dev + (b + 1) * EDGE, lanes] = lo
            dense_copy(panel, j).start()
            pair = jnp.dot(both[j], scaled[...], preferred_element_type=F32)
            total = pair[:node_dev] + pair[node_dev:]
            emit(panel * panel_dev + j, total)

        if n_panels == 1:
            for j in reversed(range(panel_dev)):
                one(j)
        else:
            @pl.loop(0, panel_dev)
            def _(j):
                @pl.when(panel > 0)
                def _():
                    dense_copy(panel, j).wait()
                one(j)

    if n_panels == 1:
        do_panel(0, True)
    else:
        @pl.loop(0, n_panels)
        def _(panel):
            do_panel(panel, panel == 0)

    for j in range(panel_dev):
        dense_copy(n_panels - 1, j).wait()


def middle_kernel(n_col, n_in, deg_ref, cot_ref, weight_ref, *refs):
    parts = refs[:n_in]
    act_ref, pulled_ref, prop_ref, gprime_ref = refs[n_in:n_in + 4]
    node_dev = cot_ref.shape[0]
    dev_blocks = node_dev // EDGE
    base = (lax.axis_index("row") * n_col + lax.axis_index("col")) * dev_blocks
    inv = jnp.concatenate([inv_column(deg_ref, base + k) for k in range(dev_blocks)], axis=0)
    summed = parts[0][...].reshape(node_dev, EDGE)
    for ref in parts[1:]:
        summed = summed + ref[...].reshape(node_dev, EDGE)
    propagated = inv * summed
    prop_ref[...] = propagated
    weight = weight_ref[...]
    pair = jnp.dot(jnp.concatenate(split(propagated), axis=0), weight, preferred_element_type=F32)
    v = pair[:node_dev] + pair[node_dev:]
    t = jnp.tanh(GELU_C * (v + GELU_K * v * v * v))
    act_ref[...] = (0.5 * v * (1.0 + t)).astype(BF16)
    slope = 0.5 * (1.0 + t) + 0.5 * v * (1.0 - t * t) * (GELU_C * (1.0 + 3.0 * GELU_K * v * v))
    gprime = cot_ref[...].astype(F32) * slope
    gprime_ref[...] = gprime
    pair = lax.dot_general(
        jnp.concatenate(split(gprime), axis=0), weight, (((1,), (1,)), ((), ())),
        preferred_element_type=F32,
    )
    pulled_ref[...] = jnp.transpose(inv * (pair[:node_dev] + pair[node_dev:]))


def weight_kernel(scale, prop_ref, gprime_ref, keep_ref, send_ref):
    part = scale * lax.dot_general(
        prop_ref[...], gprime_ref[...], (((0,), (0,)), ((), ())),
        precision=HIGH, preferred_element_type=F32,
    )
    half = keep_ref.shape[0]
    low = lax.axis_index("col") % 2 == 0
    keep_ref[...] = jnp.where(low, part[:half], part[half:])
    send_ref[...] = jnp.where(low, part[half:], part[:half])


def load_lhs(parts, stage, lhs, copies):
    width = parts[0].shape[0]
    node_dev = parts[0].shape[1]
    for i in range(len(parts)):
        copies[i].wait()
        hi, lo = split(stage[i])
        lhs[:width, i * node_dev:(i + 1) * node_dev] = hi
        lhs[width:, i * node_dev:(i + 1) * node_dev] = lo


def partial_kernel(n_in, dense_ref, *refs):
    parts, (out_ref, dense, stage, lhs, sems, dense_sems) = refs[:n_in], refs[n_in:]
    width, node_dev = parts[0].shape
    col_nodes = dense.shape[1]
    blocks = fetch(
        [(dense_ref.at[pl.ds(i * node_dev, node_dev)], dense.at[pl.ds(i * node_dev, node_dev)])
         for i in range(n_in)], dense_sems)
    load_lhs(parts, stage, lhs, fetch([(r, stage.at[i]) for i, r in enumerate(parts)], sems))
    for copy in blocks:
        copy.wait()
    step = 2 * EDGE if col_nodes % (2 * EDGE) == 0 else EDGE
    for n in range(0, col_nodes, step):
        pair = jnp.dot(lhs[...], dense[:, n:n + step], preferred_element_type=F32)
        out_ref[:, n:n + step] = pair[:width] + pair[width:]


def last_kernel(n_in, n_out, start, deg_ref, dense_ref, sofar_ref, *refs):
    parts, outs = refs[:n_in], refs[n_in:n_in + n_out]
    dense, stage, lhs, sofar, sems, dense_sem, sofar_sem = refs[n_in + n_out:]
    width, node_dev = parts[0].shape
    col_nodes = dense.shape[1]
    block = pltpu.make_async_copy(
        dense_ref.at[pl.ds(start, n_in * node_dev)], dense, dense_sem)
    before = pltpu.make_async_copy(sofar_ref, sofar, sofar_sem)
    block.start()
    copies = fetch([(r, stage.at[i]) for i, r in enumerate(parts)], sems)
    before.start()
    load_lhs(parts, stage, lhs, copies)
    block.wait()
    before.wait()
    step = 2 * EDGE if col_nodes % (2 * EDGE) == 0 else EDGE
    size = col_nodes // n_out
    first = lax.axis_index("col") * (col_nodes // EDGE)
    for n in range(0, col_nodes, step):
        pair = jnp.dot(lhs[...], dense[:, n:n + step], preferred_element_type=F32)
        total = sofar[:, n:n + step] + (pair[:width] + pair[width:])
        for at in range(n, n + step, EDGE):
            inv = inv_column(deg_ref, first + at // EDGE)
            out = outs[at // size]
            out[at % size:at % size + EDGE, :] = inv * jnp.transpose(total[:, at - n:at - n + EDGE])


def body(n_row, n_col, features, degrees, block_rows, block_cols, live_slots, blocks, weight, cotangent):
    n_chip = n_col // 2
    chip_bits, row_bits = n_chip.bit_length() - 1, n_row.bit_length() - 1
    assert n_col == 2 << chip_bits and n_row == 1 << row_bits
    node_dev, hidden = cotangent.shape
    col_nodes, width = features.shape
    row_nodes = node_dev * n_col
    nodes = col_nodes * n_col
    slots = blocks.shape[2]
    deg = degrees.reshape(nodes // EDGE, EDGE)
    col_blocks = col_nodes // EDGE
    chunk = 32

    panel_dev = n_col
    while panel_dev % 2 == 0 and panel_dev * node_dev * col_nodes * 4 > ACC_BYTES:
        panel_dev //= 2
    positions = panel_dev * (node_dev // EDGE) * col_blocks
    groups = [g for g in ([n_chip - 1], list(range(n_chip - 2, 0, -1)), [0]) if g]
    if n_chip == 1:
        groups = [[0]]
    smem = pl.BlockSpec(memory_space=pltpu.SMEM)
    hbm = pl.BlockSpec(memory_space=pl.ANY)
    vmem = pl.BlockSpec(memory_space=pltpu.VMEM)

    def params(mib):
        return pltpu.CompilerParams(vmem_limit_bytes=mib << 20)

    pieces = [
        jax.ShapeDtypeStruct((len(g), node_dev, width), F32) for g in groups for _ in range(2)
    ]
    *pieces, dense = pl.pallas_call(
        functools.partial(forward_kernel, n_col, chunk, panel_dev, node_dev, groups),
        out_shape=(*pieces, jax.ShapeDtypeStruct((row_nodes, col_nodes), BF16)),
        in_specs=[smem, smem, smem, vmem, vmem, hbm],
        out_specs=(vmem,) * len(pieces) + (hbm,),
        scratch_shapes=[
            pltpu.VMEM((positions + 1, EDGE, EDGE), F32),
            pltpu.VMEM((panel_dev, 2 * node_dev, col_nodes), BF16),
            pltpu.VMEM((slots, EDGE, EDGE), BF16),
            pltpu.VMEM((col_nodes, width), BF16),
            pltpu.SemaphoreType.DMA((slots // chunk,)),
            pltpu.SemaphoreType.DMA((panel_dev,)),
        ],
        compiler_params=params(60),
        name="densify_forward",
    )(block_rows, block_cols, live_slots, deg, features, blocks)

    swap_pairs = [(i, i ^ 1) for i in range(n_col)]

    def swap(x):
        return lax.ppermute(x, "col", swap_pairs)

    def chip_flip(x, bit):
        return lax.ppermute(x, "col", [(i, i ^ (2 << bit)) for i in range(n_col)])

    def row_flip(x, bit):
        return lax.ppermute(x, "row", [(i, i ^ (1 << bit)) for i in range(n_row)])

    def low_bit(m):
        return (m & -m).bit_length() - 1

    terms = {}
    for g, members in enumerate(groups):
        keep, got = pieces[2 * g], swap(pieces[2 * g + 1])
        for i, m in enumerate(members):
            terms[m] = [keep[i], got[i]]
    for m in range(n_chip - 1, 0, -1):
        terms[m & (m - 1)].append(chip_flip(functools.reduce(jnp.add, terms[m]), low_bit(m)))
    parts = terms[0]

    out_act, pulled, prop, gprime = pl.pallas_call(
        functools.partial(middle_kernel, n_col, len(parts)),
        out_shape=(
            jax.ShapeDtypeStruct((node_dev, hidden), BF16),
            jax.ShapeDtypeStruct((width, node_dev), F32),
            jax.ShapeDtypeStruct((node_dev, width), F32),
            jax.ShapeDtypeStruct((node_dev, hidden), F32),
        ),
        in_specs=[vmem] * (3 + len(parts)),
        out_specs=(vmem,) * 4,
        compiler_params=params(16),
        name="middle",
    )(deg, cotangent, weight, *parts)

    own = {0: pulled}
    for m in range(1, n_chip):
        own[m] = chip_flip(own[m & (m - 1)], low_bit(m))
    other = {m: swap(own[m]) for m in range(n_chip)}

    other[0], prop, gprime = lax.optimization_barrier((other[0], prop, gprime))
    half = width // 2
    wkeep, wsend = pl.pallas_call(
        functools.partial(weight_kernel, float(nodes) ** (-0.5)),
        out_shape=(jax.ShapeDtypeStruct((half, hidden), F32),) * 2,
        in_specs=[vmem] * 2,
        out_specs=(vmem,) * 2,
        compiler_params=params(16),
        name="weight_part",
    )(prop, gprime)

    early = [x for m in range(n_chip - 1) for x in (own[m], other[m])]
    late = [own[n_chip - 1], other[n_chip - 1]]
    tile_mib = row_nodes * col_nodes * 2 >> 20
    sofar = pl.pallas_call(
        functools.partial(partial_kernel, len(early)),
        out_shape=jax.ShapeDtypeStruct((width, col_nodes), F32),
        in_specs=[hbm] * (1 + len(early)),
        out_specs=vmem,
        scratch_shapes=[
            pltpu.VMEM((len(early) * node_dev, col_nodes), BF16),
            pltpu.VMEM((len(early), width, node_dev), F32),
            pltpu.VMEM((2 * width, len(early) * node_dev), BF16),
            pltpu.SemaphoreType.DMA((len(early),)),
            pltpu.SemaphoreType.DMA((len(early),)),
        ],
        compiler_params=params(tile_mib + 20),
        name="backward_early",
    )(dense, *early)

    n_piece = max(1, row_bits)
    while col_nodes % (EDGE * n_piece):
        n_piece -= 1
    size = col_nodes // n_piece
    parts = pl.pallas_call(
        functools.partial(last_kernel, len(late), n_piece, len(early) * node_dev),
        out_shape=(jax.ShapeDtypeStruct((size, width), F32),) * n_piece,
        in_specs=[vmem, hbm, hbm] + [hbm] * len(late),
        out_specs=(vmem,) * n_piece,
        scratch_shapes=[
            pltpu.VMEM((len(late) * node_dev, col_nodes), BF16),
            pltpu.VMEM((len(late), width, node_dev), F32),
            pltpu.VMEM((2 * width, len(late) * node_dev), BF16),
            pltpu.VMEM((width, col_nodes), F32),
            pltpu.SemaphoreType.DMA((len(late),)),
            pltpu.SemaphoreType.DMA,
            pltpu.SemaphoreType.DMA,
        ],
        compiler_params=params(16),
        name="backward_late",
    )(deg, dense, sofar, *late)

    done = list(parts)
    for t in range(row_bits):
        done = [x + row_flip(x, (i + t) % row_bits) for i, x in enumerate(done)]
    feat_grad = jnp.concatenate(done, axis=0) if n_piece > 1 else done[0]

    wsum = wkeep + swap(wsend)
    for t in range(row_bits):
        wsum = wsum + row_flip(wsum, t)
    for t in range(chip_bits):
        wsum = wsum + chip_flip(wsum, t)
    wother = swap(wsum)
    low = lax.axis_index("col") % 2 == 0
    weight_grad = jnp.concatenate(
        [jnp.where(low, wsum, wother), jnp.where(low, wother, wsum)], axis=0
    )
    return out_act, feat_grad, weight_grad


def solution(mesh):
    n_row, n_col = mesh.shape["row"], mesh.shape["col"]
    return jax.shard_map(
        functools.partial(body, n_row, n_col),
        mesh=mesh,
        in_specs=(
            P("col", None),
            P(),
            P("row", "col", None),
            P("row", "col", None),
            P("row", "col"),
            P("row", "col", None, None, None),
            P(),
            P(("row", "col"), None),
        ),
        out_specs=(P(("row", "col"), None), P("col", None), P()),
        check_vma=False,
    )
```

```python
import functools

import jax
import jax.numpy as jnp
from jax import lax
from jax.experimental import pallas as pl
from jax.experimental.pallas import tpu as pltpu
from jax.sharding import PartitionSpec as P

HIGH = lax.Precision.HIGHEST
F32 = jnp.float32
BF16 = jnp.bfloat16
EDGE = 128
GROUP = 8
QUAD = 4
RING = 128
ACC_BYTES = 12 << 20
GELU_C = 0.7978845608028654
GELU_K = 0.044715


def inv_column(deg_ref, start):
    row = lax.rsqrt(deg_ref[pl.ds(start, 1), :].astype(F32))
    return jnp.transpose(jnp.broadcast_to(row, (EDGE, EDGE)))


def split(value):
    hi = value.astype(BF16)
    return hi, (value - hi.astype(F32)).astype(BF16)


def fetch(pairs, sems):
    copies = [pltpu.make_async_copy(src, dst, sems.at[i]) for i, (src, dst) in enumerate(pairs)]
    for copy in copies:
        copy.start()
    return copies


def halve(value, size):
    if size & (size - 1) == 0:
        shift = size.bit_length() - 1
        return lax.shift_right_logical(value, shift), value & (size - 1)
    return lax.div(value, size), lax.rem(value, size)


def forward_kernel(
    first_unit, n_panels, node_dev,
    rows_ref, cols_ref, live_ref, deg_ref, feat_ref, blocks_ref, *refs,
):
    keep_ref, send_ref, dense_ref = refs[-13:-10]
    acc, both, ring, scaled, result, slot_list, place_list, in_sems, dense_sems, out_sems = refs[-10:]
    slots = rows_ref.shape[2]
    col_nodes, width = feat_ref.shape
    col_blocks = col_nodes // EDGE
    dev_blocks = node_dev // EDGE
    panel_dev = both.shape[0]
    panel_units = panel_dev // 2
    positions = panel_dev * dev_blocks * col_blocks
    quads = ring.shape[0] // QUAD
    me = lax.axis_index("col")
    live = live_ref[0, 0]

    def block_copy(i, u):
        at = lax.rem(i, quads)
        return pltpu.make_async_copy(
            blocks_ref.at[0, 0, slot_list[i * QUAD + u]], ring.at[at * QUAD + u], in_sems.at[at])

    def start_quad(i):
        for u in range(QUAD):
            block_copy(i, u).start()

    def dense_copy(panel, j):
        there = pl.ds((panel * panel_dev + j) * node_dev, node_dev)
        return pltpu.make_async_copy(
            both.at[j, pl.ds(0, node_dev)], dense_ref.at[there], dense_sems.at[j])

    def result_copy(panel, j):
        ref = send_ref if j % 2 else keep_ref
        return pltpu.make_async_copy(
            result.at[j], ref.at[panel * panel_units + j // 2], out_sems.at[j])

    def do_panel(panel):
        base = first_unit + panel * panel_units

        def scan(g, count):
            for u in range(GROUP):
                s = g * GROUP + u
                dev, inner = halve(rows_ref[0, 0, s], dev_blocks)
                rel = (dev ^ me) - 2 * base
                hit = (rel >= 0) & (rel < panel_dev) & (s < live)
                slot_list[count] = s
                place_list[count] = (rel * dev_blocks + inner) * col_blocks + cols_ref[0, 0, s]
                count = count + jnp.where(hit, 1, 0)
            return count

        count = lax.fori_loop(0, slots // GROUP, scan, 0)
        for u in range(QUAD - 1):
            slot_list[count + u] = 0
            place_list[count + u] = positions
        n_quads = lax.shift_right_logical(count + (QUAD - 1), QUAD.bit_length() - 1)

        @pl.loop(0, jnp.minimum(n_quads, quads))
        def _(i):
            start_quad(i)

        @pl.when(panel == 0)
        def _():
            for k in range(col_blocks):
                inv = inv_column(deg_ref, me * col_blocks + k)
                span = pl.ds(k * EDGE, EDGE)
                scaled[span, :] = (inv * feat_ref[span, :].astype(F32)).astype(BF16)

        @pl.loop(0, positions // 4)
        def _(p):
            for u in range(4):
                acc[p * 4 + u] = jnp.zeros((EDGE, EDGE), F32)

        @pl.loop(0, n_quads)
        def _(i):
            at = lax.rem(i, quads) * QUAD
            for u in range(QUAD):
                block_copy(i, u).wait()
            for u in range(0, QUAD, 2):
                p0, p1 = place_list[i * QUAD + u], place_list[i * QUAD + u + 1]
                same = jnp.where(p0 == p1, 1.0, 0.0).astype(F32)
                b0, b1 = ring[at + u].astype(F32), ring[at + u + 1].astype(F32)
                a0, a1 = acc[p0], acc[p1]
                acc[p0] = a0 + b0
                acc[p1] = a1 + (b1 + same * b0)

            @pl.when(i + quads < n_quads)
            def _():
                start_quad(i + quads)

        for j in range(panel_dev):
            if n_panels > 1:
                @pl.when(panel > 0)
                def _():
                    dense_copy(panel, j).wait()
                    result_copy(panel, j).wait()
            for b in range(dev_blocks):
                for cb in range(col_blocks):
                    hi, lo = split(acc[(j * dev_blocks + b) * col_blocks + cb])
                    lanes = slice(cb * EDGE, (cb + 1) * EDGE)
                    both[j, b * EDGE:(b + 1) * EDGE, lanes] = hi
                    both[j, node_dev + b * EDGE:node_dev + (b + 1) * EDGE, lanes] = lo
            dense_copy(panel, j).start()
            pair = jnp.dot(both[j], scaled[...], preferred_element_type=F32)
            result[j] = pair[:node_dev] + pair[node_dev:]
            result_copy(panel, j).start()

    if n_panels == 1:
        do_panel(0)
    else:
        @pl.loop(0, n_panels)
        def _(panel):
            do_panel(panel)

    for j in range(panel_dev):
        dense_copy(n_panels - 1, j).wait()
        result_copy(n_panels - 1, j).wait()


def middle_kernel(n_col, n_in, deg_ref, cot_ref, weight_ref, *refs):
    parts = refs[:n_in]
    act_ref, pulled_ref, prop_ref, gprime_ref, stage, sems = refs[n_in:]
    copies = fetch([(ref, stage.at[i]) for i, ref in enumerate(parts)], sems)
    node_dev = cot_ref.shape[0]
    dev_blocks = node_dev // EDGE
    base = (lax.axis_index("row") * n_col + lax.axis_index("col")) * dev_blocks
    inv = jnp.concatenate([inv_column(deg_ref, base + k) for k in range(dev_blocks)], axis=0)
    for copy in copies:
        copy.wait()
    summed = stage[0]
    for i in range(1, n_in):
        summed = summed + stage[i]
    propagated = inv * summed
    prop_ref[...] = propagated
    weight = weight_ref[...]
    pair = jnp.dot(jnp.concatenate(split(propagated), axis=0), weight, preferred_element_type=F32)
    v = pair[:node_dev] + pair[node_dev:]
    t = jnp.tanh(GELU_C * (v + GELU_K * v * v * v))
    act_ref[...] = (0.5 * v * (1.0 + t)).astype(BF16)
    slope = 0.5 * (1.0 + t) + 0.5 * v * (1.0 - t * t) * (GELU_C * (1.0 + 3.0 * GELU_K * v * v))
    gprime = cot_ref[...].astype(F32) * slope
    gprime_ref[...] = gprime
    pair = lax.dot_general(
        jnp.concatenate(split(gprime), axis=0), weight, (((1,), (1,)), ((), ())),
        preferred_element_type=F32,
    )
    pulled_ref[...] = jnp.transpose(inv * (pair[:node_dev] + pair[node_dev:]))


def add_kernel(*refs):
    total = refs[0][...]
    for ref in refs[1:-1]:
        total = total + ref[...]
    refs[-1][...] = total


def weight_kernel(scale, prop_ref, gprime_ref, keep_ref, send_ref):
    part = scale * lax.dot_general(
        prop_ref[...], gprime_ref[...], (((0,), (0,)), ((), ())),
        precision=HIGH, preferred_element_type=F32,
    )
    half = keep_ref.shape[0]
    low = lax.axis_index("col") % 2 == 0
    keep_ref[...] = jnp.where(low, part[:half], part[half:])
    send_ref[...] = jnp.where(low, part[half:], part[:half])


def load_lhs(parts, stage, lhs, copies):
    width = parts[0].shape[0]
    node_dev = parts[0].shape[1]
    for i in range(len(parts)):
        copies[i].wait()
        hi, lo = split(stage[i])
        lhs[:width, i * node_dev:(i + 1) * node_dev] = hi
        lhs[width:, i * node_dev:(i + 1) * node_dev] = lo


def partial_kernel(n_in, spans, *refs):
    n_dense = len(spans)
    tiles, parts = refs[:n_dense], refs[n_dense:n_dense + n_in]
    out_ref, dense, stage, lhs, sems, dense_sems = refs[n_dense + n_in:]
    width, node_dev = parts[0].shape
    col_nodes = dense.shape[1]
    blocks = fetch(
        [(tile, dense.at[pl.ds(at, size)]) for tile, (at, size) in zip(tiles, spans)], dense_sems)
    load_lhs(parts, stage, lhs, fetch([(r, stage.at[i]) for i, r in enumerate(parts)], sems))
    for copy in blocks:
        copy.wait()
    step = 2 * EDGE if col_nodes % (2 * EDGE) == 0 else EDGE
    for n in range(0, col_nodes, step):
        pair = jnp.dot(lhs[...], dense[:, n:n + step], preferred_element_type=F32)
        out_ref[:, n:n + step] = pair[:width] + pair[width:]


def last_kernel(n_in, n_out, deg_ref, dense_ref, sofar_ref, *refs):
    parts, outs = refs[:n_in], refs[n_in:n_in + n_out]
    dense, stage, lhs, sofar, sems, dense_sem, sofar_sem = refs[n_in + n_out:]
    width, node_dev = parts[0].shape
    col_nodes = dense.shape[1]
    block = pltpu.make_async_copy(dense_ref, dense, dense_sem)
    before = pltpu.make_async_copy(sofar_ref, sofar, sofar_sem)
    block.start()
    copies = fetch([(r, stage.at[i]) for i, r in enumerate(parts)], sems)
    before.start()
    load_lhs(parts, stage, lhs, copies)
    block.wait()
    before.wait()
    step = 2 * EDGE if col_nodes % (2 * EDGE) == 0 else EDGE
    size = col_nodes // n_out
    first = lax.axis_index("col") * (col_nodes // EDGE)
    for n in range(0, col_nodes, step):
        pair = jnp.dot(lhs[...], dense[:, n:n + step], preferred_element_type=F32)
        total = sofar[:, n:n + step] + (pair[:width] + pair[width:])
        for at in range(n, n + step, EDGE):
            inv = inv_column(deg_ref, first + at // EDGE)
            out = outs[at // size]
            out[at % size:at % size + EDGE, :] = inv * jnp.transpose(total[:, at - n:at - n + EDGE])


def body(n_row, n_col, features, degrees, block_rows, block_cols, live_slots, blocks, weight, cotangent):
    n_chip = n_col // 2
    chip_bits, row_bits = n_chip.bit_length() - 1, n_row.bit_length() - 1
    assert n_col == 2 << chip_bits and n_row == 1 << row_bits
    node_dev, hidden = cotangent.shape
    col_nodes, width = features.shape
    row_nodes = node_dev * n_col
    nodes = col_nodes * n_col
    slots = blocks.shape[2]
    deg = degrees.reshape(nodes // EDGE, EDGE)
    col_blocks = col_nodes // EDGE
    dev_blocks = node_dev // EDGE
    assert n_chip >= 4
    groups = [(n_chip - 1, 1), (1, n_chip - 2), (0, 1)]
    smem = pl.BlockSpec(memory_space=pltpu.SMEM)
    any_space = pl.BlockSpec(memory_space=pl.ANY)
    hbm = pl.BlockSpec(memory_space=pltpu.HBM)
    vmem = pl.BlockSpec(memory_space=pltpu.VMEM)

    def params(mib):
        return pltpu.CompilerParams(vmem_limit_bytes=mib << 20)

    def cost(flops, read):
        return pl.CostEstimate(flops=flops, bytes_accessed=read, transcendentals=0)

    def forward(first, units, after):
        panel = units
        while units % panel or 2 * panel * node_dev * col_nodes * 4 > ACC_BYTES:
            panel -= 1
        devs = 2 * panel
        return pl.pallas_call(
            functools.partial(forward_kernel, first, units // panel, node_dev),
            out_shape=(
                jax.ShapeDtypeStruct((units, node_dev, width), F32),
                jax.ShapeDtypeStruct((units, node_dev, width), F32),
                jax.ShapeDtypeStruct((units * 2 * node_dev, col_nodes), BF16),
            ),
            in_specs=[smem, smem, smem, vmem, vmem, hbm] + [any_space] * len(after),
            out_specs=(any_space, any_space, hbm),
            scratch_shapes=[
                pltpu.VMEM((devs * dev_blocks * col_blocks + 1, EDGE, EDGE), F32),
                pltpu.VMEM((devs, 2 * node_dev, col_nodes), BF16),
                pltpu.VMEM((RING, EDGE, EDGE), BF16),
                pltpu.VMEM((col_nodes, width), BF16),
                pltpu.VMEM((devs, node_dev, width), F32),
                pltpu.SMEM((slots + QUAD,), jnp.int32),
                pltpu.SMEM((slots + QUAD,), jnp.int32),
                pltpu.SemaphoreType.DMA((RING // QUAD,)),
                pltpu.SemaphoreType.DMA((devs,)),
                pltpu.SemaphoreType.DMA((devs,)),
            ],
            compiler_params=params(46 if after else 54),
            cost_estimate=cost(units * node_dev * col_nodes * width * 16, units * 5 << 20),
            name=f"forward_{first}",
        )(block_rows, block_cols, live_slots, deg, features, blocks, *after)

    swap_pairs = [(i, i ^ 1) for i in range(n_col)]

    def swap(x):
        return lax.ppermute(x, "col", swap_pairs)

    def chip_flip(x, bit):
        return lax.ppermute(x, "col", [(i, i ^ (2 << bit)) for i in range(n_col)])

    def row_flip(x, bit):
        return lax.ppermute(x, "row", [(i, i ^ (1 << bit)) for i in range(n_row)])

    def low_bit(m):
        return (m & -m).bit_length() - 1

    def add_up(*terms):
        return pl.pallas_call(
            add_kernel,
            out_shape=jax.ShapeDtypeStruct(terms[0].shape, F32),
            in_specs=[vmem] * len(terms),
            out_specs=vmem,
            compiler_params=params(16),
            cost_estimate=cost(0, 32 << 20),
            name="add_up",
        )(*terms)

    kept, got, arrived, tiles = {}, {}, {}, []

    def unit_sum(m):
        return (add_up(kept[m], *arrived[m]) if m in arrived else kept[m]) + got[m]

    def forward_group(i, after, sends):
        first, units = groups[i]
        loads = [unit_sum(m) for m in sends]
        keep, send, tile = forward(first, units, after)
        moved = [chip_flip(x, low_bit(m)) for x, m in zip(loads, sends)]
        for x, m in zip(moved, sends):
            arrived.setdefault(m & (m - 1), []).append(x)
        tiles.append(tile)
        for j in range(units):
            kept[first + j], got[first + j] = keep[j], swap(send[j])

    forward_group(0, [], [])
    last = n_chip - 1
    forward_group(1, [unit_sum(last)], [last])
    for m in range(last - 1, 2, -1):
        arrived.setdefault(m & (m - 1), []).append(chip_flip(unit_sum(m), low_bit(m)))
    forward_group(2, [unit_sum(1)], [2, 1])
    parts = [kept[0], got[0], add_up(*arrived[0])]

    out_act, pulled, prop, gprime = pl.pallas_call(
        functools.partial(middle_kernel, n_col, len(parts)),
        out_shape=(
            jax.ShapeDtypeStruct((node_dev, hidden), BF16),
            jax.ShapeDtypeStruct((width, node_dev), F32),
            jax.ShapeDtypeStruct((node_dev, width), F32),
            jax.ShapeDtypeStruct((node_dev, hidden), F32),
        ),
        in_specs=[vmem] * 3 + [any_space] * len(parts),
        out_specs=(vmem,) * 4,
        scratch_shapes=[
            pltpu.VMEM((len(parts), node_dev, width), F32),
            pltpu.SemaphoreType.DMA((len(parts),)),
        ],
        compiler_params=params(16),
        name="middle",
    )(deg, cotangent, weight, *parts)

    own = {0: pulled}
    for m in (1, 2):
        own[m] = chip_flip(pulled, low_bit(m))
    other = {0: swap(pulled)}
    half = width // 2
    wkeep, wsend = pl.pallas_call(
        functools.partial(weight_kernel, float(nodes) ** (-0.5)),
        out_shape=(jax.ShapeDtypeStruct((half, hidden), F32),) * 2,
        in_specs=[vmem] * 2,
        out_specs=(vmem,) * 2,
        compiler_params=params(16),
        name="weight_part",
    )(prop, gprime)

    wsum = wkeep + swap(wsend)
    for m in range(3, n_chip):
        own[m] = chip_flip(own[m & (m - 1)], low_bit(m))
    for m in range(1, n_chip):
        other[m] = swap(own[m])
    wsum = wsum + row_flip(wsum, 0)
    for t in range(1, row_bits):
        wsum = wsum + row_flip(wsum, t)

    early = [x for m in range(n_chip - 1) for x in (own[m], other[m])]
    late = [own[n_chip - 1], other[n_chip - 1]]
    spans = [(0, 2 * node_dev), (2 * node_dev, (n_chip - 2) * 2 * node_dev)]
    tile_mib = row_nodes * col_nodes * 2 >> 20
    sofar = pl.pallas_call(
        functools.partial(partial_kernel, len(early), spans),
        out_shape=jax.ShapeDtypeStruct((width, col_nodes), F32),
        in_specs=[hbm] * 2 + [any_space] * len(early),
        out_specs=vmem,
        scratch_shapes=[
            pltpu.VMEM((len(early) * node_dev, col_nodes), BF16),
            pltpu.VMEM((len(early), width, node_dev), F32),
            pltpu.VMEM((2 * width, len(early) * node_dev), BF16),
            pltpu.SemaphoreType.DMA((len(early),)),
            pltpu.SemaphoreType.DMA((2,)),
        ],
        compiler_params=params(tile_mib + 20),
        name="backward_early",
    )(tiles[2], tiles[1], *early)

    n_piece = max(1, row_bits)
    while col_nodes % (EDGE * n_piece):
        n_piece -= 1
    size = col_nodes // n_piece
    done = pl.pallas_call(
        functools.partial(last_kernel, len(late), n_piece),
        out_shape=(jax.ShapeDtypeStruct((size, width), F32),) * n_piece,
        in_specs=[vmem, hbm, any_space] + [any_space] * len(late),
        out_specs=(vmem,) * n_piece,
        scratch_shapes=[
            pltpu.VMEM((len(late) * node_dev, col_nodes), BF16),
            pltpu.VMEM((len(late), width, node_dev), F32),
            pltpu.VMEM((2 * width, len(late) * node_dev), BF16),
            pltpu.VMEM((width, col_nodes), F32),
            pltpu.SemaphoreType.DMA((len(late),)),
            pltpu.SemaphoreType.DMA,
            pltpu.SemaphoreType.DMA,
        ],
        compiler_params=params(16),
        name="backward_late",
    )(deg, tiles[0], sofar, *late)

    for t in range(row_bits):
        done = [x + row_flip(x, (i + t) % row_bits) for i, x in enumerate(done)]
        if t == 0:
            for bit in range(chip_bits):
                wsum = wsum + chip_flip(wsum, bit)
    feat_grad = jnp.concatenate(done, axis=0) if n_piece > 1 else done[0]

    wother = swap(wsum)
    low = lax.axis_index("col") % 2 == 0
    weight_grad = jnp.concatenate(
        [jnp.where(low, wsum, wother), jnp.where(low, wother, wsum)], axis=0
    )
    return out_act, feat_grad, weight_grad


def solution(mesh):
    n_row, n_col = mesh.shape["row"], mesh.shape["col"]
    return jax.shard_map(
        functools.partial(body, n_row, n_col),
        mesh=mesh,
        in_specs=(
            P("col", None),
            P(),
            P("row", "col", None),
            P("row", "col", None),
            P("row", "col"),
            P("row", "col", None, None, None),
            P(),
            P(("row", "col"), None),
        ),
        out_specs=(P(("row", "col"), None), P("col", None), P()),
        check_vma=False,
    )
```

```python
import functools

import jax
import jax.numpy as jnp
from jax import lax
from jax.experimental import pallas as pl
from jax.experimental.pallas import tpu as pltpu
from jax.sharding import PartitionSpec as P

HIGH = lax.Precision.HIGHEST
F32 = jnp.float32
BF16 = jnp.bfloat16
EDGE = 128
GROUP = 16
QUARTERS = 4
AHEAD = 2
ACC_BYTES = 8 << 20
GELU_C = 0.7978845608028654
GELU_K = 0.044715


def inv_column(deg_ref, start):
    row = lax.rsqrt(deg_ref[pl.ds(start, 1), :].astype(F32))
    return jnp.transpose(jnp.broadcast_to(row, (EDGE, EDGE)))


def split(value):
    hi = value.astype(BF16)
    return hi, (value - hi.astype(F32)).astype(BF16)


def fetch(pairs, sems):
    copies = [pltpu.make_async_copy(src, dst, sems.at[i]) for i, (src, dst) in enumerate(pairs)]
    for copy in copies:
        copy.start()
    return copies


def halve(value, size):
    if size & (size - 1) == 0:
        shift = size.bit_length() - 1
        return lax.shift_right_logical(value, shift), value & (size - 1)
    return lax.div(value, size), lax.rem(value, size)


def forward_kernel(
    n_col, chunk, panel_dev, node_dev,
    rows_ref, cols_ref, live_ref, deg_ref, feat_ref, blocks_ref, *refs,
):
    outs, dense_ref = refs[:n_col], refs[n_col]
    accs, (both, buf, scaled, result, in_sems, dense_sems, out_sems) = refs[n_col + 1:-7], refs[-7:]
    part = EDGE // len(accs)
    slots = buf.shape[0]
    col_nodes, width = feat_ref.shape
    col_blocks = col_nodes // EDGE
    dev_blocks = node_dev // EDGE
    panel_blocks = panel_dev * dev_blocks
    positions = panel_blocks * col_blocks
    n_panels = n_col // panel_dev
    n_chunks = slots // chunk
    me = lax.axis_index("col")
    live = live_ref[0, 0]

    def block_copy(c):
        span = pl.ds(c * chunk, chunk)
        return pltpu.make_async_copy(blocks_ref.at[0, 0, span], buf.at[span], in_sems.at[c])

    def dense_copy(panel, j):
        there = pl.ds((panel * panel_dev + j) * node_dev, node_dev)
        return pltpu.make_async_copy(
            both.at[j, pl.ds(0, node_dev)], dense_ref.at[there], dense_sems.at[j])

    def result_copy(rel, j):
        return pltpu.make_async_copy(result.at[j], outs[rel], out_sems.at[j])

    for c in range(n_chunks):
        block_copy(c).start()

    for k in range(col_blocks):
        inv = inv_column(deg_ref, me * col_blocks + k)
        span = pl.ds(k * EDGE, EDGE)
        scaled[span, :] = (inv * feat_ref[span, :].astype(F32)).astype(BF16)

    def add_slots(first, place):
        pending = []

        def finish():
            acc, p0, p1, same, a0, a1, b0, b1 = pending.pop(0)
            b0, b1 = b0.astype(F32), b1.astype(F32)
            acc[p0] = a0 + b0
            acc[p1] = a1 + (b1 + same * b0)

        for u in range(0, GROUP, 2):
            s = first + u
            p0, p1 = place(s), place(s + 1)
            same = jnp.where(p0 == p1, 1.0, 0.0).astype(F32)
            for q, acc in enumerate(accs):
                at = slice(q * part, (q + 1) * part)
                pending.append((acc, p0, p1, same, acc[p0], acc[p1], buf[s, at, :], buf[s + 1, at, :]))
                if len(pending) > AHEAD:
                    finish()
        while pending:
            finish()

    for panel in range(n_panels):
        base = panel * panel_blocks

        @pl.loop(0, positions)
        def _(p):
            for acc in accs:
                acc[p] = jnp.zeros((part, EDGE), F32)

        def place(s):
            dev, inner = halve(rows_ref[0, 0, s], dev_blocks)
            r = (dev ^ me) * dev_blocks + inner - base
            ok = s < live
            if n_panels > 1:
                ok = ok & (r >= 0) & (r < panel_blocks)
            return jnp.where(ok, r * col_blocks + cols_ref[0, 0, s], positions)

        @pl.loop(0, n_chunks)
        def _(c):
            if panel == 0:
                block_copy(c).wait()

            @pl.loop(0, chunk // GROUP)
            def _(g):
                add_slots(c * chunk + g * GROUP, place)

        for j in reversed(range(panel_dev)):
            rel = panel * panel_dev + j
            if panel:
                dense_copy(panel - 1, j).wait()
                result_copy(rel - panel_dev, j).wait()
            for b in range(dev_blocks):
                for cb in range(col_blocks):
                    lanes = slice(cb * EDGE, (cb + 1) * EDGE)
                    for q, acc in enumerate(accs):
                        hi, lo = split(acc[(j * dev_blocks + b) * col_blocks + cb])
                        at = b * EDGE + q * part
                        both[j, at:at + part, lanes] = hi
                        both[j, node_dev + at:node_dev + at + part, lanes] = lo
            dense_copy(panel, j).start()
            pair = jnp.dot(both[j], scaled[...], preferred_element_type=F32)
            result[j] = pair[:node_dev] + pair[node_dev:]
            result_copy(rel, j).start()

    for j in range(panel_dev):
        dense_copy(n_panels - 1, j).wait()
        result_copy((n_panels - 1) * panel_dev + j, j).wait()


def middle_kernel(n_col, n_in, deg_ref, cot_ref, weight_ref, *refs):
    parts = refs[:n_in]
    act_ref, pulled_ref, prop_ref, gprime_ref, stage, sems = refs[n_in:]
    copies = fetch([(ref, stage.at[i]) for i, ref in enumerate(parts)], sems)
    node_dev = cot_ref.shape[0]
    dev_blocks = node_dev // EDGE
    base = (lax.axis_index("row") * n_col + lax.axis_index("col")) * dev_blocks
    inv = jnp.concatenate([inv_column(deg_ref, base + k) for k in range(dev_blocks)], axis=0)
    for copy in copies:
        copy.wait()
    summed = stage[0]
    for i in range(1, n_in):
        summed = summed + stage[i]
    propagated = inv * summed
    prop_ref[...] = propagated
    weight = weight_ref[...]
    pair = jnp.dot(jnp.concatenate(split(propagated), axis=0), weight, preferred_element_type=F32)
    v = pair[:node_dev] + pair[node_dev:]
    t = jnp.tanh(GELU_C * (v + GELU_K * v * v * v))
    act_ref[...] = (0.5 * v * (1.0 + t)).astype(BF16)
    slope = 0.5 * (1.0 + t) + 0.5 * v * (1.0 - t * t) * (GELU_C * (1.0 + 3.0 * GELU_K * v * v))
    gprime = cot_ref[...].astype(F32) * slope
    gprime_ref[...] = gprime
    pair = lax.dot_general(
        jnp.concatenate(split(gprime), axis=0), weight, (((1,), (1,)), ((), ())),
        preferred_element_type=F32,
    )
    pulled_ref[...] = jnp.transpose(inv * (pair[:node_dev] + pair[node_dev:]))


def add_kernel(*refs):
    total = refs[0][...]
    for ref in refs[1:-1]:
        total = total + ref[...]
    refs[-1][...] = total


def weight_kernel(scale, prop_ref, gprime_ref, after_ref, keep_ref, send_ref):
    part = scale * lax.dot_general(
        prop_ref[...], gprime_ref[...], (((0,), (0,)), ((), ())),
        precision=HIGH, preferred_element_type=F32,
    )
    half = keep_ref.shape[0]
    low = lax.axis_index("col") % 2 == 0
    keep_ref[...] = jnp.where(low, part[:half], part[half:])
    send_ref[...] = jnp.where(low, part[half:], part[:half])


def load_lhs(parts, stage, lhs, copies):
    width = parts[0].shape[0]
    node_dev = parts[0].shape[1]
    for i in range(len(parts)):
        copies[i].wait()
        hi, lo = split(stage[i])
        lhs[:width, i * node_dev:(i + 1) * node_dev] = hi
        lhs[width:, i * node_dev:(i + 1) * node_dev] = lo


def partial_kernel(n_in, dense_ref, *refs):
    parts, (out_ref, dense, stage, lhs, sems, dense_sems) = refs[:n_in], refs[n_in:]
    width, node_dev = parts[0].shape
    col_nodes = dense.shape[1]
    blocks = fetch(
        [(dense_ref.at[pl.ds(i * node_dev, node_dev)], dense.at[pl.ds(i * node_dev, node_dev)])
         for i in range(n_in)], dense_sems)
    load_lhs(parts, stage, lhs, fetch([(r, stage.at[i]) for i, r in enumerate(parts)], sems))
    for copy in blocks:
        copy.wait()
    step = 2 * EDGE if col_nodes % (2 * EDGE) == 0 else EDGE
    for n in range(0, col_nodes, step):
        pair = jnp.dot(lhs[...], dense[:, n:n + step], preferred_element_type=F32)
        out_ref[:, n:n + step] = pair[:width] + pair[width:]


def last_kernel(n_in, n_out, deg_ref, dense_ref, sofar_ref, wsum_ref, *refs):
    parts, outs = refs[:n_in], refs[n_in:n_in + n_out]
    dense, stage, lhs, sofar, sems, dense_sem, sofar_sem = refs[n_in + n_out:]
    width, node_dev = parts[0].shape
    col_nodes = dense.shape[1]
    rows = n_in * node_dev
    block = pltpu.make_async_copy(
        dense_ref.at[pl.ds(dense_ref.shape[0] - rows, rows)], dense, dense_sem)
    before = pltpu.make_async_copy(sofar_ref, sofar, sofar_sem)
    block.start()
    size = col_nodes // n_out
    lanes = wsum_ref.shape[1] // n_out
    for i, out in enumerate(outs):
        for n in range(0, lanes, EDGE):
            at = size + wsum_ref.shape[0] * (n // EDGE)
            out[at:at + wsum_ref.shape[0], :] = wsum_ref[:, i * lanes + n:i * lanes + n + EDGE]
    copies = fetch([(r, stage.at[i]) for i, r in enumerate(parts)], sems)
    before.start()
    load_lhs(parts, stage, lhs, copies)
    block.wait()
    before.wait()
    step = 2 * EDGE if col_nodes % (2 * EDGE) == 0 else EDGE
    first = lax.axis_index("col") * (col_nodes // EDGE)
    for n in range(0, col_nodes, step):
        pair = jnp.dot(lhs[...], dense[:, n:n + step], preferred_element_type=F32)
        total = sofar[:, n:n + step] + (pair[:width] + pair[width:])
        for at in range(n, n + step, EDGE):
            inv = inv_column(deg_ref, first + at // EDGE)
            out = outs[at // size]
            out[at % size:at % size + EDGE, :] = inv * jnp.transpose(total[:, at - n:at - n + EDGE])


def body(n_row, n_col, features, degrees, block_rows, block_cols, live_slots, blocks, weight, cotangent):
    n_chip = n_col // 2
    chip_bits, row_bits = n_chip.bit_length() - 1, n_row.bit_length() - 1
    assert n_col == 2 << chip_bits and n_row == 1 << row_bits
    node_dev, hidden = cotangent.shape
    col_nodes, width = features.shape
    row_nodes = node_dev * n_col
    nodes = col_nodes * n_col
    slots = blocks.shape[2]
    deg = degrees.reshape(nodes // EDGE, EDGE)
    col_blocks = col_nodes // EDGE
    dev_blocks = node_dev // EDGE
    assert n_chip >= 4
    chunk = 32
    panel_dev = n_col
    while panel_dev % 2 == 0 and panel_dev * node_dev * col_nodes * 4 > ACC_BYTES:
        panel_dev //= 2
    positions = panel_dev * dev_blocks * col_blocks
    smem = pl.BlockSpec(memory_space=pltpu.SMEM)
    any_space = pl.BlockSpec(memory_space=pl.ANY)
    vmem = pl.BlockSpec(memory_space=pltpu.VMEM)

    def params(mib):
        return pltpu.CompilerParams(vmem_limit_bytes=mib << 20)

    def cost(flops, read):
        return pl.CostEstimate(flops=flops, bytes_accessed=read, transcendentals=0)

    *pieces, tile = pl.pallas_call(
        functools.partial(forward_kernel, n_col, chunk, panel_dev, node_dev),
        out_shape=[jax.ShapeDtypeStruct((node_dev, width), F32)] * n_col
        + [jax.ShapeDtypeStruct((row_nodes, col_nodes), BF16)],
        in_specs=[smem, smem, smem, vmem, vmem, any_space],
        out_specs=[any_space] * (n_col + 1),
        scratch_shapes=[
            pltpu.VMEM((positions + 1, EDGE // QUARTERS, EDGE), F32) for _ in range(QUARTERS)
        ] + [
            pltpu.VMEM((panel_dev, 2 * node_dev, col_nodes), BF16),
            pltpu.VMEM((slots, EDGE, EDGE), BF16),
            pltpu.VMEM((col_nodes, width), BF16),
            pltpu.VMEM((panel_dev, node_dev, width), F32),
            pltpu.SemaphoreType.DMA((slots // chunk,)),
            pltpu.SemaphoreType.DMA((panel_dev,)),
            pltpu.SemaphoreType.DMA((panel_dev,)),
        ],
        compiler_params=params(54),
        name="densify_forward",
    )(block_rows, block_cols, live_slots, deg, features, blocks)
    keep, send = pieces[0::2], pieces[1::2]

    swap_pairs = [(i, i ^ 1) for i in range(n_col)]

    def swap(x):
        return lax.ppermute(x, "col", swap_pairs)

    def chip_flip(x, bit):
        return lax.ppermute(x, "col", [(i, i ^ (2 << bit)) for i in range(n_col)])

    def row_flip(x, bit):
        return lax.ppermute(x, "row", [(i, i ^ (1 << bit)) for i in range(n_row)])

    def low_bit(m):
        return (m & -m).bit_length() - 1

    terms = {m: [keep[m], swap(send[m])] for m in range(n_chip - 1, -1, -1)}
    for m in range(n_chip - 1, 0, -1):
        terms[m & (m - 1)].append(chip_flip(functools.reduce(jnp.add, terms[m]), low_bit(m)))
    parts = terms[0]

    out_act, pulled, prop, gprime = pl.pallas_call(
        functools.partial(middle_kernel, n_col, len(parts)),
        out_shape=(
            jax.ShapeDtypeStruct((node_dev, hidden), BF16),
            jax.ShapeDtypeStruct((width, node_dev), F32),
            jax.ShapeDtypeStruct((node_dev, width), F32),
            jax.ShapeDtypeStruct((node_dev, hidden), F32),
        ),
        in_specs=[vmem] * 3 + [any_space] * len(parts),
        out_specs=(vmem,) * 4,
        scratch_shapes=[
            pltpu.VMEM((len(parts), node_dev, width), F32),
            pltpu.SemaphoreType.DMA((len(parts),)),
        ],
        compiler_params=params(16),
        name="middle",
    )(deg, cotangent, weight, *parts)

    own = {0: pulled}
    for m in (1, 2):
        own[m] = chip_flip(pulled, low_bit(m))
    other = {0: swap(pulled)}
    half = width // 2
    wkeep, wsend = pl.pallas_call(
        functools.partial(weight_kernel, float(nodes) ** (-0.5)),
        out_shape=(jax.ShapeDtypeStruct((half, hidden), F32),) * 2,
        in_specs=[vmem] * 2 + [any_space],
        out_specs=(vmem,) * 2,
        compiler_params=params(16),
        name="weight_part",
    )(prop, gprime, other[0])

    wsum = wkeep + swap(wsend)
    for m in range(3, n_chip):
        own[m] = chip_flip(own[m & (m - 1)], low_bit(m))
    for m in range(1, n_chip):
        other[m] = swap(own[m])
    for t in range(chip_bits):
        wsum = wsum + chip_flip(wsum, t)

    early = [x for m in range(n_chip - 1) for x in (own[m], other[m])]
    late = [own[n_chip - 1], other[n_chip - 1]]
    sofar = pl.pallas_call(
        functools.partial(partial_kernel, len(early)),
        out_shape=jax.ShapeDtypeStruct((width, col_nodes), F32),
        in_specs=[any_space] * (1 + len(early)),
        out_specs=vmem,
        scratch_shapes=[
            pltpu.VMEM((len(early) * node_dev, col_nodes), BF16),
            pltpu.VMEM((len(early), width, node_dev), F32),
            pltpu.VMEM((2 * width, len(early) * node_dev), BF16),
            pltpu.SemaphoreType.DMA((len(early),)),
            pltpu.SemaphoreType.DMA((len(early),)),
        ],
        compiler_params=params(52),
        name="backward_early",
    )(tile, *early)

    n_piece = max(1, row_bits)
    while col_nodes % (EDGE * n_piece):
        n_piece -= 1
    size = col_nodes // n_piece
    extra = half * hidden // n_piece // EDGE
    done = pl.pallas_call(
        functools.partial(last_kernel, len(late), n_piece),
        out_shape=(jax.ShapeDtypeStruct((size + extra, width), F32),) * n_piece,
        in_specs=[vmem, any_space, any_space, vmem] + [any_space] * len(late),
        out_specs=(vmem,) * n_piece,
        scratch_shapes=[
            pltpu.VMEM((len(late) * node_dev, col_nodes), BF16),
            pltpu.VMEM((len(late), width, node_dev), F32),
            pltpu.VMEM((2 * width, len(late) * node_dev), BF16),
            pltpu.VMEM((width, col_nodes), F32),
            pltpu.SemaphoreType.DMA((len(late),)),
            pltpu.SemaphoreType.DMA,
            pltpu.SemaphoreType.DMA,
        ],
        compiler_params=params(52),
        name="backward_late",
    )(deg, tile, sofar, wsum, *late)

    for t in range(row_bits):
        done = [x + row_flip(x, (i + t) % row_bits) for i, x in enumerate(done)]
    feat_grad = jnp.concatenate([x[:size] for x in done], axis=0)
    wsum = jnp.concatenate(
        [x[size + i:size + i + half] for x in done for i in range(0, extra, half)], axis=1)

    wother = swap(wsum)
    low = lax.axis_index("col") % 2 == 0
    weight_grad = jnp.concatenate(
        [jnp.where(low, wsum, wother), jnp.where(low, wother, wsum)], axis=0
    )
    return out_act, feat_grad, weight_grad


def solution(mesh):
    n_row, n_col = mesh.shape["row"], mesh.shape["col"]
    return jax.shard_map(
        functools.partial(body, n_row, n_col),
        mesh=mesh,
        in_specs=(
            P("col", None),
            P(),
            P("row", "col", None),
            P("row", "col", None),
            P("row", "col"),
            P("row", "col", None, None, None),
            P(),
            P(("row", "col"), None),
        ),
        out_specs=(P(("row", "col"), None), P("col", None), P()),
        check_vma=False,
    )
```

```python
import functools

import jax
import jax.numpy as jnp
from jax import lax
from jax.experimental import pallas as pl
from jax.experimental.pallas import tpu as pltpu
from jax.sharding import PartitionSpec as P

F32 = jnp.float32
BF16 = jnp.bfloat16
EDGE = 128
GROUP = 16
QUARTERS = 4
AHEAD = 2
FWD = 46
ACC_BYTES = 8 << 20
GELU_C = 0.7978845608028654
GELU_K = 0.044715


def inv_column(deg_ref, start):
    row = lax.rsqrt(deg_ref[pl.ds(start, 1), :].astype(F32))
    return jnp.transpose(jnp.broadcast_to(row, (EDGE, EDGE)))


def split(value):
    hi = value.astype(BF16)
    return hi, (value - hi.astype(F32)).astype(BF16)


def across(a, b):
    return lax.dot_general(a, b, (((0,), (0,)), ((), ())), preferred_element_type=F32)


def fetch(pairs, sems):
    copies = [pltpu.make_async_copy(src, dst, sems.at[i]) for i, (src, dst) in enumerate(pairs)]
    for copy in copies:
        copy.start()
    return copies


def halve(value, size):
    if size & (size - 1) == 0:
        shift = size.bit_length() - 1
        return lax.shift_right_logical(value, shift), value & (size - 1)
    return lax.div(value, size), lax.rem(value, size)


def forward_kernel(
    n_col, chunk, panel_dev, node_dev,
    rows_ref, cols_ref, live_ref, deg_ref, feat_ref, blocks_ref, *refs,
):
    outs, dense_ref = refs[:n_col], refs[n_col]
    accs, (both, buf, scaled, result, in_sems, dense_sems, out_sems) = refs[n_col + 1:-7], refs[-7:]
    part = EDGE // len(accs)
    slots = buf.shape[0]
    col_nodes, width = feat_ref.shape
    col_blocks = col_nodes // EDGE
    dev_blocks = node_dev // EDGE
    panel_blocks = panel_dev * dev_blocks
    positions = panel_blocks * col_blocks
    n_panels = n_col // panel_dev
    n_chunks = slots // chunk
    me = lax.axis_index("col")
    live = live_ref[0, 0]

    def block_copy(c):
        span = pl.ds(c * chunk, chunk)
        return pltpu.make_async_copy(blocks_ref.at[0, 0, span], buf.at[span], in_sems.at[c])

    def dense_copy(panel, j):
        there = pl.ds((panel * panel_dev + j) * node_dev, node_dev)
        return pltpu.make_async_copy(
            both.at[j, pl.ds(0, node_dev)], dense_ref.at[there], dense_sems.at[j])

    def result_copy(rel, j):
        return pltpu.make_async_copy(result.at[j], outs[rel], out_sems.at[j])

    for c in range(n_chunks):
        block_copy(c).start()

    for k in range(col_blocks):
        inv = inv_column(deg_ref, me * col_blocks + k)
        span = pl.ds(k * EDGE, EDGE)
        scaled[span, :] = (inv * feat_ref[span, :].astype(F32)).astype(BF16)

    def add_slots(first, place):
        pending = []

        def finish():
            acc, p0, p1, same, a0, a1, b0, b1 = pending.pop(0)
            b0, b1 = b0.astype(F32), b1.astype(F32)
            acc[p0] = a0 + b0
            acc[p1] = a1 + (b1 + same * b0)

        for u in range(0, GROUP, 2):
            s = first + u
            p0, p1 = place(s), place(s + 1)
            same = jnp.where(p0 == p1, 1.0, 0.0).astype(F32)
            for q, acc in enumerate(accs):
                at = slice(q * part, (q + 1) * part)
                pending.append((acc, p0, p1, same, acc[p0], acc[p1], buf[s, at, :], buf[s + 1, at, :]))
                if len(pending) > AHEAD:
                    finish()
        while pending:
            finish()

    for panel in range(n_panels):
        base = panel * panel_blocks

        @pl.loop(0, positions)
        def _(p):
            for acc in accs:
                acc[p] = jnp.zeros((part, EDGE), F32)

        def place(s):
            dev, inner = halve(rows_ref[0, 0, s], dev_blocks)
            r = (dev ^ me) * dev_blocks + inner - base
            ok = s < live
            if n_panels > 1:
                ok = ok & (r >= 0) & (r < panel_blocks)
            return jnp.where(ok, r * col_blocks + cols_ref[0, 0, s], positions)

        @pl.loop(0, n_chunks)
        def _(c):
            if panel == 0:
                block_copy(c).wait()

            @pl.loop(0, chunk // GROUP)
            def _(g):
                add_slots(c * chunk + g * GROUP, place)

        for j in reversed(range(panel_dev)):
            rel = panel * panel_dev + j
            if panel:
                dense_copy(panel - 1, j).wait()
                result_copy(rel - panel_dev, j).wait()
            for b in range(dev_blocks):
                for cb in range(col_blocks):
                    lanes = slice(cb * EDGE, (cb + 1) * EDGE)
                    for q, acc in enumerate(accs):
                        hi, lo = split(acc[(j * dev_blocks + b) * col_blocks + cb])
                        at = b * EDGE + q * part
                        both[j, at:at + part, lanes] = hi
                        both[j, node_dev + at:node_dev + at + part, lanes] = lo
            dense_copy(panel, j).start()
            pair = jnp.dot(both[j], scaled[...], preferred_element_type=F32)
            result[j] = pair[:node_dev] + pair[node_dev:]
            result_copy(rel, j).start()

    for j in range(panel_dev):
        dense_copy(n_panels - 1, j).wait()
        result_copy((n_panels - 1) * panel_dev + j, j).wait()


def middle_kernel(n_col, n_in, scale, deg_ref, cot_ref, weight_ref, *refs):
    parts = refs[:n_in]
    act_ref, pulled_ref, keep_ref, send_ref = refs[n_in:]
    node_dev = cot_ref.shape[0]
    dev_blocks = node_dev // EDGE
    base = (lax.axis_index("row") * n_col + lax.axis_index("col")) * dev_blocks
    inv = jnp.concatenate([inv_column(deg_ref, base + k) for k in range(dev_blocks)], axis=0)
    summed = parts[0][...]
    for ref in parts[1:]:
        summed = summed + ref[...]
    propagated = inv * summed
    prop_hi, prop_lo = split(propagated)
    weight = weight_ref[...]
    pair = jnp.dot(
        jnp.concatenate([prop_hi, prop_lo], axis=0), weight, preferred_element_type=F32)
    v = pair[:node_dev] + pair[node_dev:]
    t = jnp.tanh(GELU_C * (v + GELU_K * v * v * v))
    act_ref[...] = (0.5 * v * (1.0 + t)).astype(BF16)
    slope = 0.5 * (1.0 + t) + 0.5 * v * (1.0 - t * t) * (GELU_C * (1.0 + 3.0 * GELU_K * v * v))
    gprime = cot_ref[...].astype(F32) * slope
    hi, lo = split(gprime)
    pair = lax.dot_general(
        jnp.concatenate([hi, lo], axis=0), weight, (((1,), (1,)), ((), ())),
        preferred_element_type=F32,
    )
    pulled_ref[...] = jnp.transpose(inv * (pair[:node_dev] + pair[node_dev:]))
    pair = across(jnp.concatenate([prop_hi, prop_lo], axis=1), hi)
    part = scale * (pair[:EDGE] + (pair[EDGE:] + across(prop_hi, lo)))
    half = keep_ref.shape[0]
    low = lax.axis_index("col") % 2 == 0
    keep_ref[...] = jnp.where(low, part[:half], part[half:])
    send_ref[...] = jnp.where(low, part[half:], part[:half])


def load_lhs(parts, stage, lhs, copies):
    width = parts[0].shape[0]
    node_dev = parts[0].shape[1]
    for i in range(len(parts)):
        copies[i].wait()
        hi, lo = split(stage[i])
        lhs[:width, i * node_dev:(i + 1) * node_dev] = hi
        lhs[width:, i * node_dev:(i + 1) * node_dev] = lo


def partial_kernel(n_in, dense_ref, *refs):
    parts, (out_ref, dense, stage, lhs, sems, dense_sems) = refs[:n_in], refs[n_in:]
    width, node_dev = parts[0].shape
    col_nodes = dense.shape[1]
    blocks = fetch(
        [(dense_ref.at[pl.ds(i * node_dev, node_dev)], dense.at[pl.ds(i * node_dev, node_dev)])
         for i in range(n_in)], dense_sems)
    load_lhs(parts, stage, lhs, fetch([(r, stage.at[i]) for i, r in enumerate(parts)], sems))
    for copy in blocks:
        copy.wait()
    step = 2 * EDGE if col_nodes % (2 * EDGE) == 0 else EDGE
    for n in range(0, col_nodes, step):
        pair = jnp.dot(lhs[...], dense[:, n:n + step], preferred_element_type=F32)
        out_ref[:, n:n + step] = pair[:width] + pair[width:]


def last_kernel(n_in, n_out, deg_ref, dense_ref, sofar_ref, wsum_ref, *refs):
    parts, outs = refs[:n_in], refs[n_in:n_in + n_out]
    dense, stage, lhs, sofar, sems, dense_sem, sofar_sem = refs[n_in + n_out:]
    width, node_dev = parts[0].shape
    col_nodes = dense.shape[1]
    rows = n_in * node_dev
    block = pltpu.make_async_copy(
        dense_ref.at[pl.ds(dense_ref.shape[0] - rows, rows)], dense, dense_sem)
    before = pltpu.make_async_copy(sofar_ref, sofar, sofar_sem)
    block.start()
    size = col_nodes // n_out
    lanes = wsum_ref.shape[1] // n_out
    for i, out in enumerate(outs):
        for n in range(0, lanes, EDGE):
            at = size + wsum_ref.shape[0] * (n // EDGE)
            out[at:at + wsum_ref.shape[0], :] = wsum_ref[:, i * lanes + n:i * lanes + n + EDGE]
    copies = fetch([(r, stage.at[i]) for i, r in enumerate(parts)], sems)
    before.start()
    load_lhs(parts, stage, lhs, copies)
    block.wait()
    before.wait()
    step = 2 * EDGE if col_nodes % (2 * EDGE) == 0 else EDGE
    first = lax.axis_index("col") * (col_nodes // EDGE)
    for n in range(0, col_nodes, step):
        pair = jnp.dot(lhs[...], dense[:, n:n + step], preferred_element_type=F32)
        total = sofar[:, n:n + step] + (pair[:width] + pair[width:])
        for at in range(n, n + step, EDGE):
            inv = inv_column(deg_ref, first + at // EDGE)
            out = outs[at // size]
            out[at % size:at % size + EDGE, :] = inv * jnp.transpose(total[:, at - n:at - n + EDGE])


def body(n_row, n_col, features, degrees, block_rows, block_cols, live_slots, blocks, weight, cotangent):
    n_chip = n_col // 2
    chip_bits, row_bits = n_chip.bit_length() - 1, n_row.bit_length() - 1
    assert n_col == 2 << chip_bits and n_row == 1 << row_bits
    node_dev, hidden = cotangent.shape
    col_nodes, width = features.shape
    row_nodes = node_dev * n_col
    nodes = col_nodes * n_col
    slots = blocks.shape[2]
    deg = degrees.reshape(nodes // EDGE, EDGE)
    col_blocks = col_nodes // EDGE
    dev_blocks = node_dev // EDGE
    assert n_chip >= 4
    chunk = 32
    panel_dev = n_col
    while panel_dev % 2 == 0 and panel_dev * node_dev * col_nodes * 4 > ACC_BYTES:
        panel_dev //= 2
    positions = panel_dev * dev_blocks * col_blocks
    smem = pl.BlockSpec(memory_space=pltpu.SMEM)
    any_space = pl.BlockSpec(memory_space=pl.ANY)
    vmem = pl.BlockSpec(memory_space=pltpu.VMEM)

    def params(mib):
        return pltpu.CompilerParams(vmem_limit_bytes=mib << 20)

    def after(x, other):
        return x + 0.0 * other[0, 0]

    def cost(flops, read):
        return pl.CostEstimate(flops=flops, bytes_accessed=read, transcendentals=0)

    *pieces, tile = pl.pallas_call(
        functools.partial(forward_kernel, n_col, chunk, panel_dev, node_dev),
        out_shape=[jax.ShapeDtypeStruct((node_dev, width), F32)] * n_col
        + [jax.ShapeDtypeStruct((row_nodes, col_nodes), BF16)],
        in_specs=[smem, smem, smem, vmem, vmem, any_space],
        out_specs=[any_space] * (n_col + 1),
        scratch_shapes=[
            pltpu.VMEM((positions + 1, EDGE // QUARTERS, EDGE), F32) for _ in range(QUARTERS)
        ] + [
            pltpu.VMEM((panel_dev, 2 * node_dev, col_nodes), BF16),
            pltpu.VMEM((slots, EDGE, EDGE), BF16),
            pltpu.VMEM((col_nodes, width), BF16),
            pltpu.VMEM((panel_dev, node_dev, width), F32),
            pltpu.SemaphoreType.DMA((slots // chunk,)),
            pltpu.SemaphoreType.DMA((panel_dev,)),
            pltpu.SemaphoreType.DMA((panel_dev,)),
        ],
        compiler_params=params(FWD),
        cost_estimate=cost(100 * row_nodes * col_nodes * width, 1 << 20),
        name="densify_forward",
    )(block_rows, block_cols, live_slots, deg, features, blocks)
    keep, send = pieces[0::2], pieces[1::2]

    swap_pairs = [(i, i ^ 1) for i in range(n_col)]

    def swap(x):
        return lax.ppermute(x, "col", swap_pairs)

    def chip_flip(x, bit):
        return lax.ppermute(x, "col", [(i, i ^ (2 << bit)) for i in range(n_col)])

    def row_flip(x, bit):
        return lax.ppermute(x, "row", [(i, i ^ (1 << bit)) for i in range(n_row)])

    def low_bit(m):
        return (m & -m).bit_length() - 1

    terms = {m: [keep[m], swap(send[m])] for m in range(n_chip - 1, -1, -1)}
    for m in range(n_chip - 1, 0, -1):
        terms[m & (m - 1)].append(chip_flip(functools.reduce(jnp.add, terms[m]), low_bit(m)))
    parts = terms[0]

    half = width // 2
    out_act, pulled, wkeep, wsend = pl.pallas_call(
        functools.partial(middle_kernel, n_col, len(parts), float(nodes) ** (-0.5)),
        out_shape=(
            jax.ShapeDtypeStruct((node_dev, hidden), BF16),
            jax.ShapeDtypeStruct((width, node_dev), F32),
            jax.ShapeDtypeStruct((half, hidden), F32),
            jax.ShapeDtypeStruct((half, hidden), F32),
        ),
        in_specs=[vmem] * (3 + len(parts)),
        out_specs=(vmem,) * 4,
        compiler_params=params(16),
        name="middle",
    )(deg, cotangent, weight, *parts)

    own = {0: pulled}
    for m in (1, 2):
        own[m] = chip_flip(pulled, low_bit(m))
    other = {0: swap(pulled)}
    wsum = wkeep + swap(wsend)
    wsum = wsum + chip_flip(wsum, 0)
    own[2] = after(own[2], wsum)
    for m in range(3, n_chip):
        own[m] = chip_flip(own[m & (m - 1)], low_bit(m))
    for m in range(1, n_chip - 1):
        other[m] = swap(own[m])
    for t in range(1, chip_bits):
        wsum = wsum + chip_flip(wsum, t)

    early = [x for m in range(n_chip - 1) for x in (own[m], other[m])]
    sofar = pl.pallas_call(
        functools.partial(partial_kernel, len(early)),
        out_shape=jax.ShapeDtypeStruct((width, col_nodes), F32),
        in_specs=[any_space] * (1 + len(early)),
        out_specs=vmem,
        scratch_shapes=[
            pltpu.VMEM((len(early) * node_dev, col_nodes), BF16),
            pltpu.VMEM((len(early), width, node_dev), F32),
            pltpu.VMEM((2 * width, len(early) * node_dev), BF16),
            pltpu.SemaphoreType.DMA((len(early),)),
            pltpu.SemaphoreType.DMA((len(early),)),
        ],
        compiler_params=params((row_nodes * col_nodes * 2 >> 20) + 20),
        cost_estimate=cost(row_nodes * col_nodes * width * 4, 32 << 20),
        name="backward_early",
    )(tile, *early)

    own[n_chip - 1] = after(after(own[n_chip - 1], sofar), wsum)
    late = [own[n_chip - 1], swap(own[n_chip - 1])]
    n_piece = max(1, row_bits)
    while col_nodes % (EDGE * n_piece):
        n_piece -= 1
    size = col_nodes // n_piece
    extra = half * hidden // n_piece // EDGE
    done = pl.pallas_call(
        functools.partial(last_kernel, len(late), n_piece),
        out_shape=(jax.ShapeDtypeStruct((size + extra, width), F32),) * n_piece,
        in_specs=[vmem, any_space, any_space, vmem] + [any_space] * len(late),
        out_specs=(vmem,) * n_piece,
        scratch_shapes=[
            pltpu.VMEM((len(late) * node_dev, col_nodes), BF16),
            pltpu.VMEM((len(late), width, node_dev), F32),
            pltpu.VMEM((2 * width, len(late) * node_dev), BF16),
            pltpu.VMEM((width, col_nodes), F32),
            pltpu.SemaphoreType.DMA((len(late),)),
            pltpu.SemaphoreType.DMA,
            pltpu.SemaphoreType.DMA,
        ],
        compiler_params=params(24),
        name="backward_late",
    )(deg, tile, sofar, wsum, *late)

    for t in range(row_bits):
        done = [x + row_flip(x, (i + t) % row_bits) for i, x in enumerate(done)]
    feat_grad = jnp.concatenate([x[:size] for x in done], axis=0)
    wsum = jnp.concatenate(
        [x[size + i:size + i + half] for x in done for i in range(0, extra, half)], axis=1)

    wother = swap(wsum)
    low = lax.axis_index("col") % 2 == 0
    weight_grad = jnp.concatenate(
        [jnp.where(low, wsum, wother), jnp.where(low, wother, wsum)], axis=0
    )
    return out_act, feat_grad, weight_grad


def solution(mesh):
    n_row, n_col = mesh.shape["row"], mesh.shape["col"]
    return jax.shard_map(
        functools.partial(body, n_row, n_col),
        mesh=mesh,
        in_specs=(
            P("col", None),
            P(),
            P("row", "col", None),
            P("row", "col", None),
            P("row", "col"),
            P("row", "col", None, None, None),
            P(),
            P(("row", "col"), None),
        ),
        out_specs=(P(("row", "col"), None), P("col", None), P()),
        check_vma=False,
    )
```

```python
import functools

import jax
import jax.numpy as jnp
from jax import lax
from jax.experimental import pallas as pl
from jax.experimental.pallas import tpu as pltpu
from jax.sharding import PartitionSpec as P

F32 = jnp.float32
BF16 = jnp.bfloat16
EDGE = 128
GROUP = 16
QUARTERS = 4
AHEAD = 3
ACC_BYTES = 8 << 20
GELU_C = 0.7978845608028654
GELU_K = 0.044715


def inv_column(deg_ref, start):
    row = lax.rsqrt(deg_ref[pl.ds(start, 1), :].astype(F32))
    return jnp.transpose(jnp.broadcast_to(row, (EDGE, EDGE)))


def split(value):
    hi = value.astype(BF16)
    return hi, (value - hi.astype(F32)).astype(BF16)


def across(a, b):
    return lax.dot_general(a, b, (((0,), (0,)), ((), ())), preferred_element_type=F32)


def fetch(pairs, sems):
    copies = [pltpu.make_async_copy(src, dst, sems.at[i]) for i, (src, dst) in enumerate(pairs)]
    for copy in copies:
        copy.start()
    return copies


def halve(value, size):
    if size & (size - 1) == 0:
        shift = size.bit_length() - 1
        return lax.shift_right_logical(value, shift), value & (size - 1)
    return lax.div(value, size), lax.rem(value, size)


def forward_kernel(
    n_col, chunk, panel_dev, node_dev,
    rows_ref, cols_ref, live_ref, deg_ref, feat_ref, blocks_ref, *refs,
):
    outs, dense_ref = refs[:n_col], refs[n_col]
    accs, (both, buf, scaled, result, in_sems, dense_sems, out_sems) = refs[n_col + 1:-7], refs[-7:]
    part = EDGE // len(accs)
    slots = buf.shape[0]
    col_nodes, width = feat_ref.shape
    col_blocks = col_nodes // EDGE
    dev_blocks = node_dev // EDGE
    panel_blocks = panel_dev * dev_blocks
    positions = panel_blocks * col_blocks
    n_panels = n_col // panel_dev
    n_chunks = slots // chunk
    me = lax.axis_index("col")
    live = live_ref[0, 0]

    def block_copy(c):
        span = pl.ds(c * chunk, chunk)
        return pltpu.make_async_copy(blocks_ref.at[0, 0, span], buf.at[span], in_sems.at[c])

    def dense_copy(panel, j):
        there = pl.ds((panel * panel_dev + j) * node_dev, node_dev)
        return pltpu.make_async_copy(
            both.at[j, pl.ds(0, node_dev)], dense_ref.at[there], dense_sems.at[j])

    def result_copy(rel, j):
        return pltpu.make_async_copy(result.at[j], outs[rel], out_sems.at[j])

    for c in range(n_chunks):
        block_copy(c).start()

    for k in range(col_blocks):
        inv = inv_column(deg_ref, me * col_blocks + k)
        span = pl.ds(k * EDGE, EDGE)
        scaled[span, :] = (inv * feat_ref[span, :].astype(F32)).astype(BF16)

    def add_slots(first, place):
        pending = []

        def finish():
            acc, p, sofar, block = pending.pop(0)
            acc[p] = sofar + block.astype(F32)

        for s in range(GROUP):
            p = place(first + s)
            for q, acc in enumerate(accs):
                pending.append((acc, p, acc[p], buf[first + s, q * part:(q + 1) * part, :]))
                if len(pending) > AHEAD:
                    finish()
        while pending:
            finish()

    for panel in range(n_panels):
        base = panel * panel_blocks

        @pl.loop(0, positions)
        def _(p):
            for acc in accs:
                acc[p] = jnp.zeros((part, EDGE), F32)

        def place(s):
            dev, inner = halve(rows_ref[0, 0, s], dev_blocks)
            r = (dev ^ me) * dev_blocks + inner - base
            ok = s < live
            if n_panels > 1:
                ok = ok & (r >= 0) & (r < panel_blocks)
            return jnp.where(ok, r * col_blocks + cols_ref[0, 0, s], positions)

        @pl.loop(0, n_chunks)
        def _(c):
            if panel == 0:
                block_copy(c).wait()

            @pl.loop(0, chunk // GROUP)
            def _(g):
                add_slots(c * chunk + g * GROUP, place)

        for j in reversed(range(panel_dev)):
            rel = panel * panel_dev + j
            if panel:
                dense_copy(panel - 1, j).wait()
                result_copy(rel - panel_dev, j).wait()
            for b in range(dev_blocks):
                for cb in range(col_blocks):
                    lanes = slice(cb * EDGE, (cb + 1) * EDGE)
                    for q, acc in enumerate(accs):
                        hi, lo = split(acc[(j * dev_blocks + b) * col_blocks + cb])
                        at = b * EDGE + q * part
                        both[j, at:at + part, lanes] = hi
                        both[j, node_dev + at:node_dev + at + part, lanes] = lo
            dense_copy(panel, j).start()
            pair = jnp.dot(both[j], scaled[...], preferred_element_type=F32)
            result[j] = pair[:node_dev] + pair[node_dev:]
            result_copy(rel, j).start()

    for j in range(panel_dev):
        dense_copy(n_panels - 1, j).wait()
        result_copy((n_panels - 1) * panel_dev + j, j).wait()


def middle_kernel(n_col, n_in, scale, deg_ref, cot_ref, weight_ref, *refs):
    parts = refs[:n_in]
    act_ref, pulled_ref, message_ref = refs[n_in:]
    node_dev = cot_ref.shape[0]
    dev_blocks = node_dev // EDGE
    base = (lax.axis_index("row") * n_col + lax.axis_index("col")) * dev_blocks
    inv = jnp.concatenate([inv_column(deg_ref, base + k) for k in range(dev_blocks)], axis=0)
    summed = parts[0][...]
    for ref in parts[1:]:
        summed = summed + ref[...]
    propagated = inv * summed
    prop_hi, prop_lo = split(propagated)
    weight = weight_ref[...]
    pair = jnp.dot(
        jnp.concatenate([prop_hi, prop_lo], axis=0), weight, preferred_element_type=F32)
    v = pair[:node_dev] + pair[node_dev:]
    t = jnp.tanh(GELU_C * (v + GELU_K * v * v * v))
    act_ref[...] = (0.5 * v * (1.0 + t)).astype(BF16)
    slope = 0.5 * (1.0 + t) + 0.5 * v * (1.0 - t * t) * (GELU_C * (1.0 + 3.0 * GELU_K * v * v))
    gprime = cot_ref[...].astype(F32) * slope
    hi, lo = split(gprime)
    pair = lax.dot_general(
        jnp.concatenate([hi, lo], axis=0), weight, (((1,), (1,)), ((), ())),
        preferred_element_type=F32,
    )
    pulled = jnp.transpose(inv * (pair[:node_dev] + pair[node_dev:]))
    pulled_ref[...] = pulled
    message_ref[:EDGE] = pulled
    pair = across(jnp.concatenate([prop_hi, prop_lo], axis=1), hi)
    message_ref[EDGE:] = scale * (pair[:EDGE] + (pair[EDGE:] + across(prop_hi, lo)))


def load_lhs(stage, lhs, copies):
    width, node_dev = stage.shape[1:]
    for i in range(len(copies)):
        copies[i].wait()
        hi, lo = split(stage[i])
        lhs[:width, i * node_dev:(i + 1) * node_dev] = hi
        lhs[width:, i * node_dev:(i + 1) * node_dev] = lo


def partial_kernel(n_in, dense_ref, *refs):
    parts = refs[:n_in]
    out_ref, wsum_ref, dense, stage, wstage, lhs, sems, wsems, dense_sems = refs[n_in:]
    width, node_dev = stage.shape[1:]
    col_nodes = dense.shape[1]
    half = wstage.shape[1]
    mine = pl.ds(width + (lax.axis_index("col") % 2) * half, half)
    blocks = fetch(
        [(dense_ref.at[pl.ds(i * node_dev, node_dev)], dense.at[pl.ds(i * node_dev, node_dev)])
         for i in range(n_in)], dense_sems)
    copies = fetch([(r.at[pl.ds(0, width)], stage.at[i]) for i, r in enumerate(parts)], sems)
    weights = fetch([(parts[i].at[mine], wstage.at[i]) for i in range(4)], wsems)
    load_lhs(stage, lhs, copies)
    for copy in weights:
        copy.wait()
    total = (wstage[0] + wstage[1]) + (wstage[2] + wstage[3])
    for n in range(0, total.shape[1], EDGE):
        wsum_ref[n // EDGE * half:(n // EDGE + 1) * half, :] = total[:, n:n + EDGE]
    for copy in blocks:
        copy.wait()
    step = 2 * EDGE if col_nodes % (2 * EDGE) == 0 else EDGE
    for n in range(0, col_nodes, step):
        pair = jnp.dot(lhs[...], dense[:, n:n + step], preferred_element_type=F32)
        out_ref[:, n:n + step] = pair[:width] + pair[width:]


def last_kernel(n_in, n_out, deg_ref, dense_ref, sofar_ref, *refs):
    parts, outs = refs[:n_in], refs[n_in:n_in + n_out]
    dense, stage, lhs, sofar, sems, dense_sem, sofar_sem = refs[n_in + n_out:]
    width, node_dev = parts[0].shape
    col_nodes = dense.shape[1]
    rows = n_in * node_dev
    block = pltpu.make_async_copy(
        dense_ref.at[pl.ds(dense_ref.shape[0] - rows, rows)], dense, dense_sem)
    before = pltpu.make_async_copy(sofar_ref, sofar, sofar_sem)
    block.start()
    size = col_nodes // n_out
    copies = fetch([(r, stage.at[i]) for i, r in enumerate(parts)], sems)
    before.start()
    load_lhs(stage, lhs, copies)
    block.wait()
    before.wait()
    step = 2 * EDGE if col_nodes % (2 * EDGE) == 0 else EDGE
    first = lax.axis_index("col") * (col_nodes // EDGE)
    for n in range(0, col_nodes, step):
        pair = jnp.dot(lhs[...], dense[:, n:n + step], preferred_element_type=F32)
        total = sofar[:, n:n + step] + (pair[:width] + pair[width:])
        for at in range(n, n + step, EDGE):
            inv = inv_column(deg_ref, first + at // EDGE)
            out = outs[at // size]
            out[at % size:at % size + EDGE, :] = inv * jnp.transpose(total[:, at - n:at - n + EDGE])


def body(n_row, n_col, features, degrees, block_rows, block_cols, live_slots, blocks, weight, cotangent):
    n_chip = n_col // 2
    chip_bits, row_bits = n_chip.bit_length() - 1, n_row.bit_length() - 1
    assert n_col == 2 << chip_bits and n_row == 1 << row_bits
    node_dev, hidden = cotangent.shape
    col_nodes, width = features.shape
    row_nodes = node_dev * n_col
    nodes = col_nodes * n_col
    slots = blocks.shape[2]
    deg = degrees.reshape(nodes // EDGE, EDGE)
    col_blocks = col_nodes // EDGE
    dev_blocks = node_dev // EDGE
    assert n_chip >= 4
    chunk = 16
    panel_dev = n_col
    while panel_dev % 2 == 0 and panel_dev * node_dev * col_nodes * 4 > ACC_BYTES:
        panel_dev //= 2
    positions = panel_dev * dev_blocks * col_blocks
    smem = pl.BlockSpec(memory_space=pltpu.SMEM)
    any_space = pl.BlockSpec(memory_space=pl.ANY)
    vmem = pl.BlockSpec(memory_space=pltpu.VMEM)

    def params(mib):
        return pltpu.CompilerParams(vmem_limit_bytes=mib << 20)

    def after(x, other):
        corner = 0.0 * other[:8, :EDGE]
        if x.shape == other.shape[:1] + x.shape[1:]:
            return x + 0.0 * other[:, :x.shape[1]]
        return (x.reshape(-1, 8, EDGE) + corner).reshape(x.shape)

    def cost(flops, read):
        return pl.CostEstimate(flops=flops, bytes_accessed=read, transcendentals=0)

    *pieces, tile = pl.pallas_call(
        functools.partial(forward_kernel, n_col, chunk, panel_dev, node_dev),
        out_shape=[jax.ShapeDtypeStruct((node_dev, width), F32)] * n_col
        + [jax.ShapeDtypeStruct((row_nodes, col_nodes), BF16)],
        in_specs=[smem, smem, smem, vmem, vmem, any_space],
        out_specs=[any_space] * (n_col + 1),
        scratch_shapes=[
            pltpu.VMEM((positions + 1, EDGE // QUARTERS, EDGE), F32) for _ in range(QUARTERS)
        ] + [
            pltpu.VMEM((panel_dev, 2 * node_dev, col_nodes), BF16),
            pltpu.VMEM((slots, EDGE, EDGE), BF16),
            pltpu.VMEM((col_nodes, width), BF16),
            pltpu.VMEM((panel_dev, node_dev, width), F32),
            pltpu.SemaphoreType.DMA((slots // chunk,)),
            pltpu.SemaphoreType.DMA((panel_dev,)),
            pltpu.SemaphoreType.DMA((panel_dev,)),
        ],
        compiler_params=params(54),
        name="densify_forward",
    )(block_rows, block_cols, live_slots, deg, features, blocks)
    keep, send = pieces[0::2], pieces[1::2]

    swap_pairs = [(i, i ^ 1) for i in range(n_col)]

    def swap(x):
        return lax.ppermute(x, "col", swap_pairs)

    def chip_flip(x, bit):
        return lax.ppermute(x, "col", [(i, i ^ (2 << bit)) for i in range(n_col)])

    def row_flip(x, bit):
        return lax.ppermute(x, "row", [(i, i ^ (1 << bit)) for i in range(n_row)])

    def low_bit(m):
        return (m & -m).bit_length() - 1

    terms = {m: [keep[m], swap(send[m])] for m in range(n_chip - 1, -1, -1)}
    for m in range(n_chip - 1, 0, -1):
        terms[m & (m - 1)].append(chip_flip(functools.reduce(jnp.add, terms[m]), low_bit(m)))
    parts = terms[0]

    out_act, pulled, message = pl.pallas_call(
        functools.partial(middle_kernel, n_col, len(parts), float(nodes) ** (-0.5)),
        out_shape=(
            jax.ShapeDtypeStruct((node_dev, hidden), BF16),
            jax.ShapeDtypeStruct((width, node_dev), F32),
            jax.ShapeDtypeStruct((2 * width, hidden), F32),
        ),
        in_specs=[vmem] * (3 + len(parts)),
        out_specs=(vmem,) * 3,
        compiler_params=params(16),
        name="middle",
    )(deg, cotangent, weight, *parts)

    last = n_chip - 1
    own = {0: message, 1: chip_flip(message, 0), 2: chip_flip(pulled, 1)}
    for m in range(3, n_chip):
        own[m] = chip_flip(own[m & (m - 1)][:width], low_bit(m))
    other = {m: swap(own[m]) for m in range(last)}

    half = width // 2
    early = [x for m in range(last) for x in (own[m], other[m])]
    sofar, wsum = pl.pallas_call(
        functools.partial(partial_kernel, len(early)),
        out_shape=(
            jax.ShapeDtypeStruct((width, col_nodes), F32),
            jax.ShapeDtypeStruct((half * hidden // EDGE, EDGE), F32),
        ),
        in_specs=[any_space] * (1 + len(early)),
        out_specs=(vmem,) * 2,
        scratch_shapes=[
            pltpu.VMEM((len(early) * node_dev, col_nodes), BF16),
            pltpu.VMEM((len(early), width, node_dev), F32),
            pltpu.VMEM((4, half, hidden), F32),
            pltpu.VMEM((2 * width, len(early) * node_dev), BF16),
            pltpu.SemaphoreType.DMA((len(early),)),
            pltpu.SemaphoreType.DMA((4,)),
            pltpu.SemaphoreType.DMA((len(early),)),
        ],
        compiler_params=params(52),
        cost_estimate=cost(row_nodes * col_nodes * width * 4, 32 << 20),
        name="backward_early",
    )(tile, *early)

    own[last] = after(own[last], sofar)
    late = [own[last], swap(own[last])]
    for t in range(1, chip_bits):
        wsum = wsum + chip_flip(wsum, t)
    n_piece = max(1, row_bits)
    while col_nodes % (EDGE * n_piece):
        n_piece -= 1
    size = col_nodes // n_piece
    done = pl.pallas_call(
        functools.partial(last_kernel, len(late), n_piece),
        out_shape=(jax.ShapeDtypeStruct((size, width), F32),) * n_piece,
        in_specs=[vmem, any_space, any_space] + [any_space] * len(late),
        out_specs=(vmem,) * n_piece,
        scratch_shapes=[
            pltpu.VMEM((len(late) * node_dev, col_nodes), BF16),
            pltpu.VMEM((len(late), width, node_dev), F32),
            pltpu.VMEM((2 * width, len(late) * node_dev), BF16),
            pltpu.VMEM((width, col_nodes), F32),
            pltpu.SemaphoreType.DMA((len(late),)),
            pltpu.SemaphoreType.DMA,
            pltpu.SemaphoreType.DMA,
        ],
        compiler_params=params(52),
        name="backward_late",
    )(deg, tile, sofar, *late)

    done = list(done)
    for t in range(row_bits):
        wsum = after(wsum, done[0])
        wsum = wsum + row_flip(wsum, t)
        done = [x + row_flip(x, (i + t) % row_bits) for i, x in enumerate(done)]
        if t == 0:
            done[-1] = after(done[-1], wsum)
    wsum = after(wsum, done[0])
    feat_grad = jnp.concatenate(done, axis=0)

    wother = swap(wsum)
    low = lax.axis_index("col") % 2 == 0
    halves = (jnp.where(low, wsum, wother), jnp.where(low, wother, wsum))
    weight_grad = jnp.concatenate(
        [jnp.concatenate([x[i:i + half] for i in range(0, x.shape[0], half)], axis=1) for x in halves],
        axis=0,
    )
    return out_act, feat_grad, weight_grad


def solution(mesh):
    n_row, n_col = mesh.shape["row"], mesh.shape["col"]
    return jax.shard_map(
        functools.partial(body, n_row, n_col),
        mesh=mesh,
        in_specs=(
            P("col", None),
            P(),
            P("row", "col", None),
            P("row", "col", None),
            P("row", "col"),
            P("row", "col", None, None, None),
            P(),
            P(("row", "col"), None),
        ),
        out_specs=(P(("row", "col"), None), P("col", None), P()),
        check_vma=False,
    )
```

```python
import functools

import jax
import jax.numpy as jnp
from jax import lax
from jax.experimental import pallas as pl
from jax.experimental.pallas import tpu as pltpu
from jax.sharding import PartitionSpec as P

F32 = jnp.float32
BF16 = jnp.bfloat16
EDGE = 128
GROUP = 16
QUARTERS = 4
AHEAD = 3
ACC_BYTES = 8 << 20
GELU_C = 0.7978845608028654
GELU_K = 0.044715


def inv_column(deg_ref, start):
    row = lax.rsqrt(deg_ref[pl.ds(start, 1), :].astype(F32))
    return jnp.transpose(jnp.broadcast_to(row, (EDGE, EDGE)))


def split(value):
    hi = value.astype(BF16)
    return hi, (value - hi.astype(F32)).astype(BF16)


def across(a, b):
    return lax.dot_general(a, b, (((0,), (0,)), ((), ())), preferred_element_type=F32)


def fetch(pairs, sems):
    copies = [pltpu.make_async_copy(src, dst, sems.at[i]) for i, (src, dst) in enumerate(pairs)]
    for copy in copies:
        copy.start()
    return copies


def halve(value, size):
    if size & (size - 1) == 0:
        shift = size.bit_length() - 1
        return lax.shift_right_logical(value, shift), value & (size - 1)
    return lax.div(value, size), lax.rem(value, size)


def forward_kernel(
    n_col, chunk, panel_dev, node_dev,
    rows_ref, cols_ref, live_ref, deg_ref, feat_ref, blocks_ref, *refs,
):
    outs, tile_ref = refs[:n_col], refs[n_col]
    accs, (both, buf, scaled, result, in_sems, dense_sems, out_sems) = refs[n_col + 1:-7], refs[-7:]
    part = EDGE // len(accs)
    slots = buf.shape[0]
    col_nodes, width = feat_ref.shape
    col_blocks = col_nodes // EDGE
    dev_blocks = node_dev // EDGE
    panel_blocks = panel_dev * dev_blocks
    positions = panel_blocks * col_blocks
    n_panels = n_col // panel_dev
    n_chunks = slots // chunk
    me = lax.axis_index("col")
    live = live_ref[0, 0]

    def block_copy(c):
        span = pl.ds(c * chunk, chunk)
        return pltpu.make_async_copy(blocks_ref.at[0, 0, span], buf.at[span], in_sems.at[c])

    def dense_copy(rel, j):
        there = tile_ref.at[pl.ds(rel * node_dev, node_dev)]
        return pltpu.make_async_copy(both.at[j, pl.ds(0, node_dev)], there, dense_sems.at[j])

    def result_copy(rel, j):
        return pltpu.make_async_copy(result.at[j], outs[rel], out_sems.at[j])

    for c in range(n_chunks):
        block_copy(c).start()

    for k in range(col_blocks):
        inv = inv_column(deg_ref, me * col_blocks + k)
        span = pl.ds(k * EDGE, EDGE)
        scaled[span, :] = (inv * feat_ref[span, :].astype(F32)).astype(BF16)

    def add_slots(first, place):
        pending = []

        def finish():
            acc, p, sofar, block = pending.pop(0)
            acc[p] = sofar + block.astype(F32)

        for s in range(GROUP):
            p = place(first + s)
            for q, acc in enumerate(accs):
                pending.append((acc, p, acc[p], buf[first + s, q * part:(q + 1) * part, :]))
                if len(pending) > AHEAD:
                    finish()
        while pending:
            finish()

    for panel in range(n_panels):
        base = panel * panel_blocks

        @pl.loop(0, positions)
        def _(p):
            for acc in accs:
                acc[p] = jnp.zeros((part, EDGE), F32)

        def place(s):
            dev, inner = halve(rows_ref[0, 0, s], dev_blocks)
            r = (dev ^ me) * dev_blocks + inner - base
            ok = s < live
            if n_panels > 1:
                ok = ok & (r >= 0) & (r < panel_blocks)
            return jnp.where(ok, r * col_blocks + cols_ref[0, 0, s], positions)

        @pl.loop(0, n_chunks)
        def _(c):
            if panel == 0:
                block_copy(c).wait()

            @pl.loop(0, chunk // GROUP)
            def _(g):
                add_slots(c * chunk + g * GROUP, place)

        for j in reversed(range(panel_dev)):
            rel = panel * panel_dev + j
            if panel:
                dense_copy(rel - panel_dev, j).wait()
                result_copy(rel - panel_dev, j).wait()
            for b in range(dev_blocks):
                for cb in range(col_blocks):
                    lanes = slice(cb * EDGE, (cb + 1) * EDGE)
                    for q, acc in enumerate(accs):
                        hi, lo = split(acc[(j * dev_blocks + b) * col_blocks + cb])
                        at = b * EDGE + q * part
                        both[j, at:at + part, lanes] = hi
                        both[j, node_dev + at:node_dev + at + part, lanes] = lo
            dense_copy(rel, j).start()
            pair = jnp.dot(both[j], scaled[...], preferred_element_type=F32)
            result[j] = pair[:node_dev] + pair[node_dev:]
            result_copy(rel, j).start()

    for j in range(panel_dev):
        rel = (n_panels - 1) * panel_dev + j
        dense_copy(rel, j).wait()
        result_copy(rel, j).wait()


def middle_kernel(n_col, n_in, scale, deg_ref, cot_ref, weight_ref, *refs):
    parts = refs[:n_in]
    act_ref, pulled_ref, message_ref = refs[n_in:]
    node_dev = cot_ref.shape[0]
    dev_blocks = node_dev // EDGE
    base = (lax.axis_index("row") * n_col + lax.axis_index("col")) * dev_blocks
    inv = jnp.concatenate([inv_column(deg_ref, base + k) for k in range(dev_blocks)], axis=0)
    summed = parts[0][...]
    for ref in parts[1:]:
        summed = summed + ref[...]
    propagated = inv * summed
    prop_hi, prop_lo = split(propagated)
    weight = weight_ref[...]
    pair = jnp.dot(
        jnp.concatenate([prop_hi, prop_lo], axis=0), weight, preferred_element_type=F32)
    v = pair[:node_dev] + pair[node_dev:]
    t = jnp.tanh(GELU_C * (v + GELU_K * v * v * v))
    act_ref[...] = (0.5 * v * (1.0 + t)).astype(BF16)
    slope = 0.5 * (1.0 + t) + 0.5 * v * (1.0 - t * t) * (GELU_C * (1.0 + 3.0 * GELU_K * v * v))
    gprime = cot_ref[...].astype(F32) * slope
    hi, lo = split(gprime)
    pair = lax.dot_general(
        jnp.concatenate([hi, lo], axis=0), weight, (((1,), (1,)), ((), ())),
        preferred_element_type=F32,
    )
    pulled = jnp.transpose(inv * (pair[:node_dev] + pair[node_dev:]))
    pulled_ref[...] = pulled
    message_ref[:EDGE] = pulled
    pair = across(jnp.concatenate([prop_hi, prop_lo], axis=1), hi)
    message_ref[EDGE:] = scale * (pair[:EDGE] + (pair[EDGE:] + across(prop_hi, lo)))


def load_lhs(stage, lhs, copies):
    width, node_dev = stage.shape[1:]
    for i in range(len(copies)):
        copies[i].wait()
        hi, lo = split(stage[i])
        lhs[:width, i * node_dev:(i + 1) * node_dev] = hi
        lhs[width:, i * node_dev:(i + 1) * node_dev] = lo


def partial_kernel(n_in, tile_ref, *refs):
    parts = refs[:n_in]
    out_ref, wsum_ref, dense, stage, wstage, lhs, sems, wsems, dense_sems = refs[n_in:]
    width, node_dev = stage.shape[1:]
    col_nodes = dense.shape[1]
    half = wstage.shape[1]
    mine = pl.ds(width + (lax.axis_index("col") % 2) * half, half)
    blocks = fetch(
        [(tile_ref.at[span], dense.at[span]) for span in (
            pl.ds(i * node_dev, node_dev) for i in range(n_in))], dense_sems)
    copies = fetch([(r.at[pl.ds(0, width)], stage.at[i]) for i, r in enumerate(parts)], sems)
    weights = fetch([(parts[i].at[mine], wstage.at[i]) for i in range(2)], wsems)
    load_lhs(stage, lhs, copies)
    for copy in weights:
        copy.wait()
    total = wstage[0] + wstage[1]
    for n in range(0, total.shape[1], EDGE):
        wsum_ref[n // EDGE * half:(n // EDGE + 1) * half, :] = total[:, n:n + EDGE]
    for copy in blocks:
        copy.wait()
    step = 2 * EDGE if col_nodes % (2 * EDGE) == 0 else EDGE
    for n in range(0, col_nodes, step):
        pair = jnp.dot(lhs[...], dense[:, n:n + step], preferred_element_type=F32)
        out_ref[:, n:n + step] = pair[:width] + pair[width:]


def last_kernel(n_in, n_out, deg_ref, dense_ref, sofar_ref, *refs):
    parts, outs = refs[:n_in], refs[n_in:n_in + n_out]
    dense, stage, lhs, sofar, sems, dense_sem, sofar_sem = refs[n_in + n_out:]
    width, node_dev = parts[0].shape
    col_nodes = dense.shape[1]
    rows = n_in * node_dev
    block = pltpu.make_async_copy(
        dense_ref.at[pl.ds(dense_ref.shape[0] - rows, rows)], dense, dense_sem)
    before = pltpu.make_async_copy(sofar_ref, sofar, sofar_sem)
    block.start()
    size = col_nodes // n_out
    copies = fetch([(r, stage.at[i]) for i, r in enumerate(parts)], sems)
    before.start()
    load_lhs(stage, lhs, copies)
    block.wait()
    before.wait()
    step = 2 * EDGE if col_nodes % (2 * EDGE) == 0 else EDGE
    first = lax.axis_index("col") * (col_nodes // EDGE)
    for n in range(0, col_nodes, step):
        pair = jnp.dot(lhs[...], dense[:, n:n + step], preferred_element_type=F32)
        total = sofar[:, n:n + step] + (pair[:width] + pair[width:])
        for at in range(n, n + step, EDGE):
            inv = inv_column(deg_ref, first + at // EDGE)
            out = outs[at // size]
            out[at % size:at % size + EDGE, :] = inv * jnp.transpose(total[:, at - n:at - n + EDGE])


def body(n_row, n_col, features, degrees, block_rows, block_cols, live_slots, blocks, weight, cotangent):
    n_chip = n_col // 2
    chip_bits, row_bits = n_chip.bit_length() - 1, n_row.bit_length() - 1
    assert n_col == 2 << chip_bits and n_row == 1 << row_bits
    node_dev, hidden = cotangent.shape
    col_nodes, width = features.shape
    row_nodes = node_dev * n_col
    nodes = col_nodes * n_col
    slots = blocks.shape[2]
    deg = degrees.reshape(nodes // EDGE, EDGE)
    col_blocks = col_nodes // EDGE
    dev_blocks = node_dev // EDGE
    assert n_chip >= 4
    chunk = 16
    panel_dev = n_col
    while panel_dev % 2 == 0 and panel_dev * node_dev * col_nodes * 4 > ACC_BYTES:
        panel_dev //= 2
    positions = panel_dev * dev_blocks * col_blocks
    smem = pl.BlockSpec(memory_space=pltpu.SMEM)
    any_space = pl.BlockSpec(memory_space=pl.ANY)
    vmem = pl.BlockSpec(memory_space=pltpu.VMEM)

    def params(mib):
        return pltpu.CompilerParams(vmem_limit_bytes=mib << 20)

    def after(x, other):
        corner = 0.0 * other[:8, :EDGE]
        if x.shape[0] == other.shape[0] and x.shape[1] <= other.shape[1]:
            return x + 0.0 * other[:, :x.shape[1]]
        return (x.reshape(-1, 8, EDGE) + corner).reshape(x.shape)

    def cost(flops, read):
        return pl.CostEstimate(flops=flops, bytes_accessed=read, transcendentals=0)

    *pieces, tile = pl.pallas_call(
        functools.partial(forward_kernel, n_col, chunk, panel_dev, node_dev),
        out_shape=[jax.ShapeDtypeStruct((node_dev, width), F32)] * n_col
        + [jax.ShapeDtypeStruct((row_nodes, col_nodes), BF16)],
        in_specs=[smem, smem, smem, vmem, vmem, any_space],
        out_specs=[any_space] * (n_col + 1),
        scratch_shapes=[
            pltpu.VMEM((positions + 1, EDGE // QUARTERS, EDGE), F32) for _ in range(QUARTERS)
        ] + [
            pltpu.VMEM((panel_dev, 2 * node_dev, col_nodes), BF16),
            pltpu.VMEM((slots, EDGE, EDGE), BF16),
            pltpu.VMEM((col_nodes, width), BF16),
            pltpu.VMEM((panel_dev, node_dev, width), F32),
            pltpu.SemaphoreType.DMA((slots // chunk,)),
            pltpu.SemaphoreType.DMA((panel_dev,)),
            pltpu.SemaphoreType.DMA((panel_dev,)),
        ],
        compiler_params=params(54),
        name="densify_forward",
    )(block_rows, block_cols, live_slots, deg, features, blocks)
    keep, send = pieces[0::2], pieces[1::2]

    swap_pairs = [(i, i ^ 1) for i in range(n_col)]

    def swap(x):
        return lax.ppermute(x, "col", swap_pairs)

    def chip_flip(x, bit):
        return lax.ppermute(x, "col", [(i, i ^ (2 << bit)) for i in range(n_col)])

    def row_flip(x, bit):
        return lax.ppermute(x, "row", [(i, i ^ (1 << bit)) for i in range(n_row)])

    def low_bit(m):
        return (m & -m).bit_length() - 1

    last = n_chip - 1
    kept = {m: [keep[m], swap(send[m])] for m in range(last, -1, -1)}
    parts = [functools.reduce(jnp.add, kept[0])]
    kept[0] = []
    for m in range(last, 0, -1):
        unit = functools.reduce(jnp.add, kept[m])
        if m == 2:
            unit = after(unit, parts[0])
        kept[m & (m - 1)].append(chip_flip(unit, low_bit(m)))
    parts += kept[0]

    out_act, pulled, message = pl.pallas_call(
        functools.partial(middle_kernel, n_col, len(parts), float(nodes) ** (-0.5)),
        out_shape=(
            jax.ShapeDtypeStruct((node_dev, hidden), BF16),
            jax.ShapeDtypeStruct((width, node_dev), F32),
            jax.ShapeDtypeStruct((2 * width, hidden), F32),
        ),
        in_specs=[vmem] * (3 + len(parts)),
        out_specs=(vmem,) * 3,
        compiler_params=params(16),
        name="middle",
    )(deg, cotangent, weight, *parts)

    own = {0: pulled}
    for m in range(1, n_chip):
        own[m] = chip_flip(own[m & (m - 1)], low_bit(m))
    own[0], own[1] = message, after(own[1], own[2])
    other = {m: swap(own[m]) for m in range(last)}

    half = width // 2
    early = [x for m in range(last) for x in (own[m], other[m])]
    sofar, wsum = pl.pallas_call(
        functools.partial(partial_kernel, len(early)),
        out_shape=(
            jax.ShapeDtypeStruct((width, col_nodes), F32),
            jax.ShapeDtypeStruct((half * hidden // EDGE, EDGE), F32),
        ),
        in_specs=[any_space] * (1 + len(early)),
        out_specs=(vmem,) * 2,
        scratch_shapes=[
            pltpu.VMEM((len(early) * node_dev, col_nodes), BF16),
            pltpu.VMEM((len(early), width, node_dev), F32),
            pltpu.VMEM((2, half, hidden), F32),
            pltpu.VMEM((2 * width, len(early) * node_dev), BF16),
            pltpu.SemaphoreType.DMA((len(early),)),
            pltpu.SemaphoreType.DMA((2,)),
            pltpu.SemaphoreType.DMA((len(early),)),
        ],
        compiler_params=params(52),
        cost_estimate=cost(row_nodes * col_nodes * width * 4, 32 << 20),
        name="backward_early",
    )(tile, *early)

    own[last] = after(own[last], sofar)
    late = [own[last], swap(own[last])]
    wsum = wsum + chip_flip(wsum, 0)
    n_piece = max(1, row_bits)
    while col_nodes % (EDGE * n_piece):
        n_piece -= 1
    size = col_nodes // n_piece
    done = pl.pallas_call(
        functools.partial(last_kernel, len(late), n_piece),
        out_shape=(jax.ShapeDtypeStruct((size, width), F32),) * n_piece,
        in_specs=[vmem, any_space, any_space] + [any_space] * len(late),
        out_specs=(vmem,) * n_piece,
        scratch_shapes=[
            pltpu.VMEM((len(late) * node_dev, col_nodes), BF16),
            pltpu.VMEM((len(late), width, node_dev), F32),
            pltpu.VMEM((2 * width, len(late) * node_dev), BF16),
            pltpu.VMEM((width, col_nodes), F32),
            pltpu.SemaphoreType.DMA((len(late),)),
            pltpu.SemaphoreType.DMA,
            pltpu.SemaphoreType.DMA,
        ],
        compiler_params=params(52),
        name="backward_late",
    )(deg, tile, sofar, *late)

    done = list(done)
    for t in range(row_bits):
        wsum = after(wsum, done[0])
        if t == 0:
            for bit in range(1, chip_bits):
                wsum = wsum + chip_flip(wsum, bit)
        wsum = wsum + row_flip(wsum, t)
        done = [x + row_flip(x, (i + t) % row_bits) for i, x in enumerate(done)]
        if t == 0:
            done[-1] = after(done[-1], wsum)
    wsum = after(wsum, done[0])
    feat_grad = jnp.concatenate(done, axis=0)

    wother = swap(wsum)
    low = lax.axis_index("col") % 2 == 0
    halves = (jnp.where(low, wsum, wother), jnp.where(low, wother, wsum))
    weight_grad = jnp.concatenate(
        [jnp.concatenate([x[i:i + half] for i in range(0, x.shape[0], half)], axis=1) for x in halves],
        axis=0,
    )
    return out_act, feat_grad, weight_grad


def solution(mesh):
    n_row, n_col = mesh.shape["row"], mesh.shape["col"]
    return jax.shard_map(
        functools.partial(body, n_row, n_col),
        mesh=mesh,
        in_specs=(
            P("col", None),
            P(),
            P("row", "col", None),
            P("row", "col", None),
            P("row", "col"),
            P("row", "col", None, None, None),
            P(),
            P(("row", "col"), None),
        ),
        out_specs=(P(("row", "col"), None), P("col", None), P()),
        check_vma=False,
    )
```

```python
import functools

import jax
import jax.numpy as jnp
from jax import lax
from jax.experimental import pallas as pl
from jax.experimental.pallas import tpu as pltpu
from jax.sharding import PartitionSpec as P

F32 = jnp.float32
BF16 = jnp.bfloat16
EDGE = 128
GROUP = 16
QUARTERS = 4
AHEAD = 3
BWD = 50
ACC_BYTES = 8 << 20
GELU_C = 0.7978845608028654
GELU_K = 0.044715


def inv_column(deg_ref, start):
    row = lax.rsqrt(deg_ref[pl.ds(start, 1), :].astype(F32))
    return jnp.transpose(jnp.broadcast_to(row, (EDGE, EDGE)))


def split(value):
    hi = value.astype(BF16)
    return hi, (value - hi.astype(F32)).astype(BF16)


def across(a, b):
    return lax.dot_general(a, b, (((0,), (0,)), ((), ())), preferred_element_type=F32)


def fetch(pairs, sems):
    copies = [pltpu.make_async_copy(src, dst, sems.at[i]) for i, (src, dst) in enumerate(pairs)]
    for copy in copies:
        copy.start()
    return copies


def halve(value, size):
    if size & (size - 1) == 0:
        shift = size.bit_length() - 1
        return lax.shift_right_logical(value, shift), value & (size - 1)
    return lax.div(value, size), lax.rem(value, size)


def forward_kernel(
    n_col, chunk, panel_dev, node_dev,
    rows_ref, cols_ref, live_ref, deg_ref, feat_ref, blocks_ref, *refs,
):
    outs, tile_ref = refs[:n_col], refs[n_col]
    accs, (both, buf, scaled, result, in_sems, dense_sems, out_sems) = refs[n_col + 1:-7], refs[-7:]
    part = EDGE // len(accs)
    slots = buf.shape[0]
    col_nodes, width = feat_ref.shape
    col_blocks = col_nodes // EDGE
    dev_blocks = node_dev // EDGE
    panel_blocks = panel_dev * dev_blocks
    positions = panel_blocks * col_blocks
    n_panels = n_col // panel_dev
    n_chunks = slots // chunk
    me = lax.axis_index("col")
    live = live_ref[0, 0]

    def block_copy(c):
        span = pl.ds(c * chunk, chunk)
        return pltpu.make_async_copy(blocks_ref.at[0, 0, span], buf.at[span], in_sems.at[c])

    def dense_copy(rel, j):
        there = tile_ref.at[pl.ds(rel * node_dev, node_dev)]
        return pltpu.make_async_copy(both.at[j, pl.ds(0, node_dev)], there, dense_sems.at[j])

    def result_copy(rel, j):
        return pltpu.make_async_copy(result.at[j], outs[rel], out_sems.at[j])

    for c in range(n_chunks):
        block_copy(c).start()

    for k in range(col_blocks):
        inv = inv_column(deg_ref, me * col_blocks + k)
        span = pl.ds(k * EDGE, EDGE)
        scaled[span, :] = (inv * feat_ref[span, :].astype(F32)).astype(BF16)

    def add_slots(first, place):
        pending = []

        def finish():
            acc, p, sofar, block = pending.pop(0)
            acc[p] = sofar + block.astype(F32)

        for s in range(GROUP):
            p = place(first + s)
            for q, acc in enumerate(accs):
                pending.append((acc, p, acc[p], buf[first + s, q * part:(q + 1) * part, :]))
                if len(pending) > AHEAD:
                    finish()
        while pending:
            finish()

    for panel in range(n_panels):
        base = panel * panel_blocks

        @pl.loop(0, positions)
        def _(p):
            for acc in accs:
                acc[p] = jnp.zeros((part, EDGE), F32)

        def place(s):
            dev, inner = halve(rows_ref[0, 0, s], dev_blocks)
            r = (dev ^ me) * dev_blocks + inner - base
            ok = s < live
            if n_panels > 1:
                ok = ok & (r >= 0) & (r < panel_blocks)
            return jnp.where(ok, r * col_blocks + cols_ref[0, 0, s], positions)

        @pl.loop(0, n_chunks)
        def _(c):
            if panel == 0:
                block_copy(c).wait()

            @pl.loop(0, chunk // GROUP)
            def _(g):
                add_slots(c * chunk + g * GROUP, place)

        for j in reversed(range(panel_dev)):
            rel = panel * panel_dev + j
            if panel:
                dense_copy(rel - panel_dev, j).wait()
                result_copy(rel - panel_dev, j).wait()
            for b in range(dev_blocks):
                for cb in range(col_blocks):
                    lanes = slice(cb * EDGE, (cb + 1) * EDGE)
                    for q, acc in enumerate(accs):
                        hi, lo = split(acc[(j * dev_blocks + b) * col_blocks + cb])
                        at = b * EDGE + q * part
                        both[j, at:at + part, lanes] = hi
                        both[j, node_dev + at:node_dev + at + part, lanes] = lo
            dense_copy(rel, j).start()
            pair = jnp.dot(both[j], scaled[...], preferred_element_type=F32)
            result[j] = pair[:node_dev] + pair[node_dev:]
            result_copy(rel, j).start()

    for j in range(panel_dev):
        rel = (n_panels - 1) * panel_dev + j
        dense_copy(rel, j).wait()
        result_copy(rel, j).wait()


def middle_kernel(n_col, n_in, scale, deg_ref, cot_ref, weight_ref, *refs):
    parts = refs[:n_in]
    act_ref, pulled_ref, keep_ref, send_ref = refs[n_in:]
    node_dev = cot_ref.shape[0]
    dev_blocks = node_dev // EDGE
    base = (lax.axis_index("row") * n_col + lax.axis_index("col")) * dev_blocks
    inv = jnp.concatenate([inv_column(deg_ref, base + k) for k in range(dev_blocks)], axis=0)
    summed = parts[0][...]
    for ref in parts[1:]:
        summed = summed + ref[...]
    propagated = inv * summed
    prop_hi, prop_lo = split(propagated)
    weight = weight_ref[...]
    pair = jnp.dot(
        jnp.concatenate([prop_hi, prop_lo], axis=0), weight, preferred_element_type=F32)
    v = pair[:node_dev] + pair[node_dev:]
    t = jnp.tanh(GELU_C * (v + GELU_K * v * v * v))
    act_ref[...] = (0.5 * v * (1.0 + t)).astype(BF16)
    slope = 0.5 * (1.0 + t) + 0.5 * v * (1.0 - t * t) * (GELU_C * (1.0 + 3.0 * GELU_K * v * v))
    gprime = cot_ref[...].astype(F32) * slope
    hi, lo = split(gprime)
    pair = lax.dot_general(
        jnp.concatenate([hi, lo], axis=0), weight, (((1,), (1,)), ((), ())),
        preferred_element_type=F32,
    )
    pulled_ref[...] = jnp.transpose(inv * (pair[:node_dev] + pair[node_dev:]))
    pair = across(jnp.concatenate([prop_hi, prop_lo], axis=1), hi)
    part = scale * (pair[:EDGE] + (pair[EDGE:] + across(prop_hi, lo)))
    half = EDGE // 2
    low = lax.axis_index("col") % 2 == 0
    for n in range(0, part.shape[1], EDGE):
        upper, lower = part[:half, n:n + EDGE], part[half:, n:n + EDGE]
        rows = pl.ds(n // EDGE * half, half)
        keep_ref[rows, :] = jnp.where(low, upper, lower)
        send_ref[rows, :] = jnp.where(low, lower, upper)


def load_lhs(stage, lhs, copies):
    width, node_dev = stage.shape[1:]
    for i in range(len(copies)):
        copies[i].wait()
        hi, lo = split(stage[i])
        lhs[:width, i * node_dev:(i + 1) * node_dev] = hi
        lhs[width:, i * node_dev:(i + 1) * node_dev] = lo


def partial_kernel(n_in, tile_ref, *refs):
    parts = refs[:n_in]
    out_ref, rest_ref, dense, stage, lhs, sems, dense_sems, rest_sem = refs[n_in:]
    width, node_dev = stage.shape[1:]
    col_nodes = dense.shape[1]
    blocks = fetch(
        [(tile_ref.at[span], dense.at[span]) for span in (
            pl.ds(i * node_dev, node_dev) for i in range(n_in))], dense_sems)
    copies = fetch([(r, stage.at[i]) for i, r in enumerate(parts)], sems)
    rest = pltpu.make_async_copy(
        tile_ref.at[pl.ds(n_in * node_dev, rest_ref.shape[0])], rest_ref, rest_sem)
    rest.start()
    load_lhs(stage, lhs, copies)
    for copy in blocks:
        copy.wait()
    step = 2 * EDGE if col_nodes % (2 * EDGE) == 0 else EDGE
    for n in range(0, col_nodes, step):
        pair = jnp.dot(lhs[...], dense[:, n:n + step], preferred_element_type=F32)
        out_ref[:, n:n + step] = pair[:width] + pair[width:]
    rest.wait()


def last_kernel(n_in, n_out, deg_ref, dense_ref, sofar_ref, *refs):
    parts, outs = refs[:n_in], refs[n_in:n_in + n_out]
    dense, stage, lhs, sofar, sems, dense_sem, sofar_sem = refs[n_in + n_out:]
    width, node_dev = parts[0].shape
    col_nodes = dense.shape[1]
    block = pltpu.make_async_copy(dense_ref, dense, dense_sem)
    before = pltpu.make_async_copy(sofar_ref, sofar, sofar_sem)
    block.start()
    size = col_nodes // n_out
    copies = fetch([(r, stage.at[i]) for i, r in enumerate(parts)], sems)
    before.start()
    load_lhs(stage, lhs, copies)
    block.wait()
    before.wait()
    step = 2 * EDGE if col_nodes % (2 * EDGE) == 0 else EDGE
    first = lax.axis_index("col") * (col_nodes // EDGE)
    for n in range(0, col_nodes, step):
        pair = jnp.dot(lhs[...], dense[:, n:n + step], preferred_element_type=F32)
        total = sofar[:, n:n + step] + (pair[:width] + pair[width:])
        for at in range(n, n + step, EDGE):
            inv = inv_column(deg_ref, first + at // EDGE)
            out = outs[at // size]
            out[at % size:at % size + EDGE, :] = inv * jnp.transpose(total[:, at - n:at - n + EDGE])


def body(n_row, n_col, features, degrees, block_rows, block_cols, live_slots, blocks, weight, cotangent):
    n_chip = n_col // 2
    chip_bits, row_bits = n_chip.bit_length() - 1, n_row.bit_length() - 1
    assert n_col == 2 << chip_bits and n_row == 1 << row_bits
    node_dev, hidden = cotangent.shape
    col_nodes, width = features.shape
    row_nodes = node_dev * n_col
    nodes = col_nodes * n_col
    slots = blocks.shape[2]
    deg = degrees.reshape(nodes // EDGE, EDGE)
    col_blocks = col_nodes // EDGE
    dev_blocks = node_dev // EDGE
    assert n_chip >= 4
    chunk = 16
    panel_dev = n_col
    while panel_dev % 2 == 0 and panel_dev * node_dev * col_nodes * 4 > ACC_BYTES:
        panel_dev //= 2
    positions = panel_dev * dev_blocks * col_blocks
    smem = pl.BlockSpec(memory_space=pltpu.SMEM)
    any_space = pl.BlockSpec(memory_space=pl.ANY)
    vmem = pl.BlockSpec(memory_space=pltpu.VMEM)

    def params(mib):
        return pltpu.CompilerParams(vmem_limit_bytes=mib << 20)

    def after(x, other):
        corner = 0.0 * other[:8, :EDGE]
        if x.shape[0] == other.shape[0] and x.shape[1] <= other.shape[1]:
            return x + 0.0 * other[:, :x.shape[1]]
        return (x.reshape(-1, 8, EDGE) + corner).reshape(x.shape)

    def ahead(x):
        return lax.optimization_barrier(x)

    def cost(flops, read):
        return pl.CostEstimate(flops=flops, bytes_accessed=read, transcendentals=0)

    *pieces, tile = pl.pallas_call(
        functools.partial(forward_kernel, n_col, chunk, panel_dev, node_dev),
        out_shape=[jax.ShapeDtypeStruct((node_dev, width), F32)] * n_col
        + [jax.ShapeDtypeStruct((row_nodes, col_nodes), BF16)],
        in_specs=[smem, smem, smem, vmem, vmem, any_space],
        out_specs=[any_space] * (n_col + 1),
        scratch_shapes=[
            pltpu.VMEM((positions + 1, EDGE // QUARTERS, EDGE), F32) for _ in range(QUARTERS)
        ] + [
            pltpu.VMEM((panel_dev, 2 * node_dev, col_nodes), BF16),
            pltpu.VMEM((slots, EDGE, EDGE), BF16),
            pltpu.VMEM((col_nodes, width), BF16),
            pltpu.VMEM((panel_dev, node_dev, width), F32),
            pltpu.SemaphoreType.DMA((slots // chunk,)),
            pltpu.SemaphoreType.DMA((panel_dev,)),
            pltpu.SemaphoreType.DMA((panel_dev,)),
        ],
        compiler_params=params(54),
        name="densify_forward",
    )(block_rows, block_cols, live_slots, deg, features, blocks)
    keep, send = pieces[0::2], pieces[1::2]

    swap_pairs = [(i, i ^ 1) for i in range(n_col)]

    def swap(x):
        return lax.ppermute(x, "col", swap_pairs)

    def chip_flip(x, bit):
        return lax.ppermute(x, "col", [(i, i ^ (2 << bit)) for i in range(n_col)])

    def row_flip(x, bit):
        return lax.ppermute(x, "row", [(i, i ^ (1 << bit)) for i in range(n_row)])

    def low_bit(m):
        return (m & -m).bit_length() - 1

    last = n_chip - 1
    kept = {m: [keep[m], swap(send[m])] for m in range(last, -1, -1)}
    parts = [functools.reduce(jnp.add, kept[0])]
    arrived = {m: [] for m in range(n_chip)}
    for m in range(last, 0, -1):
        if m == last:
            unit = ahead(after(kept[m][0], kept[m][0])) + kept[m][1]
        else:
            unit = functools.reduce(jnp.add, kept[m])
            if m == 2:
                unit = ahead(after(unit, parts[0]))
            unit = functools.reduce(jnp.add, [unit] + arrived[m])
        arrived[m & (m - 1)].append(chip_flip(unit, low_bit(m)))
    kept[0] = arrived[0]
    parts += kept[0]

    half = width // 2
    out_act, pulled, wkeep, wsend = pl.pallas_call(
        functools.partial(middle_kernel, n_col, len(parts), float(nodes) ** (-0.5)),
        out_shape=(
            jax.ShapeDtypeStruct((node_dev, hidden), BF16),
            jax.ShapeDtypeStruct((width, node_dev), F32),
            jax.ShapeDtypeStruct((half * hidden // EDGE, EDGE), F32),
            jax.ShapeDtypeStruct((half * hidden // EDGE, EDGE), F32),
        ),
        in_specs=[vmem] * (3 + len(parts)),
        out_specs=(vmem,) * 4,
        compiler_params=params(16),
        name="middle",
    )(deg, cotangent, weight, *parts)

    own = {0: pulled}
    for m in range(1, n_chip):
        own[m] = chip_flip(own[m & (m - 1)], low_bit(m))
    own[1] = after(own[1], own[2])
    other = {m: swap(own[m]) for m in range(last)}

    wsum = wkeep + swap(wsend)
    wsum = wsum + chip_flip(wsum, 0)
    early = [x for m in range(last) for x in (own[m], other[m])]
    late_rows = 2 * node_dev
    sofar, rest = pl.pallas_call(
        functools.partial(partial_kernel, len(early)),
        out_shape=(
            jax.ShapeDtypeStruct((width, col_nodes), F32),
            jax.ShapeDtypeStruct((late_rows, col_nodes), BF16),
        ),
        in_specs=[any_space] * (1 + len(early)),
        out_specs=(vmem, any_space),
        scratch_shapes=[
            pltpu.VMEM((len(early) * node_dev, col_nodes), BF16),
            pltpu.VMEM((len(early), width, node_dev), F32),
            pltpu.VMEM((2 * width, len(early) * node_dev), BF16),
            pltpu.SemaphoreType.DMA((len(early),)),
            pltpu.SemaphoreType.DMA((len(early),)),
            pltpu.SemaphoreType.DMA,
        ],
        compiler_params=params(BWD),
        cost_estimate=cost(row_nodes * col_nodes * width * 4, 32 << 20),
        name="backward_early",
    )(tile, *early)

    own[last] = after(after(own[last], sofar), wsum)
    late = [own[last], swap(own[last])]
    for bit in range(1, chip_bits):
        wsum = wsum + chip_flip(wsum, bit)
    n_piece = max(1, row_bits)
    while col_nodes % (EDGE * n_piece):
        n_piece -= 1
    size = col_nodes // n_piece
    done = pl.pallas_call(
        functools.partial(last_kernel, len(late), n_piece),
        out_shape=(jax.ShapeDtypeStruct((size, width), F32),) * n_piece,
        in_specs=[vmem, any_space, any_space] + [any_space] * len(late),
        out_specs=(vmem,) * n_piece,
        scratch_shapes=[
            pltpu.VMEM((len(late) * node_dev, col_nodes), BF16),
            pltpu.VMEM((len(late), width, node_dev), F32),
            pltpu.VMEM((2 * width, len(late) * node_dev), BF16),
            pltpu.VMEM((width, col_nodes), F32),
            pltpu.SemaphoreType.DMA((len(late),)),
            pltpu.SemaphoreType.DMA,
            pltpu.SemaphoreType.DMA,
        ],
        compiler_params=params(BWD),
        name="backward_late",
    )(deg, rest, sofar, *late)

    done = list(done)
    for t in range(row_bits):
        wsum = after(wsum, done[0])
        wsum = wsum + row_flip(wsum, t)
        done = [x + row_flip(x, (i + t) % row_bits) for i, x in enumerate(done)]
        if t == 0:
            done[-1] = after(done[-1], wsum)
    wsum = after(wsum, done[0])
    feat_grad = jnp.concatenate(done, axis=0)

    wother = swap(wsum)
    low = lax.axis_index("col") % 2 == 0
    halves = (jnp.where(low, wsum, wother), jnp.where(low, wother, wsum))
    weight_grad = jnp.concatenate(
        [jnp.concatenate([x[i:i + half] for i in range(0, x.shape[0], half)], axis=1) for x in halves],
        axis=0,
    )
    return out_act, feat_grad, weight_grad


def solution(mesh):
    n_row, n_col = mesh.shape["row"], mesh.shape["col"]
    return jax.shard_map(
        functools.partial(body, n_row, n_col),
        mesh=mesh,
        in_specs=(
            P("col", None),
            P(),
            P("row", "col", None),
            P("row", "col", None),
            P("row", "col"),
            P("row", "col", None, None, None),
            P(),
            P(("row", "col"), None),
        ),
        out_specs=(P(("row", "col"), None), P("col", None), P()),
        check_vma=False,
    )
```

```python
import functools

import jax
import jax.numpy as jnp
from jax import lax
from jax.experimental import pallas as pl
from jax.experimental.pallas import tpu as pltpu
from jax.sharding import PartitionSpec as P

F32 = jnp.float32
BF16 = jnp.bfloat16
EDGE = 128
GROUP = 16
QUARTERS = 4
AHEAD = 3
BWD = 50
ACC_BYTES = 8 << 20
GELU_C = 0.7978845608028654
GELU_K = 0.044715


def inv_column(deg_ref, start):
    row = lax.rsqrt(deg_ref[pl.ds(start, 1), :].astype(F32))
    return jnp.transpose(jnp.broadcast_to(row, (EDGE, EDGE)))


def split(value):
    hi = value.astype(BF16)
    return hi, (value - hi.astype(F32)).astype(BF16)


def across(a, b):
    return lax.dot_general(a, b, (((0,), (0,)), ((), ())), preferred_element_type=F32)


def fetch(pairs, sems):
    copies = [pltpu.make_async_copy(src, dst, sems.at[i]) for i, (src, dst) in enumerate(pairs)]
    for copy in copies:
        copy.start()
    return copies


def halve(value, size):
    if size & (size - 1) == 0:
        shift = size.bit_length() - 1
        return lax.shift_right_logical(value, shift), value & (size - 1)
    return lax.div(value, size), lax.rem(value, size)


def forward_kernel(
    n_col, chunk, panel_dev, node_dev,
    rows_ref, cols_ref, live_ref, deg_ref, feat_ref, blocks_ref, *refs,
):
    outs, tile_ref = refs[:n_col], refs[n_col]
    accs, (both, buf, scaled, result, in_sems, dense_sems, out_sems) = refs[n_col + 1:-7], refs[-7:]
    part = EDGE // len(accs)
    slots = buf.shape[0]
    col_nodes, width = feat_ref.shape
    col_blocks = col_nodes // EDGE
    dev_blocks = node_dev // EDGE
    panel_blocks = panel_dev * dev_blocks
    positions = panel_blocks * col_blocks
    n_panels = n_col // panel_dev
    n_chunks = slots // chunk
    me = lax.axis_index("col")
    live = live_ref[0, 0]

    def block_copy(c):
        span = pl.ds(c * chunk, chunk)
        return pltpu.make_async_copy(blocks_ref.at[0, 0, span], buf.at[span], in_sems.at[c])

    def dense_copy(rel, j):
        there = tile_ref.at[pl.ds(rel * node_dev, node_dev)]
        return pltpu.make_async_copy(both.at[j, pl.ds(0, node_dev)], there, dense_sems.at[j])

    def result_copy(rel, j):
        return pltpu.make_async_copy(result.at[j], outs[rel], out_sems.at[j])

    for c in range(n_chunks):
        block_copy(c).start()

    for k in range(col_blocks):
        inv = inv_column(deg_ref, me * col_blocks + k)
        span = pl.ds(k * EDGE, EDGE)
        scaled[span, :] = (inv * feat_ref[span, :].astype(F32)).astype(BF16)

    def add_slots(first, place):
        pending = []

        def finish():
            acc, p, sofar, block = pending.pop(0)
            acc[p] = sofar + block.astype(F32)

        for s in range(GROUP):
            p = place(first + s)
            for q, acc in enumerate(accs):
                pending.append((acc, p, acc[p], buf[first + s, q * part:(q + 1) * part, :]))
                if len(pending) > AHEAD:
                    finish()
        while pending:
            finish()

    for panel in range(n_panels):
        base = panel * panel_blocks

        @pl.loop(0, positions)
        def _(p):
            for acc in accs:
                acc[p] = jnp.zeros((part, EDGE), F32)

        def place(s):
            dev, inner = halve(rows_ref[0, 0, s], dev_blocks)
            r = (dev ^ me) * dev_blocks + inner - base
            ok = s < live
            if n_panels > 1:
                ok = ok & (r >= 0) & (r < panel_blocks)
            return jnp.where(ok, r * col_blocks + cols_ref[0, 0, s], positions)

        @pl.loop(0, n_chunks)
        def _(c):
            if panel == 0:
                block_copy(c).wait()

            @pl.loop(0, chunk // GROUP)
            def _(g):
                add_slots(c * chunk + g * GROUP, place)

        for j in reversed(range(panel_dev)):
            rel = panel * panel_dev + j
            if panel:
                dense_copy(rel - panel_dev, j).wait()
                result_copy(rel - panel_dev, j).wait()
            for b in range(dev_blocks):
                for cb in range(col_blocks):
                    lanes = slice(cb * EDGE, (cb + 1) * EDGE)
                    for q, acc in enumerate(accs):
                        hi, lo = split(acc[(j * dev_blocks + b) * col_blocks + cb])
                        at = b * EDGE + q * part
                        both[j, at:at + part, lanes] = hi
                        both[j, node_dev + at:node_dev + at + part, lanes] = lo
            dense_copy(rel, j).start()
            pair = jnp.dot(both[j], scaled[...], preferred_element_type=F32)
            result[j] = pair[:node_dev] + pair[node_dev:]
            result_copy(rel, j).start()

    for j in range(panel_dev):
        rel = (n_panels - 1) * panel_dev + j
        dense_copy(rel, j).wait()
        result_copy(rel, j).wait()


def middle_kernel(n_col, n_in, scale, deg_ref, cot_ref, weight_ref, *refs):
    parts = refs[:n_in]
    act_ref, pulled_ref, keep_ref, send_ref = refs[n_in:]
    node_dev = cot_ref.shape[0]
    dev_blocks = node_dev // EDGE
    base = (lax.axis_index("row") * n_col + lax.axis_index("col")) * dev_blocks
    inv = jnp.concatenate([inv_column(deg_ref, base + k) for k in range(dev_blocks)], axis=0)
    summed = parts[0][...]
    for ref in parts[1:]:
        summed = summed + ref[...]
    propagated = inv * summed
    prop_hi, prop_lo = split(propagated)
    weight = weight_ref[...]
    pair = jnp.dot(
        jnp.concatenate([prop_hi, prop_lo], axis=0), weight, preferred_element_type=F32)
    v = pair[:node_dev] + pair[node_dev:]
    t = jnp.tanh(GELU_C * (v + GELU_K * v * v * v))
    act_ref[...] = (0.5 * v * (1.0 + t)).astype(BF16)
    slope = 0.5 * (1.0 + t) + 0.5 * v * (1.0 - t * t) * (GELU_C * (1.0 + 3.0 * GELU_K * v * v))
    gprime = cot_ref[...].astype(F32) * slope
    hi, lo = split(gprime)
    pair = lax.dot_general(
        jnp.concatenate([hi, lo], axis=0), weight, (((1,), (1,)), ((), ())),
        preferred_element_type=F32,
    )
    pulled_ref[...] = jnp.transpose(inv * (pair[:node_dev] + pair[node_dev:]))
    pair = across(jnp.concatenate([prop_hi, prop_lo], axis=1), hi)
    part = scale * (pair[:EDGE] + (pair[EDGE:] + across(prop_hi, lo)))
    half = EDGE // 2
    low = lax.axis_index("col") % 2 == 0
    for n in range(0, part.shape[1], EDGE):
        upper, lower = part[:half, n:n + EDGE], part[half:, n:n + EDGE]
        rows = pl.ds(n // EDGE * half, half)
        keep_ref[rows, :] = jnp.where(low, upper, lower)
        send_ref[rows, :] = jnp.where(low, lower, upper)


def load_lhs(stage, lhs, copies):
    width, node_dev = stage.shape[1:]
    for i in range(len(copies)):
        copies[i].wait()
        hi, lo = split(stage[i])
        lhs[:width, i * node_dev:(i + 1) * node_dev] = hi
        lhs[width:, i * node_dev:(i + 1) * node_dev] = lo


def partial_kernel(n_in, tile_ref, *refs):
    parts = refs[:n_in]
    out_ref, rest_ref, dense, stage, lhs, sems, dense_sems, rest_sem = refs[n_in:]
    width, node_dev = stage.shape[1:]
    col_nodes = dense.shape[1]
    blocks = fetch(
        [(tile_ref.at[span], dense.at[span]) for span in (
            pl.ds(i * node_dev, node_dev) for i in range(n_in))], dense_sems)
    copies = fetch([(r, stage.at[i]) for i, r in enumerate(parts)], sems)
    rest = pltpu.make_async_copy(
        tile_ref.at[pl.ds(n_in * node_dev, rest_ref.shape[0])], rest_ref, rest_sem)
    rest.start()
    load_lhs(stage, lhs, copies)
    for copy in blocks:
        copy.wait()
    step = 2 * EDGE if col_nodes % (2 * EDGE) == 0 else EDGE
    for n in range(0, col_nodes, step):
        pair = jnp.dot(lhs[...], dense[:, n:n + step], preferred_element_type=F32)
        out_ref[:, n:n + step] = pair[:width] + pair[width:]
    rest.wait()


def last_kernel(n_in, n_out, deg_ref, dense_ref, sofar_ref, *refs):
    parts, outs = refs[:n_in], refs[n_in:n_in + n_out]
    dense, stage, lhs, sofar, sems, dense_sem, sofar_sem = refs[n_in + n_out:]
    width, node_dev = parts[0].shape
    col_nodes = dense.shape[1]
    block = pltpu.make_async_copy(dense_ref, dense, dense_sem)
    before = pltpu.make_async_copy(sofar_ref, sofar, sofar_sem)
    block.start()
    size = col_nodes // n_out
    copies = fetch([(r, stage.at[i]) for i, r in enumerate(parts)], sems)
    before.start()
    load_lhs(stage, lhs, copies)
    block.wait()
    before.wait()
    step = 2 * EDGE if col_nodes % (2 * EDGE) == 0 else EDGE
    first = lax.axis_index("col") * (col_nodes // EDGE)
    for n in range(0, col_nodes, step):
        pair = jnp.dot(lhs[...], dense[:, n:n + step], preferred_element_type=F32)
        total = sofar[:, n:n + step] + (pair[:width] + pair[width:])
        for at in range(n, n + step, EDGE):
            inv = inv_column(deg_ref, first + at // EDGE)
            out = outs[at // size]
            out[at % size:at % size + EDGE, :] = inv * jnp.transpose(total[:, at - n:at - n + EDGE])


def body(n_row, n_col, features, degrees, block_rows, block_cols, live_slots, blocks, weight, cotangent):
    n_chip = n_col // 2
    chip_bits, row_bits = n_chip.bit_length() - 1, n_row.bit_length() - 1
    assert n_col == 2 << chip_bits and n_row == 1 << row_bits
    node_dev, hidden = cotangent.shape
    col_nodes, width = features.shape
    row_nodes = node_dev * n_col
    nodes = col_nodes * n_col
    slots = blocks.shape[2]
    deg = degrees.reshape(nodes // EDGE, EDGE)
    col_blocks = col_nodes // EDGE
    dev_blocks = node_dev // EDGE
    assert n_chip >= 4
    chunk = 16
    panel_dev = n_col
    while panel_dev % 2 == 0 and panel_dev * node_dev * col_nodes * 4 > ACC_BYTES:
        panel_dev //= 2
    positions = panel_dev * dev_blocks * col_blocks
    smem = pl.BlockSpec(memory_space=pltpu.SMEM)
    any_space = pl.BlockSpec(memory_space=pl.ANY)
    vmem = pl.BlockSpec(memory_space=pltpu.VMEM)

    def params(mib):
        return pltpu.CompilerParams(vmem_limit_bytes=mib << 20)

    def after(x, other):
        corner = 0.0 * other[:8, :EDGE]
        if x.shape[0] == other.shape[0] and x.shape[1] <= other.shape[1]:
            return x + 0.0 * other[:, :x.shape[1]]
        return (x.reshape(-1, 8, EDGE) + corner).reshape(x.shape)

    def ahead(x):
        return lax.optimization_barrier(x)

    def cost(flops, read):
        return pl.CostEstimate(flops=flops, bytes_accessed=read, transcendentals=0)

    *pieces, tile = pl.pallas_call(
        functools.partial(forward_kernel, n_col, chunk, panel_dev, node_dev),
        out_shape=[jax.ShapeDtypeStruct((node_dev, width), F32)] * n_col
        + [jax.ShapeDtypeStruct((row_nodes, col_nodes), BF16)],
        in_specs=[smem, smem, smem, vmem, vmem, any_space],
        out_specs=[any_space] * (n_col + 1),
        scratch_shapes=[
            pltpu.VMEM((positions + 1, EDGE // QUARTERS, EDGE), F32) for _ in range(QUARTERS)
        ] + [
            pltpu.VMEM((panel_dev, 2 * node_dev, col_nodes), BF16),
            pltpu.VMEM((slots, EDGE, EDGE), BF16),
            pltpu.VMEM((col_nodes, width), BF16),
            pltpu.VMEM((panel_dev, node_dev, width), F32),
            pltpu.SemaphoreType.DMA((slots // chunk,)),
            pltpu.SemaphoreType.DMA((panel_dev,)),
            pltpu.SemaphoreType.DMA((panel_dev,)),
        ],
        compiler_params=params(54),
        name="densify_forward",
    )(block_rows, block_cols, live_slots, deg, features, blocks)
    keep, send = pieces[0::2], pieces[1::2]

    swap_pairs = [(i, i ^ 1) for i in range(n_col)]

    def swap(x):
        return lax.ppermute(x, "col", swap_pairs)

    def chip_flip(x, bit):
        return lax.ppermute(x, "col", [(i, i ^ (2 << bit)) for i in range(n_col)])

    def row_flip(x, bit):
        return lax.ppermute(x, "row", [(i, i ^ (1 << bit)) for i in range(n_row)])

    def low_bit(m):
        return (m & -m).bit_length() - 1

    last = n_chip - 1
    kept = {m: [keep[m], swap(send[m])] for m in range(last, -1, -1)}
    parts = [functools.reduce(jnp.add, kept[0])]
    arrived = {m: [] for m in range(n_chip)}
    for m in range(last, 0, -1):
        if m == last:
            unit = ahead(after(kept[m][0], kept[m][0])) + kept[m][1]
        else:
            unit = functools.reduce(jnp.add, kept[m])
            if m == 2:
                unit = ahead(after(unit, parts[0]))
            unit = functools.reduce(jnp.add, [unit] + arrived[m])
        arrived[m & (m - 1)].append(chip_flip(unit, low_bit(m)))
    kept[0] = arrived[0]
    parts += kept[0]

    half = width // 2
    out_act, pulled, wkeep, wsend = pl.pallas_call(
        functools.partial(middle_kernel, n_col, len(parts), float(nodes) ** (-0.5)),
        out_shape=(
            jax.ShapeDtypeStruct((node_dev, hidden), BF16),
            jax.ShapeDtypeStruct((width, node_dev), F32),
            jax.ShapeDtypeStruct((half * hidden // EDGE, EDGE), F32),
            jax.ShapeDtypeStruct((half * hidden // EDGE, EDGE), F32),
        ),
        in_specs=[vmem] * (3 + len(parts)),
        out_specs=(vmem,) * 4,
        compiler_params=params(16),
        name="middle",
    )(deg, cotangent, weight, *parts)

    own = {0: pulled}
    for m in range(1, n_chip):
        own[m] = chip_flip(own[m & (m - 1)], low_bit(m))
    other = {m: swap(own[m]) for m in range(last)}

    wsum = after(wkeep + swap(wsend), other[2])
    moved = chip_flip(wsum, 0)
    early = [x for m in range(last) for x in (own[m], other[m])]
    late_rows = 2 * node_dev
    sofar, rest = pl.pallas_call(
        functools.partial(partial_kernel, len(early)),
        out_shape=(
            jax.ShapeDtypeStruct((width, col_nodes), F32),
            jax.ShapeDtypeStruct((late_rows, col_nodes), BF16),
        ),
        in_specs=[any_space] * (1 + len(early)),
        out_specs=(vmem, any_space),
        scratch_shapes=[
            pltpu.VMEM((len(early) * node_dev, col_nodes), BF16),
            pltpu.VMEM((len(early), width, node_dev), F32),
            pltpu.VMEM((2 * width, len(early) * node_dev), BF16),
            pltpu.SemaphoreType.DMA((len(early),)),
            pltpu.SemaphoreType.DMA((len(early),)),
            pltpu.SemaphoreType.DMA,
        ],
        compiler_params=params(BWD),
        cost_estimate=cost(row_nodes * col_nodes * width * 4, 32 << 20),
        name="backward_early",
    )(tile, *early)

    wsum = after(wsum, sofar) + moved
    own[last] = after(after(own[last], sofar), wsum)
    late = [own[last], swap(own[last])]
    for bit in range(1, chip_bits):
        wsum = wsum + chip_flip(wsum, bit)
    n_piece = max(1, row_bits)
    while col_nodes % (EDGE * n_piece):
        n_piece -= 1
    size = col_nodes // n_piece
    done = pl.pallas_call(
        functools.partial(last_kernel, len(late), n_piece),
        out_shape=(jax.ShapeDtypeStruct((size, width), F32),) * n_piece,
        in_specs=[vmem, any_space, any_space] + [any_space] * len(late),
        out_specs=(vmem,) * n_piece,
        scratch_shapes=[
            pltpu.VMEM((len(late) * node_dev, col_nodes), BF16),
            pltpu.VMEM((len(late), width, node_dev), F32),
            pltpu.VMEM((2 * width, len(late) * node_dev), BF16),
            pltpu.VMEM((width, col_nodes), F32),
            pltpu.SemaphoreType.DMA((len(late),)),
            pltpu.SemaphoreType.DMA,
            pltpu.SemaphoreType.DMA,
        ],
        compiler_params=params(BWD),
        name="backward_late",
    )(deg, rest, sofar, *late)

    done = list(done)
    for t in range(row_bits):
        wsum = after(wsum, done[-1 if t == 0 else 0])
        wsum = wsum + row_flip(wsum, t)
        done = [x + row_flip(x, (i + t) % row_bits) for i, x in enumerate(done)]
        if t == 0:
            done[-1] = after(done[-1], wsum)
    wsum = after(wsum, done[0])
    feat_grad = jnp.concatenate(done, axis=0)

    wother = swap(wsum)
    low = lax.axis_index("col") % 2 == 0
    halves = (jnp.where(low, wsum, wother), jnp.where(low, wother, wsum))
    weight_grad = jnp.concatenate(
        [jnp.concatenate([x[i:i + half] for i in range(0, x.shape[0], half)], axis=1) for x in halves],
        axis=0,
    )
    return out_act, feat_grad, weight_grad


def solution(mesh):
    n_row, n_col = mesh.shape["row"], mesh.shape["col"]
    return jax.shard_map(
        functools.partial(body, n_row, n_col),
        mesh=mesh,
        in_specs=(
            P("col", None),
            P(),
            P("row", "col", None),
            P("row", "col", None),
            P("row", "col"),
            P("row", "col", None, None, None),
            P(),
            P(("row", "col"), None),
        ),
        out_specs=(P(("row", "col"), None), P("col", None), P()),
        check_vma=False,
    )
```

```python
import functools

import jax
import jax.numpy as jnp
from jax import lax
from jax.experimental import pallas as pl
from jax.experimental.pallas import tpu as pltpu
from jax.sharding import PartitionSpec as P

F32 = jnp.float32
BF16 = jnp.bfloat16
EDGE = 128
GROUP = 16
QUARTERS = 4
AHEAD = 3
BWD = 50
ACC_BYTES = 8 << 20
GELU_C = 0.7978845608028654
GELU_K = 0.044715


def inv_column(deg_ref, start):
    row = lax.rsqrt(deg_ref[pl.ds(start, 1), :].astype(F32))
    return jnp.transpose(jnp.broadcast_to(row, (EDGE, EDGE)))


def split(value):
    hi = value.astype(BF16)
    return hi, (value - hi.astype(F32)).astype(BF16)


def across(a, b):
    return lax.dot_general(a, b, (((0,), (0,)), ((), ())), preferred_element_type=F32)


def fetch(pairs, sems):
    copies = [pltpu.make_async_copy(src, dst, sems.at[i]) for i, (src, dst) in enumerate(pairs)]
    for copy in copies:
        copy.start()
    return copies


def halve(value, size):
    if size & (size - 1) == 0:
        shift = size.bit_length() - 1
        return lax.shift_right_logical(value, shift), value & (size - 1)
    return lax.div(value, size), lax.rem(value, size)


def forward_kernel(
    n_col, chunk, panel_dev, node_dev,
    rows_hbm, cols_hbm, live_ref, deg_hbm, feat_hbm, blocks_ref, *refs,
):
    outs, tile_ref = refs[:n_col], refs[n_col]
    accs, refs = refs[n_col + 1:-12], refs[-12:]
    both, buf, scaled, result, rows_ref, cols_ref, deg_ref, feat_ref = refs[:8]
    in_sems, dense_sems, out_sems, small_sems = refs[8:]
    part = EDGE // len(accs)
    slots = buf.shape[0]
    col_nodes, width = feat_ref.shape
    col_blocks = col_nodes // EDGE
    dev_blocks = node_dev // EDGE
    panel_blocks = panel_dev * dev_blocks
    positions = panel_blocks * col_blocks
    n_panels = n_col // panel_dev
    n_chunks = slots // chunk
    me = lax.axis_index("col")
    live = live_ref[0, 0]

    def block_copy(c):
        span = pl.ds(c * chunk, chunk)
        return pltpu.make_async_copy(blocks_ref.at[0, 0, span], buf.at[span], in_sems.at[c])

    def dense_copy(rel, j):
        there = tile_ref.at[pl.ds(rel * node_dev, node_dev)]
        return pltpu.make_async_copy(both.at[j, pl.ds(0, node_dev)], there, dense_sems.at[j])

    def result_copy(rel, j):
        return pltpu.make_async_copy(result.at[j], outs[rel], out_sems.at[j])

    block_copy(0).start()
    small = fetch(
        [(rows_hbm, rows_ref), (cols_hbm, cols_ref), (deg_hbm, deg_ref), (feat_hbm, feat_ref)],
        small_sems)
    for c in range(1, n_chunks):
        block_copy(c).start()
    for copy in small:
        copy.wait()

    for k in range(col_blocks):
        inv = inv_column(deg_ref, me * col_blocks + k)
        span = pl.ds(k * EDGE, EDGE)
        scaled[span, :] = (inv * feat_ref[span, :].astype(F32)).astype(BF16)

    def add_slots(first, place):
        pending = []

        def finish():
            acc, p, sofar, block = pending.pop(0)
            acc[p] = sofar + block.astype(F32)

        for s in range(GROUP):
            p = place(first + s)
            for q, acc in enumerate(accs):
                pending.append((acc, p, acc[p], buf[first + s, q * part:(q + 1) * part, :]))
                if len(pending) > AHEAD:
                    finish()
        while pending:
            finish()

    for panel in range(n_panels):
        base = panel * panel_blocks

        @pl.loop(0, positions)
        def _(p):
            for acc in accs:
                acc[p] = jnp.zeros((part, EDGE), F32)

        def place(s):
            dev, inner = halve(rows_ref[0, 0, s], dev_blocks)
            r = (dev ^ me) * dev_blocks + inner - base
            ok = s < live
            if n_panels > 1:
                ok = ok & (r >= 0) & (r < panel_blocks)
            return jnp.where(ok, r * col_blocks + cols_ref[0, 0, s], positions)

        @pl.loop(0, n_chunks)
        def _(c):
            if panel == 0:
                block_copy(c).wait()

            @pl.loop(0, chunk // GROUP)
            def _(g):
                add_slots(c * chunk + g * GROUP, place)

        for j in reversed(range(panel_dev)):
            rel = panel * panel_dev + j
            if panel:
                dense_copy(rel - panel_dev, j).wait()
                result_copy(rel - panel_dev, j).wait()
            for b in range(dev_blocks):
                for cb in range(col_blocks):
                    lanes = slice(cb * EDGE, (cb + 1) * EDGE)
                    for q, acc in enumerate(accs):
                        hi, lo = split(acc[(j * dev_blocks + b) * col_blocks + cb])
                        at = b * EDGE + q * part
                        both[j, at:at + part, lanes] = hi
                        both[j, node_dev + at:node_dev + at + part, lanes] = lo
            dense_copy(rel, j).start()
            pair = jnp.dot(both[j], scaled[...], preferred_element_type=F32)
            result[j] = pair[:node_dev] + pair[node_dev:]
            result_copy(rel, j).start()

    for j in range(panel_dev):
        rel = (n_panels - 1) * panel_dev + j
        dense_copy(rel, j).wait()
        result_copy(rel, j).wait()


def middle_kernel(n_col, n_in, scale, deg_ref, cot_ref, weight_ref, *refs):
    parts = refs[:n_in]
    act_ref, pulled_ref, keep_ref, send_ref = refs[n_in:]
    node_dev = cot_ref.shape[0]
    dev_blocks = node_dev // EDGE
    base = (lax.axis_index("row") * n_col + lax.axis_index("col")) * dev_blocks
    inv = jnp.concatenate([inv_column(deg_ref, base + k) for k in range(dev_blocks)], axis=0)
    summed = parts[0][...]
    for ref in parts[1:]:
        summed = summed + ref[...]
    propagated = inv * summed
    prop_hi, prop_lo = split(propagated)
    weight = weight_ref[...]
    pair = jnp.dot(
        jnp.concatenate([prop_hi, prop_lo], axis=0), weight, preferred_element_type=F32)
    v = pair[:node_dev] + pair[node_dev:]
    t = jnp.tanh(GELU_C * (v + GELU_K * v * v * v))
    act_ref[...] = (0.5 * v * (1.0 + t)).astype(BF16)
    slope = 0.5 * (1.0 + t) + 0.5 * v * (1.0 - t * t) * (GELU_C * (1.0 + 3.0 * GELU_K * v * v))
    gprime = cot_ref[...].astype(F32) * slope
    hi, lo = split(gprime)
    pair = lax.dot_general(
        jnp.concatenate([hi, lo], axis=0), weight, (((1,), (1,)), ((), ())),
        preferred_element_type=F32,
    )
    pulled_ref[...] = jnp.transpose(inv * (pair[:node_dev] + pair[node_dev:]))
    pair = across(jnp.concatenate([prop_hi, prop_lo], axis=1), hi)
    part = scale * (pair[:EDGE] + (pair[EDGE:] + across(prop_hi, lo)))
    half = EDGE // 2
    low = lax.axis_index("col") % 2 == 0
    for n in range(0, part.shape[1], EDGE):
        upper, lower = part[:half, n:n + EDGE], part[half:, n:n + EDGE]
        rows = pl.ds(n // EDGE * half, half)
        keep_ref[rows, :] = jnp.where(low, upper, lower)
        send_ref[rows, :] = jnp.where(low, lower, upper)


def load_lhs(stage, lhs, copies):
    width, node_dev = stage.shape[1:]
    for i in range(len(copies)):
        copies[i].wait()
        hi, lo = split(stage[i])
        lhs[:width, i * node_dev:(i + 1) * node_dev] = hi
        lhs[width:, i * node_dev:(i + 1) * node_dev] = lo


def partial_kernel(n_in, tile_ref, *refs):
    parts = refs[:n_in]
    out_ref, rest_ref, dense, stage, lhs, sems, dense_sems, rest_sem = refs[n_in:]
    width, node_dev = stage.shape[1:]
    col_nodes = dense.shape[1]
    blocks = fetch(
        [(tile_ref.at[span], dense.at[span]) for span in (
            pl.ds(i * node_dev, node_dev) for i in range(n_in))], dense_sems)
    copies = fetch([(r, stage.at[i]) for i, r in enumerate(parts)], sems)
    rest = pltpu.make_async_copy(
        tile_ref.at[pl.ds(n_in * node_dev, rest_ref.shape[0])], rest_ref, rest_sem)
    rest.start()
    load_lhs(stage, lhs, copies)
    for copy in blocks:
        copy.wait()
    step = 2 * EDGE if col_nodes % (2 * EDGE) == 0 else EDGE
    for n in range(0, col_nodes, step):
        pair = jnp.dot(lhs[...], dense[:, n:n + step], preferred_element_type=F32)
        out_ref[:, n:n + step] = pair[:width] + pair[width:]
    rest.wait()


def last_kernel(n_in, n_out, deg_ref, dense_ref, sofar_ref, *refs):
    parts, outs = refs[:n_in], refs[n_in:n_in + n_out]
    dense, stage, lhs, sofar, sems, dense_sem, sofar_sem = refs[n_in + n_out:]
    width, node_dev = parts[0].shape
    col_nodes = dense.shape[1]
    block = pltpu.make_async_copy(dense_ref, dense, dense_sem)
    before = pltpu.make_async_copy(sofar_ref, sofar, sofar_sem)
    block.start()
    size = col_nodes // n_out
    copies = fetch([(r, stage.at[i]) for i, r in enumerate(parts)], sems)
    before.start()
    load_lhs(stage, lhs, copies)
    block.wait()
    before.wait()
    step = 2 * EDGE if col_nodes % (2 * EDGE) == 0 else EDGE
    first = lax.axis_index("col") * (col_nodes // EDGE)
    for n in range(0, col_nodes, step):
        pair = jnp.dot(lhs[...], dense[:, n:n + step], preferred_element_type=F32)
        total = sofar[:, n:n + step] + (pair[:width] + pair[width:])
        for at in range(n, n + step, EDGE):
            inv = inv_column(deg_ref, first + at // EDGE)
            out = outs[at // size]
            out[at % size:at % size + EDGE, :] = inv * jnp.transpose(total[:, at - n:at - n + EDGE])


def body(n_row, n_col, features, degrees, block_rows, block_cols, live_slots, blocks, weight, cotangent):
    n_chip = n_col // 2
    chip_bits, row_bits = n_chip.bit_length() - 1, n_row.bit_length() - 1
    assert n_col == 2 << chip_bits and n_row == 1 << row_bits
    node_dev, hidden = cotangent.shape
    col_nodes, width = features.shape
    row_nodes = node_dev * n_col
    nodes = col_nodes * n_col
    slots = blocks.shape[2]
    deg = degrees.reshape(nodes // EDGE, EDGE)
    col_blocks = col_nodes // EDGE
    dev_blocks = node_dev // EDGE
    assert n_chip >= 4
    chunk = 16
    panel_dev = n_col
    while panel_dev % 2 == 0 and panel_dev * node_dev * col_nodes * 4 > ACC_BYTES:
        panel_dev //= 2
    positions = panel_dev * dev_blocks * col_blocks
    smem = pl.BlockSpec(memory_space=pltpu.SMEM)
    any_space = pl.BlockSpec(memory_space=pl.ANY)
    vmem = pl.BlockSpec(memory_space=pltpu.VMEM)

    def params(mib):
        return pltpu.CompilerParams(vmem_limit_bytes=mib << 20)

    def after(x, other):
        corner = 0.0 * other[:8, :EDGE]
        if x.shape[0] == other.shape[0] and x.shape[1] <= other.shape[1]:
            return x + 0.0 * other[:, :x.shape[1]]
        return (x.reshape(-1, 8, EDGE) + corner).reshape(x.shape)

    def ahead(x):
        return lax.optimization_barrier(x)

    def cost(flops, read):
        return pl.CostEstimate(flops=flops, bytes_accessed=read, transcendentals=0)

    *pieces, tile = pl.pallas_call(
        functools.partial(forward_kernel, n_col, chunk, panel_dev, node_dev),
        out_shape=[jax.ShapeDtypeStruct((node_dev, width), F32)] * n_col
        + [jax.ShapeDtypeStruct((row_nodes, col_nodes), BF16)],
        in_specs=[any_space, any_space, smem, any_space, any_space, any_space],
        out_specs=[any_space] * (n_col + 1),
        scratch_shapes=[
            pltpu.VMEM((positions + 1, EDGE // QUARTERS, EDGE), F32) for _ in range(QUARTERS)
        ] + [
            pltpu.VMEM((panel_dev, 2 * node_dev, col_nodes), BF16),
            pltpu.VMEM((slots, EDGE, EDGE), BF16),
            pltpu.VMEM((col_nodes, width), BF16),
            pltpu.VMEM((panel_dev, node_dev, width), F32),
            pltpu.SMEM(block_rows.shape, jnp.int32),
            pltpu.SMEM(block_cols.shape, jnp.int32),
            pltpu.VMEM(deg.shape, jnp.int32),
            pltpu.VMEM(features.shape, BF16),
            pltpu.SemaphoreType.DMA((slots // chunk,)),
            pltpu.SemaphoreType.DMA((panel_dev,)),
            pltpu.SemaphoreType.DMA((panel_dev,)),
            pltpu.SemaphoreType.DMA((4,)),
        ],
        compiler_params=params(54),
        name="densify_forward",
    )(block_rows, block_cols, live_slots, deg, features, blocks)
    keep, send = pieces[0::2], pieces[1::2]

    swap_pairs = [(i, i ^ 1) for i in range(n_col)]

    def swap(x):
        return lax.ppermute(x, "col", swap_pairs)

    def chip_flip(x, bit):
        return lax.ppermute(x, "col", [(i, i ^ (2 << bit)) for i in range(n_col)])

    def row_flip(x, bit):
        return lax.ppermute(x, "row", [(i, i ^ (1 << bit)) for i in range(n_row)])

    def low_bit(m):
        return (m & -m).bit_length() - 1

    last = n_chip - 1
    kept = {m: [keep[m], swap(send[m])] for m in range(last, -1, -1)}
    parts = [functools.reduce(jnp.add, kept[0])]
    arrived = {m: [] for m in range(n_chip)}
    for m in range(last, 0, -1):
        if m == last:
            unit = ahead(after(kept[m][0], kept[m][0])) + kept[m][1]
        else:
            unit = functools.reduce(jnp.add, kept[m])
            if m == 2:
                unit = ahead(after(unit, parts[0]))
            unit = functools.reduce(jnp.add, [unit] + arrived[m])
        arrived[m & (m - 1)].append(chip_flip(unit, low_bit(m)))
    kept[0] = arrived[0]
    parts += kept[0]

    half = width // 2
    out_act, pulled, wkeep, wsend = pl.pallas_call(
        functools.partial(middle_kernel, n_col, len(parts), float(nodes) ** (-0.5)),
        out_shape=(
            jax.ShapeDtypeStruct((node_dev, hidden), BF16),
            jax.ShapeDtypeStruct((width, node_dev), F32),
            jax.ShapeDtypeStruct((half * hidden // EDGE, EDGE), F32),
            jax.ShapeDtypeStruct((half * hidden // EDGE, EDGE), F32),
        ),
        in_specs=[vmem] * (3 + len(parts)),
        out_specs=(vmem,) * 4,
        compiler_params=params(16),
        name="middle",
    )(deg, cotangent, weight, *parts)

    own = {0: pulled}
    for m in range(1, n_chip):
        own[m] = chip_flip(own[m & (m - 1)], low_bit(m))
    other = {m: swap(own[m]) for m in range(last)}

    wsum = after(wkeep + swap(wsend), other[2])
    moved = chip_flip(wsum, 0)
    early = [x for m in range(last) for x in (own[m], other[m])]
    late_rows = 2 * node_dev
    sofar, rest = pl.pallas_call(
        functools.partial(partial_kernel, len(early)),
        out_shape=(
            jax.ShapeDtypeStruct((width, col_nodes), F32),
            jax.ShapeDtypeStruct((late_rows, col_nodes), BF16),
        ),
        in_specs=[any_space] * (1 + len(early)),
        out_specs=(vmem, any_space),
        scratch_shapes=[
            pltpu.VMEM((len(early) * node_dev, col_nodes), BF16),
            pltpu.VMEM((len(early), width, node_dev), F32),
            pltpu.VMEM((2 * width, len(early) * node_dev), BF16),
            pltpu.SemaphoreType.DMA((len(early),)),
            pltpu.SemaphoreType.DMA((len(early),)),
            pltpu.SemaphoreType.DMA,
        ],
        compiler_params=params(BWD),
        cost_estimate=cost(row_nodes * col_nodes * width * 4, 32 << 20),
        name="backward_early",
    )(tile, *early)

    wsum = after(wsum, sofar) + moved
    own[last] = after(own[last], sofar)
    late = [own[last], swap(own[last])]
    for bit in range(1, chip_bits):
        wsum = wsum + chip_flip(wsum, bit)
    n_piece = max(1, row_bits)
    while col_nodes % (EDGE * n_piece):
        n_piece -= 1
    size = col_nodes // n_piece
    done = pl.pallas_call(
        functools.partial(last_kernel, len(late), n_piece),
        out_shape=(jax.ShapeDtypeStruct((size, width), F32),) * n_piece,
        in_specs=[vmem, any_space, any_space] + [any_space] * len(late),
        out_specs=(vmem,) * n_piece,
        scratch_shapes=[
            pltpu.VMEM((len(late) * node_dev, col_nodes), BF16),
            pltpu.VMEM((len(late), width, node_dev), F32),
            pltpu.VMEM((2 * width, len(late) * node_dev), BF16),
            pltpu.VMEM((width, col_nodes), F32),
            pltpu.SemaphoreType.DMA((len(late),)),
            pltpu.SemaphoreType.DMA,
            pltpu.SemaphoreType.DMA,
        ],
        compiler_params=params(BWD),
        name="backward_late",
    )(deg, rest, sofar, *late)

    done = list(done)
    for t in range(row_bits):
        wsum = after(wsum, done[-1 if t == 0 else 0])
        wsum = wsum + row_flip(wsum, (t + 1) % row_bits)
        done = [x + row_flip(x, (i + t) % row_bits) for i, x in enumerate(done)]
        if t == 0:
            done[-1] = after(done[-1], wsum)
    wsum = after(wsum, done[0])
    feat_grad = jnp.concatenate(done, axis=0)

    wother = swap(wsum)
    low = lax.axis_index("col") % 2 == 0
    halves = (jnp.where(low, wsum, wother), jnp.where(low, wother, wsum))
    weight_grad = jnp.concatenate(
        [jnp.concatenate([x[i:i + half] for i in range(0, x.shape[0], half)], axis=1) for x in halves],
        axis=0,
    )
    return out_act, feat_grad, weight_grad


def solution(mesh):
    n_row, n_col = mesh.shape["row"], mesh.shape["col"]
    return jax.shard_map(
        functools.partial(body, n_row, n_col),
        mesh=mesh,
        in_specs=(
            P("col", None),
            P(),
            P("row", "col", None),
            P("row", "col", None),
            P("row", "col"),
            P("row", "col", None, None, None),
            P(),
            P(("row", "col"), None),
        ),
        out_specs=(P(("row", "col"), None), P("col", None), P()),
        check_vma=False,
    )
```

```python
import functools

import jax
import jax.numpy as jnp
from jax import lax
from jax.experimental import pallas as pl
from jax.experimental.pallas import tpu as pltpu
from jax.sharding import PartitionSpec as P

F32 = jnp.float32
BF16 = jnp.bfloat16
EDGE = 128
GROUP = 16
QUARTERS = 4
AHEAD = 3
BWD = 50
ACC_BYTES = 8 << 20
GELU_C = 0.7978845608028654
GELU_K = 0.044715


def inv_column(deg_ref, start):
    row = lax.rsqrt(deg_ref[pl.ds(start, 1), :].astype(F32))
    return jnp.transpose(jnp.broadcast_to(row, (EDGE, EDGE)))


def split(value):
    hi = value.astype(BF16)
    return hi, (value - hi.astype(F32)).astype(BF16)


def across(a, b):
    return lax.dot_general(a, b, (((0,), (0,)), ((), ())), preferred_element_type=F32)


def fetch(pairs, sems):
    copies = [pltpu.make_async_copy(src, dst, sems.at[i]) for i, (src, dst) in enumerate(pairs)]
    for copy in copies:
        copy.start()
    return copies


def halve(value, size):
    if size & (size - 1) == 0:
        shift = size.bit_length() - 1
        return lax.shift_right_logical(value, shift), value & (size - 1)
    return lax.div(value, size), lax.rem(value, size)


def forward_kernel(
    n_col, chunk, panel_dev, node_dev,
    rows_hbm, cols_hbm, live_ref, deg_hbm, feat_hbm, blocks_ref, *refs,
):
    outs, tile_ref = refs[:n_col], refs[n_col]
    accs, refs = refs[n_col + 1:-12], refs[-12:]
    both, buf, scaled, result, rows_ref, cols_ref, deg_ref, feat_ref = refs[:8]
    in_sems, dense_sems, out_sems, small_sems = refs[8:]
    part = EDGE // len(accs)
    slots = buf.shape[0]
    col_nodes, width = feat_ref.shape
    col_blocks = col_nodes // EDGE
    dev_blocks = node_dev // EDGE
    panel_blocks = panel_dev * dev_blocks
    positions = panel_blocks * col_blocks
    n_panels = n_col // panel_dev
    n_chunks = slots // chunk
    me = lax.axis_index("col")
    live = live_ref[0, 0]

    def block_copy(c):
        span = pl.ds(c * chunk, chunk)
        return pltpu.make_async_copy(blocks_ref.at[0, 0, span], buf.at[span], in_sems.at[c])

    def dense_copy(rel, j):
        there = tile_ref.at[pl.ds(rel * node_dev, node_dev)]
        return pltpu.make_async_copy(both.at[j, pl.ds(0, node_dev)], there, dense_sems.at[j])

    def result_copy(rel, j):
        return pltpu.make_async_copy(result.at[j], outs[rel], out_sems.at[j])

    small = fetch(
        [(rows_hbm, rows_ref), (cols_hbm, cols_ref), (deg_hbm, deg_ref), (feat_hbm, feat_ref)],
        small_sems)
    for c in range(n_chunks):
        block_copy(c).start()

    def clear():
        @pl.loop(0, positions // 4)
        def _(p):
            for acc in accs:
                acc[pl.ds(p * 4, 4)] = jnp.zeros((4, part, EDGE), F32)

    clear()
    for copy in small:
        copy.wait()
    for k in range(col_blocks):
        inv = inv_column(deg_ref, me * col_blocks + k)
        span = pl.ds(k * EDGE, EDGE)
        scaled[span, :] = (inv * feat_ref[span, :].astype(F32)).astype(BF16)

    def add_slots(first, place):
        pending = []

        def finish():
            acc, p, sofar, block = pending.pop(0)
            acc[p] = sofar + block.astype(F32)

        for s in range(GROUP):
            p = place(first + s)
            for q, acc in enumerate(accs):
                pending.append((acc, p, acc[p], buf[first + s, q * part:(q + 1) * part, :]))
                if len(pending) > AHEAD:
                    finish()
        while pending:
            finish()

    for panel in range(n_panels):
        base = panel * panel_blocks

        if panel:
            clear()

        def place(s):
            dev, inner = halve(rows_ref[0, 0, s], dev_blocks)
            r = (dev ^ me) * dev_blocks + inner - base
            ok = s < live
            if n_panels > 1:
                ok = ok & (r >= 0) & (r < panel_blocks)
            return jnp.where(ok, r * col_blocks + cols_ref[0, 0, s], positions)

        @pl.loop(0, n_chunks)
        def _(c):
            if panel == 0:
                block_copy(c).wait()

            @pl.loop(0, chunk // GROUP)
            def _(g):
                add_slots(c * chunk + g * GROUP, place)

        for j in reversed(range(panel_dev)):
            rel = panel * panel_dev + j
            if panel:
                dense_copy(rel - panel_dev, j).wait()
                result_copy(rel - panel_dev, j).wait()
            for b in range(dev_blocks):
                for cb in range(col_blocks):
                    lanes = slice(cb * EDGE, (cb + 1) * EDGE)
                    for q, acc in enumerate(accs):
                        hi, lo = split(acc[(j * dev_blocks + b) * col_blocks + cb])
                        at = b * EDGE + q * part
                        both[j, at:at + part, lanes] = hi
                        both[j, node_dev + at:node_dev + at + part, lanes] = lo
            dense_copy(rel, j).start()
            pair = jnp.dot(both[j], scaled[...], preferred_element_type=F32)
            result[j] = pair[:node_dev] + pair[node_dev:]
            result_copy(rel, j).start()

    for j in range(panel_dev):
        rel = (n_panels - 1) * panel_dev + j
        dense_copy(rel, j).wait()
        result_copy(rel, j).wait()


def middle_kernel(n_col, n_in, scale, deg_ref, cot_ref, weight_ref, *refs):
    parts = refs[:n_in]
    act_ref, pulled_ref, keep_ref, send_ref = refs[n_in:]
    node_dev = cot_ref.shape[0]
    dev_blocks = node_dev // EDGE
    base = (lax.axis_index("row") * n_col + lax.axis_index("col")) * dev_blocks
    inv = jnp.concatenate([inv_column(deg_ref, base + k) for k in range(dev_blocks)], axis=0)
    summed = parts[0][...]
    for ref in parts[1:]:
        summed = summed + ref[...]
    propagated = inv * summed
    prop_hi, prop_lo = split(propagated)
    weight = weight_ref[...]
    pair = jnp.dot(
        jnp.concatenate([prop_hi, prop_lo], axis=0), weight, preferred_element_type=F32)
    v = pair[:node_dev] + pair[node_dev:]
    t = jnp.tanh(GELU_C * (v + GELU_K * v * v * v))
    act_ref[...] = (0.5 * v * (1.0 + t)).astype(BF16)
    slope = 0.5 * (1.0 + t) + 0.5 * v * (1.0 - t * t) * (GELU_C * (1.0 + 3.0 * GELU_K * v * v))
    gprime = cot_ref[...].astype(F32) * slope
    hi, lo = split(gprime)
    pair = lax.dot_general(
        jnp.concatenate([hi, lo], axis=0), weight, (((1,), (1,)), ((), ())),
        preferred_element_type=F32,
    )
    pulled_ref[...] = jnp.transpose(inv * (pair[:node_dev] + pair[node_dev:]))
    pair = across(jnp.concatenate([prop_hi, prop_lo], axis=1), hi)
    part = scale * (pair[:EDGE] + (pair[EDGE:] + across(prop_hi, lo)))
    half = EDGE // 2
    low = lax.axis_index("col") % 2 == 0
    for n in range(0, part.shape[1], EDGE):
        upper, lower = part[:half, n:n + EDGE], part[half:, n:n + EDGE]
        rows = pl.ds(n // EDGE * half, half)
        keep_ref[rows, :] = jnp.where(low, upper, lower)
        send_ref[rows, :] = jnp.where(low, lower, upper)


def load_lhs(stage, lhs, copies):
    width, node_dev = stage.shape[1:]
    for i in range(len(copies)):
        copies[i].wait()
        hi, lo = split(stage[i])
        lhs[:width, i * node_dev:(i + 1) * node_dev] = hi
        lhs[width:, i * node_dev:(i + 1) * node_dev] = lo


def partial_kernel(n_in, tile_ref, *refs):
    parts = refs[:n_in]
    out_ref, rest_ref, dense, stage, lhs, sems, dense_sems, rest_sem = refs[n_in:]
    width, node_dev = stage.shape[1:]
    col_nodes = dense.shape[1]
    blocks = fetch(
        [(tile_ref.at[span], dense.at[span]) for span in (
            pl.ds(i * node_dev, node_dev) for i in range(n_in))], dense_sems)
    copies = fetch([(r, stage.at[i]) for i, r in enumerate(parts)], sems)
    rest = pltpu.make_async_copy(
        tile_ref.at[pl.ds(n_in * node_dev, rest_ref.shape[0])], rest_ref, rest_sem)
    rest.start()
    load_lhs(stage, lhs, copies)
    for copy in blocks:
        copy.wait()
    step = 2 * EDGE if col_nodes % (2 * EDGE) == 0 else EDGE
    for n in range(0, col_nodes, step):
        pair = jnp.dot(lhs[...], dense[:, n:n + step], preferred_element_type=F32)
        out_ref[:, n:n + step] = pair[:width] + pair[width:]
    rest.wait()


def last_kernel(n_in, n_out, deg_ref, dense_ref, sofar_ref, *refs):
    parts, outs = refs[:n_in], refs[n_in:n_in + n_out]
    dense, stage, lhs, sofar, sems, dense_sem, sofar_sem = refs[n_in + n_out:]
    width, node_dev = parts[0].shape
    col_nodes = dense.shape[1]
    block = pltpu.make_async_copy(dense_ref, dense, dense_sem)
    before = pltpu.make_async_copy(sofar_ref, sofar, sofar_sem)
    block.start()
    size = col_nodes // n_out
    copies = fetch([(r, stage.at[i]) for i, r in enumerate(parts)], sems)
    before.start()
    load_lhs(stage, lhs, copies)
    block.wait()
    before.wait()
    step = 2 * EDGE if col_nodes % (2 * EDGE) == 0 else EDGE
    first = lax.axis_index("col") * (col_nodes // EDGE)
    for n in range(0, col_nodes, step):
        pair = jnp.dot(lhs[...], dense[:, n:n + step], preferred_element_type=F32)
        total = sofar[:, n:n + step] + (pair[:width] + pair[width:])
        for at in range(n, n + step, EDGE):
            inv = inv_column(deg_ref, first + at // EDGE)
            out = outs[at // size]
            out[at % size:at % size + EDGE, :] = inv * jnp.transpose(total[:, at - n:at - n + EDGE])


def body(n_row, n_col, features, degrees, block_rows, block_cols, live_slots, blocks, weight, cotangent):
    n_chip = n_col // 2
    chip_bits, row_bits = n_chip.bit_length() - 1, n_row.bit_length() - 1
    assert n_col == 2 << chip_bits and n_row == 1 << row_bits
    node_dev, hidden = cotangent.shape
    col_nodes, width = features.shape
    row_nodes = node_dev * n_col
    nodes = col_nodes * n_col
    slots = blocks.shape[2]
    deg = degrees.reshape(nodes // EDGE, EDGE)
    col_blocks = col_nodes // EDGE
    dev_blocks = node_dev // EDGE
    assert n_chip >= 4
    chunk = 16
    panel_dev = n_col
    while panel_dev % 2 == 0 and panel_dev * node_dev * col_nodes * 4 > ACC_BYTES:
        panel_dev //= 2
    positions = panel_dev * dev_blocks * col_blocks
    smem = pl.BlockSpec(memory_space=pltpu.SMEM)
    any_space = pl.BlockSpec(memory_space=pl.ANY)
    vmem = pl.BlockSpec(memory_space=pltpu.VMEM)

    def params(mib):
        return pltpu.CompilerParams(vmem_limit_bytes=mib << 20)

    def after(x, other):
        corner = 0.0 * other[:8, :EDGE]
        if x.shape[0] == other.shape[0] and x.shape[1] <= other.shape[1]:
            return x + 0.0 * other[:, :x.shape[1]]
        return (x.reshape(-1, 8, EDGE) + corner).reshape(x.shape)

    def ahead(x):
        return lax.optimization_barrier(x)

    def cost(flops, read):
        return pl.CostEstimate(flops=flops, bytes_accessed=read, transcendentals=0)

    *pieces, tile = pl.pallas_call(
        functools.partial(forward_kernel, n_col, chunk, panel_dev, node_dev),
        out_shape=[jax.ShapeDtypeStruct((node_dev, width), F32)] * n_col
        + [jax.ShapeDtypeStruct((row_nodes, col_nodes), BF16)],
        in_specs=[any_space, any_space, smem, any_space, any_space, any_space],
        out_specs=[any_space] * (n_col + 1),
        scratch_shapes=[
            pltpu.VMEM((positions + 1, EDGE // QUARTERS, EDGE), F32) for _ in range(QUARTERS)
        ] + [
            pltpu.VMEM((panel_dev, 2 * node_dev, col_nodes), BF16),
            pltpu.VMEM((slots, EDGE, EDGE), BF16),
            pltpu.VMEM((col_nodes, width), BF16),
            pltpu.VMEM((panel_dev, node_dev, width), F32),
            pltpu.SMEM(block_rows.shape, jnp.int32),
            pltpu.SMEM(block_cols.shape, jnp.int32),
            pltpu.VMEM(deg.shape, jnp.int32),
            pltpu.VMEM(features.shape, BF16),
            pltpu.SemaphoreType.DMA((slots // chunk,)),
            pltpu.SemaphoreType.DMA((panel_dev,)),
            pltpu.SemaphoreType.DMA((panel_dev,)),
            pltpu.SemaphoreType.DMA((4,)),
        ],
        compiler_params=params(54),
        name="densify_forward",
    )(block_rows, block_cols, live_slots, deg, features, blocks)
    keep, send = pieces[0::2], pieces[1::2]

    swap_pairs = [(i, i ^ 1) for i in range(n_col)]

    def swap(x):
        return lax.ppermute(x, "col", swap_pairs)

    def chip_flip(x, bit):
        return lax.ppermute(x, "col", [(i, i ^ (2 << bit)) for i in range(n_col)])

    def row_flip(x, bit):
        return lax.ppermute(x, "row", [(i, i ^ (1 << bit)) for i in range(n_row)])

    def low_bit(m):
        return (m & -m).bit_length() - 1

    last = n_chip - 1
    kept = {m: [keep[m], swap(send[m])] for m in range(last, -1, -1)}
    parts = [functools.reduce(jnp.add, kept[0])]
    arrived = {m: [] for m in range(n_chip)}
    for m in range(last, 0, -1):
        if m == last:
            unit = ahead(after(kept[m][0], kept[m][0])) + kept[m][1]
        else:
            unit = functools.reduce(jnp.add, kept[m])
            if m == 2:
                unit = ahead(after(unit, parts[0]))
            unit = functools.reduce(jnp.add, [unit] + arrived[m])
        arrived[m & (m - 1)].append(chip_flip(unit, low_bit(m)))
    kept[0] = arrived[0]
    parts += kept[0]

    half = width // 2
    out_act, pulled, wkeep, wsend = pl.pallas_call(
        functools.partial(middle_kernel, n_col, len(parts), float(nodes) ** (-0.5)),
        out_shape=(
            jax.ShapeDtypeStruct((node_dev, hidden), BF16),
            jax.ShapeDtypeStruct((width, node_dev), F32),
            jax.ShapeDtypeStruct((half * hidden // EDGE, EDGE), F32),
            jax.ShapeDtypeStruct((half * hidden // EDGE, EDGE), F32),
        ),
        in_specs=[vmem] * (3 + len(parts)),
        out_specs=(vmem,) * 4,
        compiler_params=params(16),
        name="middle",
    )(deg, cotangent, weight, *parts)

    own = {0: pulled}
    for m in range(1, n_chip):
        own[m] = chip_flip(own[m & (m - 1)], low_bit(m))
    own[1] = after(own[1], own[2])
    other = {m: swap(own[m]) for m in range(last)}

    wsum = wkeep + swap(wsend)
    wsum = wsum + chip_flip(wsum, 0)
    early = [x for m in range(last) for x in (own[m], other[m])]
    late_rows = 2 * node_dev
    sofar, rest = pl.pallas_call(
        functools.partial(partial_kernel, len(early)),
        out_shape=(
            jax.ShapeDtypeStruct((width, col_nodes), F32),
            jax.ShapeDtypeStruct((late_rows, col_nodes), BF16),
        ),
        in_specs=[any_space] * (1 + len(early)),
        out_specs=(vmem, any_space),
        scratch_shapes=[
            pltpu.VMEM((len(early) * node_dev, col_nodes), BF16),
            pltpu.VMEM((len(early), width, node_dev), F32),
            pltpu.VMEM((2 * width, len(early) * node_dev), BF16),
            pltpu.SemaphoreType.DMA((len(early),)),
            pltpu.SemaphoreType.DMA((len(early),)),
            pltpu.SemaphoreType.DMA,
        ],
        compiler_params=params(BWD),
        cost_estimate=cost(row_nodes * col_nodes * width * 4, 32 << 20),
        name="backward_early",
    )(tile, *early)

    own[last] = after(after(own[last], sofar), wsum)
    late = [own[last], swap(own[last])]
    for bit in range(1, chip_bits):
        wsum = wsum + chip_flip(wsum, bit)
    n_piece = max(1, row_bits)
    while col_nodes % (EDGE * n_piece):
        n_piece -= 1
    size = col_nodes // n_piece
    done = pl.pallas_call(
        functools.partial(last_kernel, len(late), n_piece),
        out_shape=(jax.ShapeDtypeStruct((size, width), F32),) * n_piece,
        in_specs=[vmem, any_space, any_space] + [any_space] * len(late),
        out_specs=(vmem,) * n_piece,
        scratch_shapes=[
            pltpu.VMEM((len(late) * node_dev, col_nodes), BF16),
            pltpu.VMEM((len(late), width, node_dev), F32),
            pltpu.VMEM((2 * width, len(late) * node_dev), BF16),
            pltpu.VMEM((width, col_nodes), F32),
            pltpu.SemaphoreType.DMA((len(late),)),
            pltpu.SemaphoreType.DMA,
            pltpu.SemaphoreType.DMA,
        ],
        compiler_params=params(BWD),
        name="backward_late",
    )(deg, rest, sofar, *late)

    done = list(done)
    for t in range(row_bits):
        wsum = after(wsum, done[0])
        wsum = wsum + row_flip(wsum, t)
        done = [x + row_flip(x, (i + t) % row_bits) for i, x in enumerate(done)]
        if t == 0:
            done[-1] = after(done[-1], wsum)
    wsum = after(wsum, done[0])
    feat_grad = jnp.concatenate(done, axis=0)

    wother = swap(wsum)
    low = lax.axis_index("col") % 2 == 0
    halves = (jnp.where(low, wsum, wother), jnp.where(low, wother, wsum))
    weight_grad = jnp.concatenate(
        [jnp.concatenate([x[i:i + half] for i in range(0, x.shape[0], half)], axis=1) for x in halves],
        axis=0,
    )
    return out_act, feat_grad, weight_grad


def solution(mesh):
    n_row, n_col = mesh.shape["row"], mesh.shape["col"]
    return jax.shard_map(
        functools.partial(body, n_row, n_col),
        mesh=mesh,
        in_specs=(
            P("col", None),
            P(),
            P("row", "col", None),
            P("row", "col", None),
            P("row", "col"),
            P("row", "col", None, None, None),
            P(),
            P(("row", "col"), None),
        ),
        out_specs=(P(("row", "col"), None), P("col", None), P()),
        check_vma=False,
    )
```

```python
import functools

import jax
import jax.numpy as jnp
from jax import lax
from jax.experimental import pallas as pl
from jax.experimental.pallas import tpu as pltpu
from jax.sharding import PartitionSpec as P

F32 = jnp.float32
BF16 = jnp.bfloat16
EDGE = 128
GROUP = 16
QUARTERS = 4
AHEAD = 3
DEPTH = 2
BWD = 50
ACC_BYTES = 8 << 20
GELU_C = 0.7978845608028654
GELU_K = 0.044715


def inv_column(deg_ref, start):
    row = lax.rsqrt(deg_ref[pl.ds(start, 1), :].astype(F32))
    return jnp.transpose(jnp.broadcast_to(row, (EDGE, EDGE)))


def split(value):
    hi = value.astype(BF16)
    return hi, (value - hi.astype(F32)).astype(BF16)


def across(a, b):
    return lax.dot_general(a, b, (((0,), (0,)), ((), ())), preferred_element_type=F32)


def fetch(pairs, sems):
    copies = [pltpu.make_async_copy(src, dst, sems.at[i]) for i, (src, dst) in enumerate(pairs)]
    for copy in copies:
        copy.start()
    return copies


def halve(value, size):
    if size & (size - 1) == 0:
        shift = size.bit_length() - 1
        return lax.shift_right_logical(value, shift), value & (size - 1)
    return lax.div(value, size), lax.rem(value, size)


def product_kernel(
    n_col, chunk, rows_ref, cols_ref, live_ref, deg_ref, feat_ref, blocks_ref, *refs,
):
    outs, (acc, buf, scaled, in_sems, out_sems) = refs[:n_col], refs[n_col:]
    slots = buf.shape[0]
    col_blocks = feat_ref.shape[0] // EDGE
    dev_blocks = outs[0].shape[0]
    row_blocks = n_col * dev_blocks
    part = EDGE // QUARTERS
    n_chunks = slots // chunk
    me = lax.axis_index("col")
    live = live_ref[0, 0]

    def block_copy(c):
        span = pl.ds(c * chunk, chunk)
        return pltpu.make_async_copy(blocks_ref.at[0, 0, span], buf.at[span], in_sems.at[c])

    for c in range(n_chunks):
        block_copy(c).start()
    for k in range(col_blocks):
        inv = inv_column(deg_ref, me * col_blocks + k)
        span = pl.ds(k * EDGE, EDGE)
        scaled[span, :] = (inv * feat_ref[span, :].astype(F32)).astype(BF16)

    @pl.loop(0, row_blocks)
    def _(p):
        acc[p] = jnp.zeros((EDGE, EDGE), F32)

    def product(s):
        dev, inner = halve(rows_ref[0, 0, s], dev_blocks)
        p = jnp.where(s < live, (dev ^ me) * dev_blocks + inner, row_blocks)
        at = pl.multiple_of(cols_ref[0, 0, s] * EDGE, EDGE)
        return p, jnp.dot(buf[s], scaled[pl.ds(at, EDGE), :], preferred_element_type=F32)

    def add_slots(first):
        products, pending = [], []

        def finish():
            p, rows, sofar, value = pending.pop(0)
            acc[p, rows, :] = sofar + value

        for s in range(GROUP + DEPTH):
            if s < GROUP:
                products.append(product(first + s))
            if s >= DEPTH:
                p, value = products.pop(0)
                for q in range(QUARTERS):
                    rows = slice(q * part, (q + 1) * part)
                    pending.append((p, rows, acc[p, rows, :], value[rows]))
                    if len(pending) > AHEAD:
                        finish()
        while pending:
            finish()

    @pl.loop(0, n_chunks)
    def _(c):
        block_copy(c).wait()

        @pl.loop(0, chunk // GROUP)
        def _(g):
            add_slots(c * chunk + g * GROUP)

    copies = [
        pltpu.make_async_copy(acc.at[pl.ds(j * dev_blocks, dev_blocks)], outs[j], out_sems.at[j])
        for j in range(n_col)
    ]
    for copy in copies:
        copy.start()
    for copy in copies:
        copy.wait()


def densify_kernel(
    n_col, chunk, panel_dev, node_dev,
    rows_ref, cols_ref, live_ref, blocks_ref, tile_ref, mark_ref, *refs,
):
    mark_ref[...] = jnp.zeros(mark_ref.shape, F32)
    accs, (both, buf, in_sems, dense_sems) = refs[:-4], refs[-4:]
    part = EDGE // len(accs)
    slots = buf.shape[0]
    col_blocks = tile_ref.shape[1] // EDGE
    dev_blocks = node_dev // EDGE
    panel_blocks = panel_dev * dev_blocks
    positions = panel_blocks * col_blocks
    n_panels = n_col // panel_dev
    n_chunks = slots // chunk
    me = lax.axis_index("col")
    live = live_ref[0, 0]

    def block_copy(c):
        span = pl.ds(c * chunk, chunk)
        return pltpu.make_async_copy(blocks_ref.at[0, 0, span], buf.at[span], in_sems.at[c])

    def dense_copy(rel, j):
        there = tile_ref.at[pl.ds(rel * node_dev, node_dev)]
        return pltpu.make_async_copy(both.at[j], there, dense_sems.at[j])

    for c in range(n_chunks):
        block_copy(c).start()

    def add_slots(first, place):
        pending = []

        def finish():
            acc, p, sofar, block = pending.pop(0)
            acc[p] = sofar + block.astype(F32)

        for s in range(GROUP):
            p = place(first + s)
            for q, acc in enumerate(accs):
                pending.append((acc, p, acc[p], buf[first + s, q * part:(q + 1) * part, :]))
                if len(pending) > AHEAD:
                    finish()
        while pending:
            finish()

    for panel in range(n_panels):
        base = panel * panel_blocks

        @pl.loop(0, positions)
        def _(p):
            for acc in accs:
                acc[p] = jnp.zeros((part, EDGE), F32)

        def place(s):
            dev, inner = halve(rows_ref[0, 0, s], dev_blocks)
            r = (dev ^ me) * dev_blocks + inner - base
            ok = s < live
            if n_panels > 1:
                ok = ok & (r >= 0) & (r < panel_blocks)
            return jnp.where(ok, r * col_blocks + cols_ref[0, 0, s], positions)

        @pl.loop(0, n_chunks)
        def _(c):
            if panel == 0:
                block_copy(c).wait()

            @pl.loop(0, chunk // GROUP)
            def _(g):
                add_slots(c * chunk + g * GROUP, place)

        for j in reversed(range(panel_dev)):
            rel = panel * panel_dev + j
            if panel:
                dense_copy(rel - panel_dev, j).wait()
            for b in range(dev_blocks):
                for cb in range(col_blocks):
                    lanes = slice(cb * EDGE, (cb + 1) * EDGE)
                    for q, acc in enumerate(accs):
                        at = b * EDGE + q * part
                        total = acc[(j * dev_blocks + b) * col_blocks + cb]
                        both[j, at:at + part, lanes] = total.astype(BF16)
            dense_copy(rel, j).start()

    for j in range(panel_dev):
        rel = (n_panels - 1) * panel_dev + j
        dense_copy(rel, j).wait()


def middle_kernel(n_col, n_in, scale, deg_ref, cot_ref, weight_ref, *refs):
    parts = refs[:n_in]
    act_ref, pulled_ref, keep_ref, send_ref = refs[n_in + 1:]
    node_dev = cot_ref.shape[0]
    dev_blocks = node_dev // EDGE
    base = (lax.axis_index("row") * n_col + lax.axis_index("col")) * dev_blocks
    inv = jnp.concatenate([inv_column(deg_ref, base + k) for k in range(dev_blocks)], axis=0)
    summed = parts[0][...]
    for ref in parts[1:]:
        summed = summed + ref[...]
    propagated = inv * summed
    prop_hi, prop_lo = split(propagated)
    weight = weight_ref[...]
    pair = jnp.dot(
        jnp.concatenate([prop_hi, prop_lo], axis=0), weight, preferred_element_type=F32)
    v = pair[:node_dev] + pair[node_dev:]
    t = jnp.tanh(GELU_C * (v + GELU_K * v * v * v))
    act_ref[...] = (0.5 * v * (1.0 + t)).astype(BF16)
    slope = 0.5 * (1.0 + t) + 0.5 * v * (1.0 - t * t) * (GELU_C * (1.0 + 3.0 * GELU_K * v * v))
    gprime = cot_ref[...].astype(F32) * slope
    hi, lo = split(gprime)
    pair = lax.dot_general(
        jnp.concatenate([hi, lo], axis=0), weight, (((1,), (1,)), ((), ())),
        preferred_element_type=F32,
    )
    pulled_ref[...] = jnp.transpose(inv * (pair[:node_dev] + pair[node_dev:]))
    pair = across(jnp.concatenate([prop_hi, prop_lo], axis=1), hi)
    part = scale * (pair[:EDGE] + (pair[EDGE:] + across(prop_hi, lo)))
    half = EDGE // 2
    low = lax.axis_index("col") % 2 == 0
    for n in range(0, part.shape[1], EDGE):
        upper, lower = part[:half, n:n + EDGE], part[half:, n:n + EDGE]
        rows = pl.ds(n // EDGE * half, half)
        keep_ref[rows, :] = jnp.where(low, upper, lower)
        send_ref[rows, :] = jnp.where(low, lower, upper)


def load_lhs(stage, lhs, copies):
    width, node_dev = stage.shape[1:]
    for i in range(len(copies)):
        copies[i].wait()
        hi, lo = split(stage[i])
        lhs[:width, i * node_dev:(i + 1) * node_dev] = hi
        lhs[width:, i * node_dev:(i + 1) * node_dev] = lo


def partial_kernel(n_in, tile_ref, *refs):
    parts = refs[:n_in]
    out_ref, rest_ref, dense, stage, lhs, sems, dense_sems, rest_sem = refs[n_in:]
    width, node_dev = stage.shape[1:]
    col_nodes = dense.shape[1]
    blocks = fetch(
        [(tile_ref.at[span], dense.at[span]) for span in (
            pl.ds(i * node_dev, node_dev) for i in range(n_in))], dense_sems)
    copies = fetch([(r, stage.at[i]) for i, r in enumerate(parts)], sems)
    rest = pltpu.make_async_copy(
        tile_ref.at[pl.ds(n_in * node_dev, rest_ref.shape[0])], rest_ref, rest_sem)
    rest.start()
    load_lhs(stage, lhs, copies)
    for copy in blocks:
        copy.wait()
    step = 2 * EDGE if col_nodes % (2 * EDGE) == 0 else EDGE
    for n in range(0, col_nodes, step):
        pair = jnp.dot(lhs[...], dense[:, n:n + step], preferred_element_type=F32)
        out_ref[:, n:n + step] = pair[:width] + pair[width:]
    rest.wait()


def last_kernel(n_in, n_out, deg_ref, dense_ref, sofar_ref, *refs):
    parts, outs = refs[:n_in], refs[n_in:n_in + n_out]
    dense, stage, lhs, sofar, sems, dense_sem, sofar_sem = refs[n_in + n_out:]
    width, node_dev = parts[0].shape
    col_nodes = dense.shape[1]
    block = pltpu.make_async_copy(dense_ref, dense, dense_sem)
    before = pltpu.make_async_copy(sofar_ref, sofar, sofar_sem)
    block.start()
    size = col_nodes // n_out
    copies = fetch([(r, stage.at[i]) for i, r in enumerate(parts)], sems)
    before.start()
    load_lhs(stage, lhs, copies)
    block.wait()
    before.wait()
    step = 2 * EDGE if col_nodes % (2 * EDGE) == 0 else EDGE
    first = lax.axis_index("col") * (col_nodes // EDGE)
    for n in range(0, col_nodes, step):
        pair = jnp.dot(lhs[...], dense[:, n:n + step], preferred_element_type=F32)
        total = sofar[:, n:n + step] + (pair[:width] + pair[width:])
        for at in range(n, n + step, EDGE):
            inv = inv_column(deg_ref, first + at // EDGE)
            out = outs[at // size]
            out[at % size:at % size + EDGE, :] = inv * jnp.transpose(total[:, at - n:at - n + EDGE])


def body(n_row, n_col, features, degrees, block_rows, block_cols, live_slots, blocks, weight, cotangent):
    n_chip = n_col // 2
    chip_bits, row_bits = n_chip.bit_length() - 1, n_row.bit_length() - 1
    assert n_col == 2 << chip_bits and n_row == 1 << row_bits
    node_dev, hidden = cotangent.shape
    col_nodes, width = features.shape
    row_nodes = node_dev * n_col
    nodes = col_nodes * n_col
    slots = blocks.shape[2]
    deg = degrees.reshape(nodes // EDGE, EDGE)
    col_blocks = col_nodes // EDGE
    dev_blocks = node_dev // EDGE
    assert n_chip >= 4
    chunk = 16
    panel_dev = n_col
    while panel_dev % 2 == 0 and panel_dev * node_dev * col_nodes * 4 > ACC_BYTES:
        panel_dev //= 2
    positions = panel_dev * dev_blocks * col_blocks
    smem = pl.BlockSpec(memory_space=pltpu.SMEM)
    any_space = pl.BlockSpec(memory_space=pl.ANY)
    vmem = pl.BlockSpec(memory_space=pltpu.VMEM)

    def params(mib):
        return pltpu.CompilerParams(vmem_limit_bytes=mib << 20)

    def after(x, other):
        corner = 0.0 * other[:8, :EDGE]
        if x.shape[0] == other.shape[0] and x.shape[1] <= other.shape[1]:
            return x + 0.0 * other[:, :x.shape[1]]
        return (x.reshape(-1, 8, EDGE) + corner).reshape(x.shape)

    def ahead(x):
        return lax.optimization_barrier(x)

    def cost(flops, read):
        return pl.CostEstimate(flops=flops, bytes_accessed=read, transcendentals=0)

    pieces = pl.pallas_call(
        functools.partial(product_kernel, n_col, chunk),
        out_shape=[jax.ShapeDtypeStruct((dev_blocks, EDGE, width), F32)] * n_col,
        in_specs=[smem, smem, smem, vmem, vmem, any_space],
        out_specs=[any_space] * n_col,
        scratch_shapes=[
            pltpu.VMEM((n_col * dev_blocks + 1, EDGE, width), F32),
            pltpu.VMEM((slots, EDGE, EDGE), BF16),
            pltpu.VMEM((col_nodes, width), BF16),
            pltpu.SemaphoreType.DMA((slots // chunk,)),
            pltpu.SemaphoreType.DMA((n_col,)),
        ],
        compiler_params=params(54),
        name="product",
    )(block_rows, block_cols, live_slots, deg, features, blocks)
    pieces = [x.reshape(node_dev, width) for x in pieces]
    keep, send = pieces[0::2], pieces[1::2]

    tile, mark = pl.pallas_call(
        functools.partial(densify_kernel, n_col, chunk, panel_dev, node_dev),
        out_shape=(
            jax.ShapeDtypeStruct((row_nodes, col_nodes), BF16),
            jax.ShapeDtypeStruct((8, EDGE), F32),
        ),
        in_specs=[smem, smem, smem, any_space],
        out_specs=(any_space, vmem),
        scratch_shapes=[
            pltpu.VMEM((positions + 1, EDGE // QUARTERS, EDGE), F32) for _ in range(QUARTERS)
        ] + [
            pltpu.VMEM((panel_dev, node_dev, col_nodes), BF16),
            pltpu.VMEM((slots, EDGE, EDGE), BF16),
            pltpu.SemaphoreType.DMA((slots // chunk,)),
            pltpu.SemaphoreType.DMA((panel_dev,)),
        ],
        compiler_params=params(52),
        cost_estimate=cost(0, 40 << 20),
        name="densify",
    )(block_rows, block_cols, live_slots, blocks)

    swap_pairs = [(i, i ^ 1) for i in range(n_col)]

    def swap(x):
        return lax.ppermute(x, "col", swap_pairs)

    def chip_flip(x, bit):
        return lax.ppermute(x, "col", [(i, i ^ (2 << bit)) for i in range(n_col)])

    def row_flip(x, bit):
        return lax.ppermute(x, "row", [(i, i ^ (1 << bit)) for i in range(n_row)])

    def low_bit(m):
        return (m & -m).bit_length() - 1

    last = n_chip - 1
    kept = {m: [keep[m], swap(send[m])] for m in range(last, -1, -1)}
    parts = [functools.reduce(jnp.add, kept[0])]
    arrived = {m: [] for m in range(n_chip)}
    for m in range(last, 0, -1):
        if m == last:
            unit = first = ahead(after(kept[m][0], kept[m][0])) + kept[m][1]
        else:
            unit = functools.reduce(jnp.add, kept[m])
            if m == 2:
                unit = ahead(after(after(unit, parts[0]), first))
            unit = functools.reduce(jnp.add, [unit] + arrived[m])
        arrived[m & (m - 1)].append(chip_flip(unit, low_bit(m)))
    kept[0] = arrived[0]
    parts += kept[0]

    half = width // 2
    out_act, pulled, wkeep, wsend = pl.pallas_call(
        functools.partial(middle_kernel, n_col, len(parts), float(nodes) ** (-0.5)),
        out_shape=(
            jax.ShapeDtypeStruct((node_dev, hidden), BF16),
            jax.ShapeDtypeStruct((width, node_dev), F32),
            jax.ShapeDtypeStruct((half * hidden // EDGE, EDGE), F32),
            jax.ShapeDtypeStruct((half * hidden // EDGE, EDGE), F32),
        ),
        in_specs=[vmem] * (3 + len(parts)) + [any_space],
        out_specs=(vmem,) * 4,
        compiler_params=params(16),
        name="middle",
    )(deg, cotangent, weight, *parts, mark)

    own = {0: pulled}
    for m in range(1, n_chip):
        own[m] = chip_flip(own[m & (m - 1)], low_bit(m))
    own[1] = after(own[1], own[2])
    other = {m: swap(own[m]) for m in range(last)}

    wsum = wkeep + swap(wsend)
    wsum = wsum + chip_flip(wsum, 0)
    early = [x for m in range(last) for x in (own[m], other[m])]
    late_rows = 2 * node_dev
    sofar, rest = pl.pallas_call(
        functools.partial(partial_kernel, len(early)),
        out_shape=(
            jax.ShapeDtypeStruct((width, col_nodes), F32),
            jax.ShapeDtypeStruct((late_rows, col_nodes), BF16),
        ),
        in_specs=[any_space] * (1 + len(early)),
        out_specs=(vmem, any_space),
        scratch_shapes=[
            pltpu.VMEM((len(early) * node_dev, col_nodes), BF16),
            pltpu.VMEM((len(early), width, node_dev), F32),
            pltpu.VMEM((2 * width, len(early) * node_dev), BF16),
            pltpu.SemaphoreType.DMA((len(early),)),
            pltpu.SemaphoreType.DMA((len(early),)),
            pltpu.SemaphoreType.DMA,
        ],
        compiler_params=params(BWD),
        cost_estimate=cost(row_nodes * col_nodes * width * 4, 32 << 20),
        name="backward_early",
    )(tile, *early)

    own[last] = after(after(own[last], sofar), wsum)
    late = [own[last], swap(own[last])]
    for bit in range(1, chip_bits):
        wsum = wsum + chip_flip(wsum, bit)
    n_piece = max(1, row_bits)
    while col_nodes % (EDGE * n_piece):
        n_piece -= 1
    size = col_nodes // n_piece
    done = pl.pallas_call(
        functools.partial(last_kernel, len(late), n_piece),
        out_shape=(jax.ShapeDtypeStruct((size, width), F32),) * n_piece,
        in_specs=[vmem, any_space, any_space] + [any_space] * len(late),
        out_specs=(vmem,) * n_piece,
        scratch_shapes=[
            pltpu.VMEM((len(late) * node_dev, col_nodes), BF16),
            pltpu.VMEM((len(late), width, node_dev), F32),
            pltpu.VMEM((2 * width, len(late) * node_dev), BF16),
            pltpu.VMEM((width, col_nodes), F32),
            pltpu.SemaphoreType.DMA((len(late),)),
            pltpu.SemaphoreType.DMA,
            pltpu.SemaphoreType.DMA,
        ],
        compiler_params=params(BWD),
        name="backward_late",
    )(deg, rest, sofar, *late)

    done = list(done)
    for t in range(row_bits):
        wsum = after(wsum, done[0])
        wsum = wsum + row_flip(wsum, t)
        done = [x + row_flip(x, (i + t) % row_bits) for i, x in enumerate(done)]
        if t == 0:
            done[-1] = after(done[-1], wsum)
    wsum = after(wsum, done[0])
    feat_grad = jnp.concatenate(done, axis=0)

    wother = swap(wsum)
    low = lax.axis_index("col") % 2 == 0
    halves = (jnp.where(low, wsum, wother), jnp.where(low, wother, wsum))
    weight_grad = jnp.concatenate(
        [jnp.concatenate([x[i:i + half] for i in range(0, x.shape[0], half)], axis=1) for x in halves],
        axis=0,
    )
    return out_act, feat_grad, weight_grad


def solution(mesh):
    n_row, n_col = mesh.shape["row"], mesh.shape["col"]
    return jax.shard_map(
        functools.partial(body, n_row, n_col),
        mesh=mesh,
        in_specs=(
            P("col", None),
            P(),
            P("row", "col", None),
            P("row", "col", None),
            P("row", "col"),
            P("row", "col", None, None, None),
            P(),
            P(("row", "col"), None),
        ),
        out_specs=(P(("row", "col"), None), P("col", None), P()),
        check_vma=False,
    )
```

```python
import functools

import jax
import jax.numpy as jnp
from jax import lax
from jax.experimental import pallas as pl
from jax.experimental.pallas import tpu as pltpu
from jax.sharding import PartitionSpec as P

F32 = jnp.float32
BF16 = jnp.bfloat16
EDGE = 128
GROUP = 16
QUARTERS = 4
AHEAD = 3
BWD = 50
ACC_BYTES = 8 << 20
GELU_C = 0.7978845608028654
GELU_K = 0.044715


def inv_column(deg_ref, start):
    row = lax.rsqrt(deg_ref[pl.ds(start, 1), :].astype(F32))
    return jnp.transpose(jnp.broadcast_to(row, (EDGE, EDGE)))


def split(value):
    hi = value.astype(BF16)
    return hi, (value - hi.astype(F32)).astype(BF16)


def across(a, b):
    return lax.dot_general(a, b, (((0,), (0,)), ((), ())), preferred_element_type=F32)


def fetch(pairs, sems):
    copies = [pltpu.make_async_copy(src, dst, sems.at[i]) for i, (src, dst) in enumerate(pairs)]
    for copy in copies:
        copy.start()
    return copies


def halve(value, size):
    if size & (size - 1) == 0:
        shift = size.bit_length() - 1
        return lax.shift_right_logical(value, shift), value & (size - 1)
    return lax.div(value, size), lax.rem(value, size)


def forward_kernel(
    n_col, chunk, panel_dev, node_dev,
    rows_ref, cols_ref, live_ref, deg_ref, feat_ref, blocks_ref, *refs,
):
    outs, tile_ref = refs[:n_col], refs[n_col]
    accs, (both, buf, scaled, result, in_sems, dense_sems, out_sems) = refs[n_col + 1:-7], refs[-7:]
    part = EDGE // len(accs)
    slots = buf.shape[0]
    col_nodes, width = feat_ref.shape
    col_blocks = col_nodes // EDGE
    dev_blocks = node_dev // EDGE
    panel_blocks = panel_dev * dev_blocks
    positions = panel_blocks * col_blocks
    n_panels = n_col // panel_dev
    n_chunks = slots // chunk
    me = lax.axis_index("col")
    live = live_ref[0, 0]

    def block_copy(c):
        span = pl.ds(c * chunk, chunk)
        return pltpu.make_async_copy(blocks_ref.at[0, 0, span], buf.at[span], in_sems.at[c])

    def dense_copy(rel, j):
        there = tile_ref.at[pl.ds(rel * node_dev, node_dev)]
        return pltpu.make_async_copy(both.at[j, pl.ds(0, node_dev)], there, dense_sems.at[j])

    def result_copy(rel, j):
        return pltpu.make_async_copy(result.at[j], outs[rel], out_sems.at[j])

    for c in range(n_chunks):
        block_copy(c).start()

    for k in range(col_blocks):
        inv = inv_column(deg_ref, me * col_blocks + k)
        span = pl.ds(k * EDGE, EDGE)
        scaled[span, :] = (inv * feat_ref[span, :].astype(F32)).astype(BF16)

    def add_slots(first, place):
        pending = []

        def finish():
            acc, p, sofar, block = pending.pop(0)
            acc[p] = sofar + block.astype(F32)

        for s in range(GROUP):
            p = place(first + s)
            for q, acc in enumerate(accs):
                pending.append((acc, p, acc[p], buf[first + s, q * part:(q + 1) * part, :]))
                if len(pending) > AHEAD:
                    finish()
        while pending:
            finish()

    for panel in range(n_panels):
        base = panel * panel_blocks

        @pl.loop(0, positions // 4)
        def _(p):
            for acc in accs:
                acc[pl.ds(p * 4, 4)] = jnp.zeros((4, part, EDGE), F32)

        def place(s):
            dev, inner = halve(rows_ref[0, 0, s], dev_blocks)
            r = (dev ^ me) * dev_blocks + inner - base
            ok = s < live
            if n_panels > 1:
                ok = ok & (r >= 0) & (r < panel_blocks)
            return jnp.where(ok, r * col_blocks + cols_ref[0, 0, s], positions)

        @pl.loop(0, n_chunks)
        def _(c):
            if panel == 0:
                block_copy(c).wait()

            @pl.loop(0, chunk // GROUP)
            def _(g):
                add_slots(c * chunk + g * GROUP, place)

        for j in reversed(range(panel_dev)):
            rel = panel * panel_dev + j
            if panel:
                dense_copy(rel - panel_dev, j).wait()
                result_copy(rel - panel_dev, j).wait()
            for b in range(dev_blocks):
                for cb in range(col_blocks):
                    lanes = slice(cb * EDGE, (cb + 1) * EDGE)
                    for q, acc in enumerate(accs):
                        hi, lo = split(acc[(j * dev_blocks + b) * col_blocks + cb])
                        at = b * EDGE + q * part
                        both[j, at:at + part, lanes] = hi
                        both[j, node_dev + at:node_dev + at + part, lanes] = lo
            dense_copy(rel, j).start()
            pair = jnp.dot(both[j], scaled[...], preferred_element_type=F32)
            result[j] = pair[:node_dev] + pair[node_dev:]
            result_copy(rel, j).start()

    for j in range(panel_dev):
        rel = (n_panels - 1) * panel_dev + j
        dense_copy(rel, j).wait()
        result_copy(rel, j).wait()


def middle_kernel(n_col, n_in, scale, deg_ref, cot_ref, weight_ref, *refs):
    parts = refs[:n_in]
    act_ref, pulled_ref, keep_ref, send_ref = refs[n_in:]
    node_dev = cot_ref.shape[0]
    dev_blocks = node_dev // EDGE
    base = (lax.axis_index("row") * n_col + lax.axis_index("col")) * dev_blocks
    inv = jnp.concatenate([inv_column(deg_ref, base + k) for k in range(dev_blocks)], axis=0)
    summed = parts[0][...]
    for ref in parts[1:]:
        summed = summed + ref[...]
    propagated = inv * summed
    prop_hi, prop_lo = split(propagated)
    weight = weight_ref[...]
    pair = jnp.dot(
        jnp.concatenate([prop_hi, prop_lo], axis=0), weight, preferred_element_type=F32)
    v = pair[:node_dev] + pair[node_dev:]
    t = jnp.tanh(GELU_C * (v + GELU_K * v * v * v))
    act_ref[...] = (0.5 * v * (1.0 + t)).astype(BF16)
    slope = 0.5 * (1.0 + t) + 0.5 * v * (1.0 - t * t) * (GELU_C * (1.0 + 3.0 * GELU_K * v * v))
    gprime = cot_ref[...].astype(F32) * slope
    hi, lo = split(gprime)
    pair = lax.dot_general(
        jnp.concatenate([hi, lo], axis=0), weight, (((1,), (1,)), ((), ())),
        preferred_element_type=F32,
    )
    pulled_ref[...] = jnp.transpose(inv * (pair[:node_dev] + pair[node_dev:]))
    pair = across(jnp.concatenate([prop_hi, prop_lo], axis=1), hi)
    part = scale * (pair[:EDGE] + (pair[EDGE:] + across(prop_hi, lo)))
    half = EDGE // 2
    low = lax.axis_index("col") % 2 == 0
    for n in range(0, part.shape[1], EDGE):
        upper, lower = part[:half, n:n + EDGE], part[half:, n:n + EDGE]
        rows = pl.ds(n // EDGE * half, half)
        keep_ref[rows, :] = jnp.where(low, upper, lower)
        send_ref[rows, :] = jnp.where(low, lower, upper)


def load_lhs(stage, lhs, copies):
    width, node_dev = stage.shape[1:]
    for i in range(len(copies)):
        copies[i].wait()
        hi, lo = split(stage[i])
        lhs[:width, i * node_dev:(i + 1) * node_dev] = hi
        lhs[width:, i * node_dev:(i + 1) * node_dev] = lo


def partial_kernel(n_in, tile_ref, *refs):
    parts = refs[:n_in]
    out_ref, rest_ref, dense, stage, lhs, sems, dense_sems, rest_sem = refs[n_in:]
    width, node_dev = stage.shape[1:]
    col_nodes = dense.shape[1]
    blocks = fetch(
        [(tile_ref.at[span], dense.at[span]) for span in (
            pl.ds(i * node_dev, node_dev) for i in range(n_in))], dense_sems)
    copies = fetch([(r, stage.at[i]) for i, r in enumerate(parts)], sems)
    rest = pltpu.make_async_copy(
        tile_ref.at[pl.ds(n_in * node_dev, rest_ref.shape[0])], rest_ref, rest_sem)
    rest.start()
    load_lhs(stage, lhs, copies)
    for copy in blocks:
        copy.wait()
    step = 2 * EDGE if col_nodes % (2 * EDGE) == 0 else EDGE
    for n in range(0, col_nodes, step):
        pair = jnp.dot(lhs[...], dense[:, n:n + step], preferred_element_type=F32)
        out_ref[:, n:n + step] = pair[:width] + pair[width:]
    rest.wait()


def last_kernel(n_in, n_out, deg_ref, dense_ref, sofar_ref, *refs):
    parts, outs = refs[:n_in], refs[n_in:n_in + n_out]
    dense, stage, lhs, sofar, sems, dense_sem, sofar_sem = refs[n_in + n_out:]
    width, node_dev = parts[0].shape
    col_nodes = dense.shape[1]
    block = pltpu.make_async_copy(dense_ref, dense, dense_sem)
    before = pltpu.make_async_copy(sofar_ref, sofar, sofar_sem)
    block.start()
    size = col_nodes // n_out
    copies = fetch([(r, stage.at[i]) for i, r in enumerate(parts)], sems)
    before.start()
    load_lhs(stage, lhs, copies)
    block.wait()
    before.wait()
    step = 2 * EDGE if col_nodes % (2 * EDGE) == 0 else EDGE
    first = lax.axis_index("col") * (col_nodes // EDGE)
    for n in range(0, col_nodes, step):
        pair = jnp.dot(lhs[...], dense[:, n:n + step], preferred_element_type=F32)
        total = sofar[:, n:n + step] + (pair[:width] + pair[width:])
        for at in range(n, n + step, EDGE):
            inv = inv_column(deg_ref, first + at // EDGE)
            out = outs[at // size]
            out[at % size:at % size + EDGE, :] = inv * jnp.transpose(total[:, at - n:at - n + EDGE])


def body(n_row, n_col, features, degrees, block_rows, block_cols, live_slots, blocks, weight, cotangent):
    n_chip = n_col // 2
    chip_bits, row_bits = n_chip.bit_length() - 1, n_row.bit_length() - 1
    assert n_col == 2 << chip_bits and n_row == 1 << row_bits
    node_dev, hidden = cotangent.shape
    col_nodes, width = features.shape
    row_nodes = node_dev * n_col
    nodes = col_nodes * n_col
    slots = blocks.shape[2]
    deg = degrees.reshape(nodes // EDGE, EDGE)
    col_blocks = col_nodes // EDGE
    dev_blocks = node_dev // EDGE
    assert n_chip >= 4
    chunk = 16
    panel_dev = n_col
    while panel_dev % 2 == 0 and panel_dev * node_dev * col_nodes * 4 > ACC_BYTES:
        panel_dev //= 2
    positions = panel_dev * dev_blocks * col_blocks
    smem = pl.BlockSpec(memory_space=pltpu.SMEM)
    any_space = pl.BlockSpec(memory_space=pl.ANY)
    vmem = pl.BlockSpec(memory_space=pltpu.VMEM)

    def params(mib):
        return pltpu.CompilerParams(vmem_limit_bytes=mib << 20)

    def after(x, other):
        corner = 0.0 * other[:8, :EDGE]
        if x.shape[0] == other.shape[0] and x.shape[1] <= other.shape[1]:
            return x + 0.0 * other[:, :x.shape[1]]
        return (x.reshape(-1, 8, EDGE) + corner).reshape(x.shape)

    def ahead(x):
        return lax.optimization_barrier(x)

    def cost(flops, read):
        return pl.CostEstimate(flops=flops, bytes_accessed=read, transcendentals=0)

    *pieces, tile = pl.pallas_call(
        functools.partial(forward_kernel, n_col, chunk, panel_dev, node_dev),
        out_shape=[jax.ShapeDtypeStruct((node_dev, width), F32)] * n_col
        + [jax.ShapeDtypeStruct((row_nodes, col_nodes), BF16)],
        in_specs=[smem, smem, smem, vmem, vmem, any_space],
        out_specs=[any_space] * (n_col + 1),
        scratch_shapes=[
            pltpu.VMEM((positions + 1, EDGE // QUARTERS, EDGE), F32) for _ in range(QUARTERS)
        ] + [
            pltpu.VMEM((panel_dev, 2 * node_dev, col_nodes), BF16),
            pltpu.VMEM((slots, EDGE, EDGE), BF16),
            pltpu.VMEM((col_nodes, width), BF16),
            pltpu.VMEM((panel_dev, node_dev, width), F32),
            pltpu.SemaphoreType.DMA((slots // chunk,)),
            pltpu.SemaphoreType.DMA((panel_dev,)),
            pltpu.SemaphoreType.DMA((panel_dev,)),
        ],
        compiler_params=params(54),
        name="densify_forward",
    )(block_rows, block_cols, live_slots, deg, features, blocks)
    keep, send = pieces[0::2], pieces[1::2]

    swap_pairs = [(i, i ^ 1) for i in range(n_col)]

    def swap(x):
        return lax.ppermute(x, "col", swap_pairs)

    def chip_flip(x, bit):
        return lax.ppermute(x, "col", [(i, i ^ (2 << bit)) for i in range(n_col)])

    def row_flip(x, bit):
        return lax.ppermute(x, "row", [(i, i ^ (1 << bit)) for i in range(n_row)])

    def low_bit(m):
        return (m & -m).bit_length() - 1

    last = n_chip - 1
    kept = {m: [keep[m], swap(send[m])] for m in range(last, -1, -1)}
    parts = [functools.reduce(jnp.add, kept[0])]
    arrived = {m: [] for m in range(n_chip)}
    for m in range(last, 0, -1):
        if m == last:
            unit = ahead(after(kept[m][0], kept[m][0])) + kept[m][1]
        else:
            unit = functools.reduce(jnp.add, kept[m])
            if m == 2:
                unit = ahead(after(unit, parts[0]))
            unit = functools.reduce(jnp.add, [unit] + arrived[m])
        arrived[m & (m - 1)].append(chip_flip(unit, low_bit(m)))
    kept[0] = arrived[0]
    parts += kept[0]

    half = width // 2
    out_act, pulled, wkeep, wsend = pl.pallas_call(
        functools.partial(middle_kernel, n_col, len(parts), float(nodes) ** (-0.5)),
        out_shape=(
            jax.ShapeDtypeStruct((node_dev, hidden), BF16),
            jax.ShapeDtypeStruct((width, node_dev), F32),
            jax.ShapeDtypeStruct((half * hidden // EDGE, EDGE), F32),
            jax.ShapeDtypeStruct((half * hidden // EDGE, EDGE), F32),
        ),
        in_specs=[vmem] * (3 + len(parts)),
        out_specs=(vmem,) * 4,
        compiler_params=params(16),
        name="middle",
    )(deg, cotangent, weight, *parts)

    own = {0: pulled}
    for m in range(1, n_chip):
        own[m] = chip_flip(own[m & (m - 1)], low_bit(m))
    other = {m: swap(own[m]) for m in range(last)}

    wsum = after(wkeep + swap(wsend), other[2])
    moved = chip_flip(wsum, 0)
    early = [x for m in range(last) for x in (own[m], other[m])]
    late_rows = 2 * node_dev
    sofar, rest = pl.pallas_call(
        functools.partial(partial_kernel, len(early)),
        out_shape=(
            jax.ShapeDtypeStruct((width, col_nodes), F32),
            jax.ShapeDtypeStruct((late_rows, col_nodes), BF16),
        ),
        in_specs=[any_space] * (1 + len(early)),
        out_specs=(vmem, any_space),
        scratch_shapes=[
            pltpu.VMEM((len(early) * node_dev, col_nodes), BF16),
            pltpu.VMEM((len(early), width, node_dev), F32),
            pltpu.VMEM((2 * width, len(early) * node_dev), BF16),
            pltpu.SemaphoreType.DMA((len(early),)),
            pltpu.SemaphoreType.DMA((len(early),)),
            pltpu.SemaphoreType.DMA,
        ],
        compiler_params=params(BWD),
        cost_estimate=cost(row_nodes * col_nodes * width * 4, 32 << 20),
        name="backward_early",
    )(tile, *early)

    wsum = after(wsum, sofar) + moved
    own[last] = after(own[last], sofar)
    late = [own[last], swap(own[last])]
    for bit in range(1, chip_bits):
        wsum = wsum + chip_flip(wsum, bit)
    n_piece = max(1, row_bits)
    while col_nodes % (EDGE * n_piece):
        n_piece -= 1
    size = col_nodes // n_piece
    done = pl.pallas_call(
        functools.partial(last_kernel, len(late), n_piece),
        out_shape=(jax.ShapeDtypeStruct((size, width), F32),) * n_piece,
        in_specs=[vmem, any_space, any_space] + [any_space] * len(late),
        out_specs=(vmem,) * n_piece,
        scratch_shapes=[
            pltpu.VMEM((len(late) * node_dev, col_nodes), BF16),
            pltpu.VMEM((len(late), width, node_dev), F32),
            pltpu.VMEM((2 * width, len(late) * node_dev), BF16),
            pltpu.VMEM((width, col_nodes), F32),
            pltpu.SemaphoreType.DMA((len(late),)),
            pltpu.SemaphoreType.DMA,
            pltpu.SemaphoreType.DMA,
        ],
        compiler_params=params(BWD),
        name="backward_late",
    )(deg, rest, sofar, *late)

    done = list(done)
    for t in range(row_bits):
        if t == 0:
            wsum = after(wsum, done[-1])
        else:
            wsum = after(wsum, done[-1])
        wsum = wsum + row_flip(wsum, t)
        done = [x + row_flip(x, (i + t) % row_bits) for i, x in enumerate(done)]
    wsum = after(wsum, done[0])
    feat_grad = jnp.concatenate(done, axis=0)

    wother = swap(wsum)
    low = lax.axis_index("col") % 2 == 0
    halves = (jnp.where(low, wsum, wother), jnp.where(low, wother, wsum))
    weight_grad = jnp.concatenate(
        [jnp.concatenate([x[i:i + half] for i in range(0, x.shape[0], half)], axis=1) for x in halves],
        axis=0,
    )
    return out_act, feat_grad, weight_grad


def solution(mesh):
    n_row, n_col = mesh.shape["row"], mesh.shape["col"]
    return jax.shard_map(
        functools.partial(body, n_row, n_col),
        mesh=mesh,
        in_specs=(
            P("col", None),
            P(),
            P("row", "col", None),
            P("row", "col", None),
            P("row", "col"),
            P("row", "col", None, None, None),
            P(),
            P(("row", "col"), None),
        ),
        out_specs=(P(("row", "col"), None), P("col", None), P()),
        check_vma=False,
    )
```

```python
import functools

import jax
import jax.numpy as jnp
from jax import lax
from jax.experimental import pallas as pl
from jax.experimental.pallas import tpu as pltpu
from jax.sharding import PartitionSpec as P

F32 = jnp.float32
BF16 = jnp.bfloat16
EDGE = 128
GROUP = 16
QUARTERS = 4
AHEAD = 3
BWD = 50
ACC_BYTES = 8 << 20
GELU_C = 0.7978845608028654
GELU_K = 0.044715


def inv_column(deg_ref, start):
    row = lax.rsqrt(deg_ref[pl.ds(start, 1), :].astype(F32))
    return jnp.transpose(jnp.broadcast_to(row, (EDGE, EDGE)))


def split(value):
    hi = value.astype(BF16)
    return hi, (value - hi.astype(F32)).astype(BF16)


def across(a, b):
    return lax.dot_general(a, b, (((0,), (0,)), ((), ())), preferred_element_type=F32)


def fetch(pairs, sems):
    copies = [pltpu.make_async_copy(src, dst, sems.at[i]) for i, (src, dst) in enumerate(pairs)]
    for copy in copies:
        copy.start()
    return copies


def halve(value, size):
    if size & (size - 1) == 0:
        shift = size.bit_length() - 1
        return lax.shift_right_logical(value, shift), value & (size - 1)
    return lax.div(value, size), lax.rem(value, size)


def forward_kernel(
    n_col, chunk, panel_dev, node_dev,
    rows_ref, cols_ref, live_ref, deg_ref, feat_ref, blocks_ref, *refs,
):
    outs, tile_ref = refs[:n_col], refs[n_col]
    accs, (both, buf, scaled, result, in_sems, dense_sems, out_sems) = refs[n_col + 1:-7], refs[-7:]
    part = EDGE // len(accs)
    slots = buf.shape[0]
    col_nodes, width = feat_ref.shape
    col_blocks = col_nodes // EDGE
    dev_blocks = node_dev // EDGE
    panel_blocks = panel_dev * dev_blocks
    positions = panel_blocks * col_blocks
    n_panels = n_col // panel_dev
    n_chunks = slots // chunk
    me = lax.axis_index("col")
    live = live_ref[0, 0]

    def block_copy(c):
        span = pl.ds(c * chunk, chunk)
        return pltpu.make_async_copy(blocks_ref.at[0, 0, span], buf.at[span], in_sems.at[c])

    def dense_copy(rel, j):
        there = tile_ref.at[pl.ds(rel * node_dev, node_dev)]
        return pltpu.make_async_copy(both.at[j, pl.ds(0, node_dev)], there, dense_sems.at[j])

    def result_copy(rel, j):
        return pltpu.make_async_copy(result.at[j], outs[rel], out_sems.at[j])

    for c in range(n_chunks):
        block_copy(c).start()

    for k in range(col_blocks):
        inv = inv_column(deg_ref, me * col_blocks + k)
        span = pl.ds(k * EDGE, EDGE)
        scaled[span, :] = (inv * feat_ref[span, :].astype(F32)).astype(BF16)

    def add_slots(first, place):
        pending = []

        def finish():
            acc, p, sofar, block = pending.pop(0)
            acc[p] = sofar + block.astype(F32)

        for s in range(GROUP):
            p = place(first + s)
            for q, acc in enumerate(accs):
                pending.append((acc, p, acc[p], buf[first + s, q * part:(q + 1) * part, :]))
                if len(pending) > AHEAD:
                    finish()
        while pending:
            finish()

    for panel in range(n_panels):
        base = panel * panel_blocks

        @pl.loop(0, positions // 4)
        def _(p):
            for acc in accs:
                acc[pl.ds(p * 4, 4)] = jnp.zeros((4, part, EDGE), F32)

        def place(s):
            dev, inner = halve(rows_ref[0, 0, s], dev_blocks)
            r = (dev ^ me) * dev_blocks + inner - base
            ok = s < live
            if n_panels > 1:
                ok = ok & (r >= 0) & (r < panel_blocks)
            return jnp.where(ok, r * col_blocks + cols_ref[0, 0, s], positions)

        @pl.loop(0, n_chunks)
        def _(c):
            if panel == 0:
                block_copy(c).wait()

            @pl.loop(0, chunk // GROUP)
            def _(g):
                add_slots(c * chunk + g * GROUP, place)

        for j in reversed(range(panel_dev)):
            rel = panel * panel_dev + j
            if panel:
                dense_copy(rel - panel_dev, j).wait()
                result_copy(rel - panel_dev, j).wait()
            for b in range(dev_blocks):
                for cb in range(col_blocks):
                    lanes = slice(cb * EDGE, (cb + 1) * EDGE)
                    for q, acc in enumerate(accs):
                        hi, lo = split(acc[(j * dev_blocks + b) * col_blocks + cb])
                        at = b * EDGE + q * part
                        both[j, at:at + part, lanes] = hi
                        both[j, node_dev + at:node_dev + at + part, lanes] = lo
            dense_copy(rel, j).start()
            pair = jnp.dot(both[j], scaled[...], preferred_element_type=F32)
            result[j] = pair[:node_dev] + pair[node_dev:]
            result_copy(rel, j).start()

    for j in range(panel_dev):
        rel = (n_panels - 1) * panel_dev + j
        dense_copy(rel, j).wait()
        result_copy(rel, j).wait()


def middle_kernel(n_col, n_in, scale, deg_ref, cot_ref, weight_ref, *refs):
    parts = refs[:n_in]
    act_ref, pulled_ref, keep_ref, send_ref = refs[n_in:]
    node_dev = cot_ref.shape[0]
    dev_blocks = node_dev // EDGE
    base = (lax.axis_index("row") * n_col + lax.axis_index("col")) * dev_blocks
    inv = jnp.concatenate([inv_column(deg_ref, base + k) for k in range(dev_blocks)], axis=0)
    summed = parts[0][...]
    for ref in parts[1:]:
        summed = summed + ref[...]
    propagated = inv * summed
    prop_hi, prop_lo = split(propagated)
    weight = weight_ref[...]
    pair = jnp.dot(
        jnp.concatenate([prop_hi, prop_lo], axis=0), weight, preferred_element_type=F32)
    v = pair[:node_dev] + pair[node_dev:]
    t = jnp.tanh(GELU_C * (v + GELU_K * v * v * v))
    act_ref[...] = (0.5 * v * (1.0 + t)).astype(BF16)
    slope = 0.5 * (1.0 + t) + 0.5 * v * (1.0 - t * t) * (GELU_C * (1.0 + 3.0 * GELU_K * v * v))
    gprime = cot_ref[...].astype(F32) * slope
    hi, lo = split(gprime)
    pair = lax.dot_general(
        jnp.concatenate([hi, lo], axis=0), weight, (((1,), (1,)), ((), ())),
        preferred_element_type=F32,
    )
    pulled_ref[...] = jnp.transpose(inv * (pair[:node_dev] + pair[node_dev:]))
    pair = across(jnp.concatenate([prop_hi, prop_lo], axis=1), hi)
    part = scale * (pair[:EDGE] + (pair[EDGE:] + across(prop_hi, lo)))
    half = EDGE // 2
    low = lax.axis_index("col") % 2 == 0
    for n in range(0, part.shape[1], EDGE):
        upper, lower = part[:half, n:n + EDGE], part[half:, n:n + EDGE]
        rows = pl.ds(n // EDGE * half, half)
        keep_ref[rows, :] = jnp.where(low, upper, lower)
        send_ref[rows, :] = jnp.where(low, lower, upper)


def load_lhs(stage, lhs, copies):
    width, node_dev = stage.shape[1:]
    for i in range(len(copies)):
        copies[i].wait()
        hi, lo = split(stage[i])
        lhs[:width, i * node_dev:(i + 1) * node_dev] = hi
        lhs[width:, i * node_dev:(i + 1) * node_dev] = lo


def partial_kernel(n_in, tile_ref, *refs):
    parts = refs[:n_in]
    out_ref, rest_ref, dense, stage, lhs, sems, dense_sems, rest_sem = refs[n_in:]
    width, node_dev = stage.shape[1:]
    col_nodes = dense.shape[1]
    blocks = fetch(
        [(tile_ref.at[span], dense.at[span]) for span in (
            pl.ds(i * node_dev, node_dev) for i in range(n_in))], dense_sems)
    copies = fetch([(r, stage.at[i]) for i, r in enumerate(parts)], sems)
    rest = pltpu.make_async_copy(
        tile_ref.at[pl.ds(n_in * node_dev, rest_ref.shape[0])], rest_ref, rest_sem)
    rest.start()
    load_lhs(stage, lhs, copies)
    for copy in blocks:
        copy.wait()
    step = 2 * EDGE if col_nodes % (2 * EDGE) == 0 else EDGE
    for n in range(0, col_nodes, step):
        pair = jnp.dot(lhs[...], dense[:, n:n + step], preferred_element_type=F32)
        out_ref[:, n:n + step] = pair[:width] + pair[width:]
    rest.wait()


def last_kernel(n_in, n_out, deg_ref, dense_ref, sofar_ref, *refs):
    parts, outs = refs[:n_in], refs[n_in:n_in + n_out]
    dense, stage, lhs, sofar, sems, dense_sem, sofar_sem = refs[n_in + n_out:]
    width, node_dev = parts[0].shape
    col_nodes = dense.shape[1]
    block = pltpu.make_async_copy(dense_ref, dense, dense_sem)
    before = pltpu.make_async_copy(sofar_ref, sofar, sofar_sem)
    block.start()
    size = col_nodes // n_out
    copies = fetch([(r, stage.at[i]) for i, r in enumerate(parts)], sems)
    before.start()
    load_lhs(stage, lhs, copies)
    block.wait()
    before.wait()
    step = 2 * EDGE if col_nodes % (2 * EDGE) == 0 else EDGE
    first = lax.axis_index("col") * (col_nodes // EDGE)
    for n in range(0, col_nodes, step):
        pair = jnp.dot(lhs[...], dense[:, n:n + step], preferred_element_type=F32)
        total = sofar[:, n:n + step] + (pair[:width] + pair[width:])
        for at in range(n, n + step, EDGE):
            inv = inv_column(deg_ref, first + at // EDGE)
            out = outs[at // size]
            out[at % size:at % size + EDGE, :] = inv * jnp.transpose(total[:, at - n:at - n + EDGE])


def body(n_row, n_col, features, degrees, block_rows, block_cols, live_slots, blocks, weight, cotangent):
    n_chip = n_col // 2
    chip_bits, row_bits = n_chip.bit_length() - 1, n_row.bit_length() - 1
    assert n_col == 2 << chip_bits and n_row == 1 << row_bits
    node_dev, hidden = cotangent.shape
    col_nodes, width = features.shape
    row_nodes = node_dev * n_col
    nodes = col_nodes * n_col
    slots = blocks.shape[2]
    deg = degrees.reshape(nodes // EDGE, EDGE)
    col_blocks = col_nodes // EDGE
    dev_blocks = node_dev // EDGE
    assert n_chip >= 4
    chunk = 16
    panel_dev = n_col
    while panel_dev % 2 == 0 and panel_dev * node_dev * col_nodes * 4 > ACC_BYTES:
        panel_dev //= 2
    positions = panel_dev * dev_blocks * col_blocks
    smem = pl.BlockSpec(memory_space=pltpu.SMEM)
    any_space = pl.BlockSpec(memory_space=pl.ANY)
    vmem = pl.BlockSpec(memory_space=pltpu.VMEM)

    def params(mib):
        return pltpu.CompilerParams(vmem_limit_bytes=mib << 20)

    def after(x, other):
        corner = 0.0 * other[:8, :EDGE]
        if x.shape[0] == other.shape[0] and x.shape[1] <= other.shape[1]:
            return x + 0.0 * other[:, :x.shape[1]]
        return (x.reshape(-1, 8, EDGE) + corner).reshape(x.shape)

    def ahead(x):
        return lax.optimization_barrier(x)

    def cost(flops, read):
        return pl.CostEstimate(flops=flops, bytes_accessed=read, transcendentals=0)

    *pieces, tile = pl.pallas_call(
        functools.partial(forward_kernel, n_col, chunk, panel_dev, node_dev),
        out_shape=[jax.ShapeDtypeStruct((node_dev, width), F32)] * n_col
        + [jax.ShapeDtypeStruct((row_nodes, col_nodes), BF16)],
        in_specs=[smem, smem, smem, vmem, vmem, any_space],
        out_specs=[any_space] * (n_col + 1),
        scratch_shapes=[
            pltpu.VMEM((positions + 1, EDGE // QUARTERS, EDGE), F32) for _ in range(QUARTERS)
        ] + [
            pltpu.VMEM((panel_dev, 2 * node_dev, col_nodes), BF16),
            pltpu.VMEM((slots, EDGE, EDGE), BF16),
            pltpu.VMEM((col_nodes, width), BF16),
            pltpu.VMEM((panel_dev, node_dev, width), F32),
            pltpu.SemaphoreType.DMA((slots // chunk,)),
            pltpu.SemaphoreType.DMA((panel_dev,)),
            pltpu.SemaphoreType.DMA((panel_dev,)),
        ],
        compiler_params=params(54),
        name="densify_forward",
    )(block_rows, block_cols, live_slots, deg, features, blocks)
    keep, send = pieces[0::2], pieces[1::2]

    swap_pairs = [(i, i ^ 1) for i in range(n_col)]

    def swap(x):
        return lax.ppermute(x, "col", swap_pairs)

    def chip_flip(x, bit):
        return lax.ppermute(x, "col", [(i, i ^ (2 << bit)) for i in range(n_col)])

    def row_flip(x, bit):
        return lax.ppermute(x, "row", [(i, i ^ (1 << bit)) for i in range(n_row)])

    def low_bit(m):
        return (m & -m).bit_length() - 1

    last = n_chip - 1
    kept = {m: [keep[m], swap(send[m])] for m in range(last, -1, -1)}
    parts = [functools.reduce(jnp.add, kept[0])]
    arrived = {m: [] for m in range(n_chip)}
    for m in range(last, 0, -1):
        if m == last:
            unit = ahead(after(kept[m][0], kept[m][0])) + kept[m][1]
        else:
            unit = functools.reduce(jnp.add, kept[m])
            if m == 2:
                unit = ahead(after(unit, parts[0]))
            unit = functools.reduce(jnp.add, [unit] + arrived[m])
        arrived[m & (m - 1)].append(chip_flip(unit, low_bit(m)))
    kept[0] = arrived[0]
    parts += kept[0]

    half = width // 2
    out_act, pulled, wkeep, wsend = pl.pallas_call(
        functools.partial(middle_kernel, n_col, len(parts), float(nodes) ** (-0.5)),
        out_shape=(
            jax.ShapeDtypeStruct((node_dev, hidden), BF16),
            jax.ShapeDtypeStruct((width, node_dev), F32),
            jax.ShapeDtypeStruct((half * hidden // EDGE, EDGE), F32),
            jax.ShapeDtypeStruct((half * hidden // EDGE, EDGE), F32),
        ),
        in_specs=[vmem] * (3 + len(parts)),
        out_specs=(vmem,) * 4,
        compiler_params=params(16),
        name="middle",
    )(deg, cotangent, weight, *parts)

    own = {0: pulled}
    for m in range(1, n_chip):
        own[m] = chip_flip(own[m & (m - 1)], low_bit(m))
    other = {m: swap(own[m]) for m in range(last)}

    wsum = after(wkeep + swap(wsend), other[2])
    moved = chip_flip(wsum, 0)
    early = [x for m in range(last) for x in (own[m], other[m])]
    late_rows = 2 * node_dev
    sofar, rest = pl.pallas_call(
        functools.partial(partial_kernel, len(early)),
        out_shape=(
            jax.ShapeDtypeStruct((width, col_nodes), F32),
            jax.ShapeDtypeStruct((late_rows, col_nodes), BF16),
        ),
        in_specs=[any_space] * (1 + len(early)),
        out_specs=(vmem, any_space),
        scratch_shapes=[
            pltpu.VMEM((len(early) * node_dev, col_nodes), BF16),
            pltpu.VMEM((len(early), width, node_dev), F32),
            pltpu.VMEM((2 * width, len(early) * node_dev), BF16),
            pltpu.SemaphoreType.DMA((len(early),)),
            pltpu.SemaphoreType.DMA((len(early),)),
            pltpu.SemaphoreType.DMA,
        ],
        compiler_params=params(BWD),
        cost_estimate=cost(row_nodes * col_nodes * width * 4, 32 << 20),
        name="backward_early",
    )(tile, *early)

    wsum = after(wsum, sofar) + moved
    own[last] = after(own[last], sofar)
    late = [own[last], swap(own[last])]
    for bit in range(1, chip_bits):
        wsum = wsum + chip_flip(wsum, bit)
    n_piece = max(1, row_bits)
    while col_nodes % (EDGE * n_piece):
        n_piece -= 1
    size = col_nodes // n_piece
    done = pl.pallas_call(
        functools.partial(last_kernel, len(late), n_piece),
        out_shape=(jax.ShapeDtypeStruct((size, width), F32),) * n_piece,
        in_specs=[vmem, any_space, any_space] + [any_space] * len(late),
        out_specs=(vmem,) * n_piece,
        scratch_shapes=[
            pltpu.VMEM((len(late) * node_dev, col_nodes), BF16),
            pltpu.VMEM((len(late), width, node_dev), F32),
            pltpu.VMEM((2 * width, len(late) * node_dev), BF16),
            pltpu.VMEM((width, col_nodes), F32),
            pltpu.SemaphoreType.DMA((len(late),)),
            pltpu.SemaphoreType.DMA,
            pltpu.SemaphoreType.DMA,
        ],
        compiler_params=params(BWD),
        name="backward_late",
    )(deg, rest, sofar, *late)

    done = list(done)
    for t in range(row_bits):
        if t:
            wsum = after(wsum, done[-1])
        wsum = wsum + row_flip(wsum, t)
        done = [x + row_flip(x, (i + t) % row_bits) for i, x in enumerate(done)]
    wsum = after(wsum, done[0])
    feat_grad = jnp.concatenate(done, axis=0)

    wother = swap(wsum)
    low = lax.axis_index("col") % 2 == 0
    halves = (jnp.where(low, wsum, wother), jnp.where(low, wother, wsum))
    weight_grad = jnp.concatenate(
        [jnp.concatenate([x[i:i + half] for i in range(0, x.shape[0], half)], axis=1) for x in halves],
        axis=0,
    )
    return out_act, feat_grad, weight_grad


def solution(mesh):
    n_row, n_col = mesh.shape["row"], mesh.shape["col"]
    return jax.shard_map(
        functools.partial(body, n_row, n_col),
        mesh=mesh,
        in_specs=(
            P("col", None),
            P(),
            P("row", "col", None),
            P("row", "col", None),
            P("row", "col"),
            P("row", "col", None, None, None),
            P(),
            P(("row", "col"), None),
        ),
        out_specs=(P(("row", "col"), None), P("col", None), P()),
        check_vma=False,
    )
```

```python
import functools

import jax
import jax.numpy as jnp
from jax import lax
from jax.experimental import pallas as pl
from jax.experimental.pallas import tpu as pltpu
from jax.sharding import PartitionSpec as P

F32 = jnp.float32
BF16 = jnp.bfloat16
EDGE = 128
GROUP = 16
QUARTERS = 4
AHEAD = 3
BWD = 50
ACC_BYTES = 8 << 20
GELU_C = 0.7978845608028654
GELU_K = 0.044715


def inv_column(deg_ref, start):
    row = lax.rsqrt(deg_ref[pl.ds(start, 1), :].astype(F32))
    return jnp.transpose(jnp.broadcast_to(row, (EDGE, EDGE)))


def split(value):
    hi = value.astype(BF16)
    return hi, (value - hi.astype(F32)).astype(BF16)


def across(a, b):
    return lax.dot_general(a, b, (((0,), (0,)), ((), ())), preferred_element_type=F32)


def fetch(pairs, sems):
    copies = [pltpu.make_async_copy(src, dst, sems.at[i]) for i, (src, dst) in enumerate(pairs)]
    for copy in copies:
        copy.start()
    return copies


def halve(value, size):
    if size & (size - 1) == 0:
        shift = size.bit_length() - 1
        return lax.shift_right_logical(value, shift), value & (size - 1)
    return lax.div(value, size), lax.rem(value, size)


def forward_kernel(
    n_col, chunk, panel_dev, node_dev,
    rows_ref, cols_ref, live_ref, deg_ref, feat_ref, blocks_ref, *refs,
):
    outs, tile_ref = refs[:n_col], refs[n_col]
    accs, (both, buf, scaled, result, in_sems, dense_sems, out_sems) = refs[n_col + 1:-7], refs[-7:]
    part = EDGE // len(accs)
    slots = buf.shape[0]
    col_nodes, width = feat_ref.shape
    col_blocks = col_nodes // EDGE
    dev_blocks = node_dev // EDGE
    panel_blocks = panel_dev * dev_blocks
    positions = panel_blocks * col_blocks
    n_panels = n_col // panel_dev
    n_chunks = slots // chunk
    me = lax.axis_index("col")
    live = live_ref[0, 0]

    def block_copy(c):
        span = pl.ds(c * chunk, chunk)
        return pltpu.make_async_copy(blocks_ref.at[0, 0, span], buf.at[span], in_sems.at[c])

    def dense_copy(rel, j):
        there = tile_ref.at[pl.ds(rel * node_dev, node_dev)]
        return pltpu.make_async_copy(both.at[j, pl.ds(0, node_dev)], there, dense_sems.at[j])

    def result_copy(rel, j):
        return pltpu.make_async_copy(result.at[j], outs[rel], out_sems.at[j])

    for c in range(n_chunks):
        block_copy(c).start()

    for k in range(col_blocks):
        inv = inv_column(deg_ref, me * col_blocks + k)
        span = pl.ds(k * EDGE, EDGE)
        scaled[span, :] = (inv * feat_ref[span, :].astype(F32)).astype(BF16)

    def add_slots(first, place):
        pending = []

        def finish():
            acc, p, sofar, block = pending.pop(0)
            acc[p] = sofar + block.astype(F32)

        for s in range(GROUP):
            p = place(first + s)
            for q, acc in enumerate(accs):
                pending.append((acc, p, acc[p], buf[first + s, q * part:(q + 1) * part, :]))
                if len(pending) > AHEAD:
                    finish()
        while pending:
            finish()

    for panel in range(n_panels):
        base = panel * panel_blocks

        @pl.loop(0, positions // 4)
        def _(p):
            for acc in accs:
                acc[pl.ds(p * 4, 4)] = jnp.zeros((4, part, EDGE), F32)

        def place(s):
            dev, inner = halve(rows_ref[0, 0, s], dev_blocks)
            r = (dev ^ me) * dev_blocks + inner - base
            ok = s < live
            if n_panels > 1:
                ok = ok & (r >= 0) & (r < panel_blocks)
            return jnp.where(ok, r * col_blocks + cols_ref[0, 0, s], positions)

        @pl.loop(0, n_chunks)
        def _(c):
            if panel == 0:
                block_copy(c).wait()

            @pl.loop(0, chunk // GROUP)
            def _(g):
                add_slots(c * chunk + g * GROUP, place)

        for j in reversed(range(panel_dev)):
            rel = panel * panel_dev + j
            if panel:
                dense_copy(rel - panel_dev, j).wait()
                result_copy(rel - panel_dev, j).wait()
            for b in range(dev_blocks):
                for cb in range(col_blocks):
                    lanes = slice(cb * EDGE, (cb + 1) * EDGE)
                    for q, acc in enumerate(accs):
                        hi, lo = split(acc[(j * dev_blocks + b) * col_blocks + cb])
                        at = b * EDGE + q * part
                        both[j, at:at + part, lanes] = hi
                        both[j, node_dev + at:node_dev + at + part, lanes] = lo
            dense_copy(rel, j).start()
            pair = jnp.dot(both[j], scaled[...], preferred_element_type=F32)
            result[j] = pair[:node_dev] + pair[node_dev:]
            result_copy(rel, j).start()

    for j in range(panel_dev):
        rel = (n_panels - 1) * panel_dev + j
        dense_copy(rel, j).wait()
        result_copy(rel, j).wait()


def middle_kernel(n_col, n_in, scale, deg_ref, cot_ref, weight_ref, *refs):
    parts = refs[:n_in]
    act_ref, pulled_ref, keep_ref, send_ref = refs[n_in:]
    node_dev = cot_ref.shape[0]
    dev_blocks = node_dev // EDGE
    base = (lax.axis_index("row") * n_col + lax.axis_index("col")) * dev_blocks
    inv = jnp.concatenate([inv_column(deg_ref, base + k) for k in range(dev_blocks)], axis=0)
    summed = parts[0][...]
    for ref in parts[1:]:
        summed = summed + ref[...]
    propagated = inv * summed
    prop_hi, prop_lo = split(propagated)
    weight = weight_ref[...]
    pair = jnp.dot(
        jnp.concatenate([prop_hi, prop_lo], axis=0), weight, preferred_element_type=F32)
    v = pair[:node_dev] + pair[node_dev:]
    t = jnp.tanh(GELU_C * (v + GELU_K * v * v * v))
    act_ref[...] = (0.5 * v * (1.0 + t)).astype(BF16)
    slope = 0.5 * (1.0 + t) + 0.5 * v * (1.0 - t * t) * (GELU_C * (1.0 + 3.0 * GELU_K * v * v))
    gprime = cot_ref[...].astype(F32) * slope
    hi, lo = split(gprime)
    pair = lax.dot_general(
        jnp.concatenate([hi, lo], axis=0), weight, (((1,), (1,)), ((), ())),
        preferred_element_type=F32,
    )
    pulled_ref[...] = jnp.transpose(inv * (pair[:node_dev] + pair[node_dev:]))
    pair = across(jnp.concatenate([prop_hi, prop_lo], axis=1), hi)
    part = scale * (pair[:EDGE] + (pair[EDGE:] + across(prop_hi, lo)))
    half = EDGE // 2
    low = lax.axis_index("col") % 2 == 0
    for n in range(0, part.shape[1], EDGE):
        upper, lower = part[:half, n:n + EDGE], part[half:, n:n + EDGE]
        rows = pl.ds(n // EDGE * half, half)
        keep_ref[rows, :] = jnp.where(low, upper, lower)
        send_ref[rows, :] = jnp.where(low, lower, upper)


def load_lhs(stage, lhs, copies):
    width, node_dev = stage.shape[1:]
    for i in range(len(copies)):
        copies[i].wait()
        hi, lo = split(stage[i])
        lhs[:width, i * node_dev:(i + 1) * node_dev] = hi
        lhs[width:, i * node_dev:(i + 1) * node_dev] = lo


def partial_kernel(n_in, tile_ref, *refs):
    parts = refs[:n_in]
    out_ref, rest_ref, dense, stage, lhs, sems, dense_sems, rest_sem = refs[n_in:]
    width, node_dev = stage.shape[1:]
    col_nodes = dense.shape[1]
    blocks = fetch(
        [(tile_ref.at[span], dense.at[span]) for span in (
            pl.ds(i * node_dev, node_dev) for i in range(n_in))], dense_sems)
    copies = fetch([(r, stage.at[i]) for i, r in enumerate(parts)], sems)
    rest = pltpu.make_async_copy(
        tile_ref.at[pl.ds(n_in * node_dev, rest_ref.shape[0])], rest_ref, rest_sem)
    rest.start()
    load_lhs(stage, lhs, copies)
    for copy in blocks:
        copy.wait()
    step = 2 * EDGE if col_nodes % (2 * EDGE) == 0 else EDGE
    for n in range(0, col_nodes, step):
        pair = jnp.dot(lhs[...], dense[:, n:n + step], preferred_element_type=F32)
        out_ref[:, n:n + step] = pair[:width] + pair[width:]
    rest.wait()


def last_kernel(n_in, n_out, deg_ref, dense_ref, sofar_ref, *refs):
    parts, outs = refs[:n_in], refs[n_in:n_in + 2 * n_out]
    dense, stage, lhs, sofar, sems, dense_sem, sofar_sem = refs[n_in + 2 * n_out:]
    row = lax.axis_index("row")
    width, node_dev = parts[0].shape
    col_nodes = dense.shape[1]
    block = pltpu.make_async_copy(dense_ref, dense, dense_sem)
    before = pltpu.make_async_copy(sofar_ref, sofar, sofar_sem)
    block.start()
    size = col_nodes // n_out
    copies = fetch([(r, stage.at[i]) for i, r in enumerate(parts)], sems)
    before.start()
    load_lhs(stage, lhs, copies)
    block.wait()
    before.wait()
    step = 2 * EDGE if col_nodes % (2 * EDGE) == 0 else EDGE
    first = lax.axis_index("col") * (col_nodes // EDGE)
    for n in range(0, col_nodes, step):
        pair = jnp.dot(lhs[...], dense[:, n:n + step], preferred_element_type=F32)
        total = sofar[:, n:n + step] + (pair[:width] + pair[width:])
        for at in range(n, n + step, EDGE):
            inv = inv_column(deg_ref, first + at // EDGE)
            value = inv * jnp.transpose(total[:, at - n:at - n + EDGE])
            piece, upper = at // size, at % size >= size // 2
            bit = lax.shift_right_logical(row, piece) & 1
            span = pl.ds(at % (size // 2), EDGE)

            @pl.when(bit == int(upper))
            def _():
                outs[2 * piece][span, :] = value

            @pl.when(bit != int(upper))
            def _():
                outs[2 * piece + 1][span, :] = value


def body(n_row, n_col, features, degrees, block_rows, block_cols, live_slots, blocks, weight, cotangent):
    n_chip = n_col // 2
    chip_bits, row_bits = n_chip.bit_length() - 1, n_row.bit_length() - 1
    assert n_col == 2 << chip_bits and n_row == 1 << row_bits
    node_dev, hidden = cotangent.shape
    col_nodes, width = features.shape
    row_nodes = node_dev * n_col
    nodes = col_nodes * n_col
    slots = blocks.shape[2]
    deg = degrees.reshape(nodes // EDGE, EDGE)
    col_blocks = col_nodes // EDGE
    dev_blocks = node_dev // EDGE
    assert n_chip >= 4
    chunk = 16
    panel_dev = n_col
    while panel_dev % 2 == 0 and panel_dev * node_dev * col_nodes * 4 > ACC_BYTES:
        panel_dev //= 2
    positions = panel_dev * dev_blocks * col_blocks
    smem = pl.BlockSpec(memory_space=pltpu.SMEM)
    any_space = pl.BlockSpec(memory_space=pl.ANY)
    vmem = pl.BlockSpec(memory_space=pltpu.VMEM)

    def params(mib):
        return pltpu.CompilerParams(vmem_limit_bytes=mib << 20)

    def after(x, other):
        corner = 0.0 * other[:8, :EDGE]
        if x.shape[0] == other.shape[0] and x.shape[1] <= other.shape[1]:
            return x + 0.0 * other[:, :x.shape[1]]
        return (x.reshape(-1, 8, EDGE) + corner).reshape(x.shape)

    def ahead(x):
        return lax.optimization_barrier(x)

    def cost(flops, read):
        return pl.CostEstimate(flops=flops, bytes_accessed=read, transcendentals=0)

    *pieces, tile = pl.pallas_call(
        functools.partial(forward_kernel, n_col, chunk, panel_dev, node_dev),
        out_shape=[jax.ShapeDtypeStruct((node_dev, width), F32)] * n_col
        + [jax.ShapeDtypeStruct((row_nodes, col_nodes), BF16)],
        in_specs=[smem, smem, smem, vmem, vmem, any_space],
        out_specs=[any_space] * (n_col + 1),
        scratch_shapes=[
            pltpu.VMEM((positions + 1, EDGE // QUARTERS, EDGE), F32) for _ in range(QUARTERS)
        ] + [
            pltpu.VMEM((panel_dev, 2 * node_dev, col_nodes), BF16),
            pltpu.VMEM((slots, EDGE, EDGE), BF16),
            pltpu.VMEM((col_nodes, width), BF16),
            pltpu.VMEM((panel_dev, node_dev, width), F32),
            pltpu.SemaphoreType.DMA((slots // chunk,)),
            pltpu.SemaphoreType.DMA((panel_dev,)),
            pltpu.SemaphoreType.DMA((panel_dev,)),
        ],
        compiler_params=params(54),
        name="densify_forward",
    )(block_rows, block_cols, live_slots, deg, features, blocks)
    keep, send = pieces[0::2], pieces[1::2]

    swap_pairs = [(i, i ^ 1) for i in range(n_col)]

    def swap(x):
        return lax.ppermute(x, "col", swap_pairs)

    def chip_flip(x, bit):
        return lax.ppermute(x, "col", [(i, i ^ (2 << bit)) for i in range(n_col)])

    def row_flip(x, bit):
        return lax.ppermute(x, "row", [(i, i ^ (1 << bit)) for i in range(n_row)])

    def low_bit(m):
        return (m & -m).bit_length() - 1

    last = n_chip - 1
    kept = {m: [keep[m], swap(send[m])] for m in range(last, -1, -1)}
    parts = [functools.reduce(jnp.add, kept[0])]
    arrived = {m: [] for m in range(n_chip)}
    for m in range(last, 0, -1):
        if m == last:
            unit = ahead(after(kept[m][0], kept[m][0])) + kept[m][1]
        else:
            unit = functools.reduce(jnp.add, kept[m])
            if m == 2:
                unit = ahead(after(unit, parts[0]))
            unit = functools.reduce(jnp.add, [unit] + arrived[m])
        arrived[m & (m - 1)].append(chip_flip(unit, low_bit(m)))
    kept[0] = arrived[0]
    parts += kept[0]

    half = width // 2
    out_act, pulled, wkeep, wsend = pl.pallas_call(
        functools.partial(middle_kernel, n_col, len(parts), float(nodes) ** (-0.5)),
        out_shape=(
            jax.ShapeDtypeStruct((node_dev, hidden), BF16),
            jax.ShapeDtypeStruct((width, node_dev), F32),
            jax.ShapeDtypeStruct((half * hidden // EDGE, EDGE), F32),
            jax.ShapeDtypeStruct((half * hidden // EDGE, EDGE), F32),
        ),
        in_specs=[vmem] * (3 + len(parts)),
        out_specs=(vmem,) * 4,
        compiler_params=params(16),
        name="middle",
    )(deg, cotangent, weight, *parts)

    own = {0: pulled}
    for m in range(1, n_chip):
        own[m] = chip_flip(own[m & (m - 1)], low_bit(m))
    other = {m: swap(own[m]) for m in range(last)}

    wsum = after(wkeep + swap(wsend), other[2])
    moved = chip_flip(wsum, 0)
    early = [x for m in range(last) for x in (own[m], other[m])]
    late_rows = 2 * node_dev
    sofar, rest = pl.pallas_call(
        functools.partial(partial_kernel, len(early)),
        out_shape=(
            jax.ShapeDtypeStruct((width, col_nodes), F32),
            jax.ShapeDtypeStruct((late_rows, col_nodes), BF16),
        ),
        in_specs=[any_space] * (1 + len(early)),
        out_specs=(vmem, any_space),
        scratch_shapes=[
            pltpu.VMEM((len(early) * node_dev, col_nodes), BF16),
            pltpu.VMEM((len(early), width, node_dev), F32),
            pltpu.VMEM((2 * width, len(early) * node_dev), BF16),
            pltpu.SemaphoreType.DMA((len(early),)),
            pltpu.SemaphoreType.DMA((len(early),)),
            pltpu.SemaphoreType.DMA,
        ],
        compiler_params=params(BWD),
        cost_estimate=cost(row_nodes * col_nodes * width * 4, 32 << 20),
        name="backward_early",
    )(tile, *early)

    wsum = after(wsum, sofar) + moved
    own[last] = after(own[last], sofar)
    late = [own[last], swap(own[last])]
    for bit in range(1, chip_bits):
        wsum = wsum + chip_flip(wsum, bit)
    assert row_bits >= 2
    n_piece = row_bits
    while col_nodes % (2 * EDGE * n_piece):
        n_piece -= 1
    size = col_nodes // n_piece
    done = pl.pallas_call(
        functools.partial(last_kernel, len(late), n_piece),
        out_shape=(jax.ShapeDtypeStruct((size // 2, width), F32),) * (2 * n_piece),
        in_specs=[vmem, any_space, any_space] + [any_space] * len(late),
        out_specs=(vmem,) * (2 * n_piece),
        scratch_shapes=[
            pltpu.VMEM((len(late) * node_dev, col_nodes), BF16),
            pltpu.VMEM((len(late), width, node_dev), F32),
            pltpu.VMEM((2 * width, len(late) * node_dev), BF16),
            pltpu.VMEM((width, col_nodes), F32),
            pltpu.SemaphoreType.DMA((len(late),)),
            pltpu.SemaphoreType.DMA,
            pltpu.SemaphoreType.DMA,
        ],
        compiler_params=params(BWD),
        name="backward_late",
    )(deg, rest, sofar, *late)

    wsum = after(wsum, done[0])
    done = [done[2 * i] + row_flip(done[2 * i + 1], i) for i in range(n_piece)]
    wsum = wsum + row_flip(wsum, 0)
    for t in range(1, row_bits):
        done = [x + row_flip(x, (i + t) % row_bits) for i, x in enumerate(done)]
        wsum = after(wsum, done[0])
        wsum = wsum + row_flip(wsum, t)
    wsum = after(wsum, done[0])
    halves = []
    for i, x in enumerate(done):
        low = lax.shift_right_logical(lax.axis_index("row"), i) & 1 == 0
        far = row_flip(x, i)
        halves += [jnp.where(low, x, far), jnp.where(low, far, x)]
    feat_grad = jnp.concatenate(halves, axis=0)

    wother = swap(wsum)
    low = lax.axis_index("col") % 2 == 0
    halves = (jnp.where(low, wsum, wother), jnp.where(low, wother, wsum))
    weight_grad = jnp.concatenate(
        [jnp.concatenate([x[i:i + half] for i in range(0, x.shape[0], half)], axis=1) for x in halves],
        axis=0,
    )
    return out_act, feat_grad, weight_grad


def solution(mesh):
    n_row, n_col = mesh.shape["row"], mesh.shape["col"]
    return jax.shard_map(
        functools.partial(body, n_row, n_col),
        mesh=mesh,
        in_specs=(
            P("col", None),
            P(),
            P("row", "col", None),
            P("row", "col", None),
            P("row", "col"),
            P("row", "col", None, None, None),
            P(),
            P(("row", "col"), None),
        ),
        out_specs=(P(("row", "col"), None), P("col", None), P()),
        check_vma=False,
    )
```
